512 devices in a mesh: comp: 4 (over x), row: 8 (over y_lo, core), col: 16 (over y_hi, z).
Axes of the slice: x: 4, y: 8 (y_hi: 2, y_lo: 4; y = y_hi * 4 + y_lo), z: 8, core: 2. Of those that a mesh axis runs over, the one named last changes fastest.
Arguments:
- atmosphere_level_state: float32 [4, 72, 262144], P(None, None, ('comp', 'row', 'col')), may hold values from -6 to 6
- atmosphere_mixing_map: float32 [72, 72], replicated, may hold values from -0.5 to 1, as said below
- sea_surface_temps: float32 [262144], P(('comp', 'row', 'col')), may hold values from -6 to 6
- tracers: float32 [2, 80, 256, 2048], P(None, None, ('comp', 'row'), 'col'), may hold values from -6 to 6
- currents: float32 [2, 256, 2048], P(None, ('comp', 'row'), 'col'), may hold values from -3 to 3
- ocean_advect_velocity: bfloat16 [2, 80, 256, 2048], P(None, None, ('comp', 'row'), 'col'), may hold values from -0.29882812 to 0.29882812
- ocean_mixing_map: float32 [80, 80], replicated, may hold values from -0.5 to 1, as said below
- ocean_cell_mask: int32 [256, 2048], P(('comp', 'row'), 'col'), may hold values 0 or 1
- remap_weight_tiles: bfloat16 [4, 128, 64, 4096], P('comp', ('row', 'col')), may hold values from 0 to 0.0078125
- outgoing_block_table: int32 [4, 128, 128, 2], P('comp', ('row', 'col')), may hold values from -1 to 7, as said below
- arrival_slot_table: int32 [4, 128, 64], P('comp', ('row', 'col')), may hold values from 0 to 255, as said below
Outputs:
- atm_final: float32 [4, 72, 262144], P(None, None, ('comp', 'row', 'col'))
- ocean_tracers: float32 [2, 80, 256, 2048], P(None, None, ('comp', 'row'), 'col')
- ocean_currents: float32 [2, 256, 2048], P(None, ('comp', 'row'), 'col')
- returned: float32 [3, 262144], P(None, ('comp', 'row', 'col'))
The draws below stay inside these ranges and needn't reach their ends.
Inputs may be any that keep to these rules, and one draw needn't show every extreme that they name: outgoing_block_table[c, p, d, s] is the block, within device p's 8 blocks, that device p of band c sends to device d in slot s, or -1 where no contribution of d names that slot; in every band some source device has all its slots to every device named. arrival_slot_table[c, d, j] = p * 2 + s names the slot of source device p through which contribution j of device d arrives; one device d never names a slot twice. `ocean_cell_mask`: 1 marks an ocean cell, 0 land. `atmosphere_mixing_map`: a fixed linear map over one column's levels. `ocean_mixing_map`: a fixed linear map over one column's levels.
All inputs are finite; a program needn't handle non-finite values. No bound on the sum of `ocean_cell_mask` on one device may be relied on, other than what follows from the above.
Results may differ from the reference program's by a relative error of at most 0.0027.
Values may be sent and summed in bfloat16 or wider, within the bound.
No kernel may reach another device: no remote copies, remote signals or barrier semaphores. Data moves between devices by JAX's collectives and lax.ppermute only.
A program may use at most 64 MiB of HBM per device.

```python
import jax
import jax.numpy as jnp
from jax import lax

ATM_LEVELS = 72
OCEAN_LEVELS = 80
MICRO_STEPS = 6
SOURCES = 4
OCEAN_ROWS = 8
OCEAN_COLS = 128
ATM_BLOCKS = 8
OCEAN_BLOCKS = 16
CONTRIBUTIONS = 64
SECTION = 128
PEER_SLOTS = 2
ATMOS_COLUMNS = 262144
GRID_ROWS = 256
GRID_COLS = 2048
N_COMP = 4
N_ROW = 8
N_COL = 16


def remap_pattern(key):
    token_count = SECTION * PEER_SLOTS
    device_count = N_COMP * SECTION
    hub_key = jax.random.fold_in(key, 11)
    band_hubs = jax.random.randint(hub_key, (N_COMP,), 0, SECTION, dtype=jnp.int32)
    device_hubs = jnp.repeat(band_hubs, SECTION).astype(jnp.int32)
    key_list = jax.random.split(key, device_count)

    def one_device(device_key, leader):
        first_key, second_key, third_key = jax.random.split(device_key, 3)
        shuffled = jax.random.permutation(first_key, token_count).astype(jnp.int32)
        tokens = jnp.arange(token_count, dtype=jnp.int32)
        position = jnp.zeros((token_count,), jnp.int32).at[shuffled].set(tokens)
        favoured = tokens // PEER_SLOTS == leader
        ranking = jnp.where(favoured, tokens % PEER_SLOTS, position + PEER_SLOTS)
        chosen = jnp.argsort(ranking, stable=True)[:CONTRIBUTIONS].astype(jnp.int32)
        reorder = jax.random.permutation(second_key, CONTRIBUTIONS)
        arrival = chosen[reorder].astype(jnp.int32)
        blocks = jax.random.randint(third_key, (CONTRIBUTIONS,), 0, ATM_BLOCKS, dtype=jnp.int32)
        sender = jnp.full((token_count,), -1, jnp.int32).at[arrival].set(blocks)
        return (sender.reshape(SECTION, PEER_SLOTS), arrival)
    senders, arrivals = jax.vmap(one_device)(key_list, device_hubs)
    senders = jnp.transpose(senders.reshape(N_COMP, SECTION, SECTION, PEER_SLOTS), (0, 2, 1, 3))
    return (senders.astype(jnp.int32), arrivals.reshape(N_COMP, SECTION, CONTRIBUTIONS).astype(jnp.int32))


def with_diagonal(noise, size):
    row_index = lax.broadcasted_iota(jnp.int32, (size, size), 0)
    col_index = lax.broadcasted_iota(jnp.int32, (size, size), 1)
    return (jnp.where(row_index == col_index, 0.7, 0.0) + noise).astype(jnp.float32)


def draw_outgoing_block_table(key, part):
    shared = remap_pattern(key)
    return shared[0]


def draw_arrival_slot_table(key, part):
    shared = remap_pattern(key)
    return shared[1]


def draw_atmosphere_mixing_map(key, part):
    key = jax.random.fold_in(key, 3)
    noise = jax.random.normal(key, (ATM_LEVELS, ATM_LEVELS), jnp.float32) * (0.2 / ATM_LEVELS ** 0.5)
    return with_diagonal(noise, ATM_LEVELS)


def draw_ocean_mixing_map(key, part):
    key = jax.random.fold_in(key, 5)
    noise = jax.random.normal(key, (OCEAN_LEVELS, OCEAN_LEVELS), jnp.float32) * (0.2 / OCEAN_LEVELS ** 0.5)
    return with_diagonal(noise, OCEAN_LEVELS)


def with_ends(entries, key, least, high):
    index_at = [jax.random.randint(jax.random.fold_in(key, axis), (), 0, length) for axis, length in enumerate(entries.shape)]
    longest = entries.shape.index(max(entries.shape))
    neighbour = index_at[:longest] + [(index_at[longest] + 1) % entries.shape[longest]] + index_at[longest + 1:]
    return entries.at[tuple(index_at)].set(least).at[tuple(neighbour)].set(high)


def block_scale(stream_key, shape, shards, smallest, high):
    gain = 1.0
    for dim, parts in shards:
        heights = jax.random.uniform(jax.random.fold_in(jax.random.fold_in(stream_key, 6), dim), (parts,), jnp.float32, smallest / len(shards), high / len(shards))
        gain = gain * jnp.repeat(jnp.exp(heights), shape[dim] // parts).reshape((-1,) + (1,) * (len(shape) - 1 - dim))
    return gain


def normal_values(key, shape, width, most, cuts=(), held_as=jnp.bfloat16):
    result = jax.random.normal(key, shape, jnp.float32) * width
    if len(cuts) > 0:
        result = block_scale(key, shape, cuts, -0.22, 0.18) * result
    return jnp.clip(result, min=-most, max=most).astype(held_as)


def setup_inputs(seed: int = 0) -> dict:
    splits = jax.random.split(jax.random.key(seed), 12)
    return {
        "atmosphere_level_state": normal_values(splits[0], (4, ATM_LEVELS, ATMOS_COLUMNS), 1.0, 6.0, ((2, 512),), jnp.float32),
        "atmosphere_mixing_map": draw_atmosphere_mixing_map(jax.random.fold_in(splits[11], 71), 0),
        "sea_surface_temps": normal_values(splits[2], (ATMOS_COLUMNS,), 1.0, 6.0, ((0, 512),), jnp.float32),
        "tracers": normal_values(splits[3], (2, OCEAN_LEVELS, GRID_ROWS, GRID_COLS), 1.0, 6.0, ((2, 32), (3, 16)), jnp.float32),
        "currents": normal_values(splits[4], (2, GRID_ROWS, GRID_COLS), 0.5, 3.0, ((1, 32), (2, 16)), jnp.float32),
        "ocean_advect_velocity": jnp.clip(jax.random.uniform(splits[5], (2, OCEAN_LEVELS, GRID_ROWS, GRID_COLS), jnp.float32, -0.29882812, 0.29882812) * block_scale(splits[5], (2, OCEAN_LEVELS, GRID_ROWS, GRID_COLS), ((2, 32), (3, 16)), -0.4, 0.0), -0.29882812, 0.29882812).astype(jnp.bfloat16),
        "ocean_mixing_map": draw_ocean_mixing_map(jax.random.fold_in(splits[11], 71), 0),
        "ocean_cell_mask": with_ends((jax.random.randint(splits[7], (GRID_ROWS, GRID_COLS), 0, 10) < 7).astype(jnp.int32), jax.random.fold_in(splits[7], 1), 0, 1),
        "remap_weight_tiles": jnp.clip(0.0078125 * jax.random.uniform(splits[8], (N_COMP, SECTION, CONTRIBUTIONS, 4096), jnp.float32) ** block_scale(splits[8], (N_COMP, SECTION, CONTRIBUTIONS, 4096), ((0, 4), (1, 128)), -0.2, 0.2), 0.0, 0.0078125).astype(jnp.bfloat16),
        "outgoing_block_table": draw_outgoing_block_table(jax.random.fold_in(splits[11], 71), 0),
        "arrival_slot_table": draw_arrival_slot_table(jax.random.fold_in(splits[11], 71), 0),
    }


heat_rate = 0.5
vapour_rate = 0.5
drag_rate = 0.3
heat_gain = 0.3
vapour_gain = 0.3
stress_gain = 0.3
saturation = 0.6
diffusion = 0.15
surface_heat = 0.3
surface_salt = 0.3
surface_push = 0.3
current_drag = 0.1
coriolis = 0.2
largest_value = lax.Precision.HIGHEST

def advance_atmosphere(air_column_state, sea_surface, vertical_mixing_map):
    bottom = air_column_state[:, -1, :]
    wind_speed = jnp.sqrt(bottom[2] * bottom[2] + bottom[3] * bottom[3] + 1.0)
    heat_flux = heat_rate * wind_speed * (sea_surface - bottom[0])
    vapour_flux = vapour_rate * wind_speed * (saturation * sea_surface - bottom[1])
    stress_east = drag_rate * wind_speed * bottom[2]
    stress_north = drag_rate * wind_speed * bottom[3]
    surface_flux_values = jnp.stack([heat_flux, vapour_flux, stress_east, stress_north])
    level_gains = jnp.array([heat_gain, vapour_gain, -stress_gain, -stress_gain], dtype=jnp.float32)
    raised_values = air_column_state.at[:, -1, :].add(level_gains[:, None] * surface_flux_values)
    levels_after_mixing = jnp.einsum('qf,ufe->uqe', vertical_mixing_map, raised_values, precision=largest_value)
    return (levels_after_mixing, surface_flux_values.astype(jnp.bfloat16))

def ocean_update(padded, wet_pad, ocean_now, currents_now, forcing, drift_field, vertical_mixing_map):
    wet_here = wet_pad[1:-1, 1:-1]
    east_diff = wet_pad[1:-1, 2:] * (padded[:, :, 1:-1, 2:] - ocean_now)
    west_diff = wet_pad[1:-1, :-2] * (padded[:, :, 1:-1, :-2] - ocean_now)
    north_diff = wet_pad[2:, 1:-1] * (padded[:, :, 2:, 1:-1] - ocean_now)
    south_diff = wet_pad[:-2, 1:-1] * (padded[:, :, :-2, 1:-1] - ocean_now)
    spread = diffusion * (east_diff + west_diff + north_diff + south_diff)
    carried = 0.5 * (drift_field[0] * (east_diff - west_diff) + drift_field[1] * (north_diff - south_diff))
    stepped = ocean_now + wet_here * (spread - carried)
    surface = jnp.stack([-surface_heat * forcing[0], surface_salt * forcing[1]]) * wet_here
    stepped = stepped.at[:, 0].add(surface)
    levels_after_mixing = jnp.einsum('kl,slyx->skyx', vertical_mixing_map, stepped, precision=largest_value)
    current_east = currents_now[0] + wet_here * (surface_push * forcing[2] - current_drag * currents_now[0] + coriolis * currents_now[1])
    current_north = currents_now[1] + wet_here * (surface_push * forcing[3] - current_drag * currents_now[1] - coriolis * currents_now[0])
    return (levels_after_mixing, jnp.stack([current_east, current_north]))

def section_index(outgoing_block_table, arrival_slot_table):
    slot_count = outgoing_block_table.shape[3]
    source_peer = (arrival_slot_table // slot_count).astype(jnp.int32)
    slot_within = (arrival_slot_table % slot_count).astype(jnp.int32)
    comp_index = jnp.arange(N_COMP, dtype=jnp.int32)[:, None, None]
    dest_index = jnp.arange(SECTION, dtype=jnp.int32)[None, :, None]
    block_sent = outgoing_block_table[comp_index, source_peer, dest_index, slot_within]
    return ((comp_index * SECTION + source_peer) * ATM_BLOCKS + block_sent).astype(jnp.int32)

def to_devices(field):
    field_count = field.shape[0]
    split_grid = field.reshape(field_count, N_COMP, N_ROW, OCEAN_ROWS, N_COL, OCEAN_COLS)
    reordered = jnp.transpose(split_grid, (1, 2, 4, 0, 3, 5))
    return reordered.reshape(N_COMP * SECTION, field_count, OCEAN_BLOCKS, 64)

def from_devices(device_blocks):
    field_count = device_blocks.shape[1]
    split_grid = device_blocks.reshape(N_COMP, N_ROW, N_COL, field_count, OCEAN_ROWS, OCEAN_COLS)
    reordered = jnp.transpose(split_grid, (3, 0, 1, 4, 2, 5))
    return reordered.reshape(field_count, GRID_ROWS, GRID_COLS)

def remap_forward(surface_flux_values, remap_weight_tiles, block_index):
    source_blocks = jnp.transpose(surface_flux_values.reshape(4, N_COMP * SECTION * ATM_BLOCKS, 64), (1, 0, 2))
    flat_index = block_index.reshape(N_COMP * SECTION, CONTRIBUTIONS)
    flat_tiles = remap_weight_tiles.reshape(N_COMP * SECTION, CONTRIBUTIONS, 64, 64)

    def per_device(device_item):
        chosen, square = device_item
        source = source_blocks[chosen].astype(jnp.float32)
        product = jnp.einsum('jfc,jic->fji', source, square.astype(jnp.float32), precision=largest_value)
        summed = product.reshape(4, OCEAN_BLOCKS, SOURCES, 64).sum(axis=2)
        return summed.reshape(4, OCEAN_ROWS, OCEAN_COLS)
    return from_devices(lax.map(per_device, (flat_index, flat_tiles)))

def remap_back(surface_fields, remap_weight_tiles, block_index):
    local_fields = to_devices(surface_fields)
    flat_tiles = remap_weight_tiles.reshape(N_COMP * SECTION, OCEAN_BLOCKS, SOURCES, 64, 64)

    def per_device(device_item):
        surface_blocks, square = device_item
        terms = jnp.einsum('fbi,bkic->bkfc', surface_blocks.astype(jnp.float32), square.astype(jnp.float32), precision=largest_value)
        return terms.reshape(CONTRIBUTIONS, 3, 64)
    partial_terms = lax.map(per_device, (local_fields, flat_tiles))
    block_totals = jax.ops.segment_sum(partial_terms.reshape(-1, 3, 64), block_index.reshape(-1), num_segments=N_COMP * SECTION * ATM_BLOCKS)
    return jnp.transpose(block_totals, (1, 0, 2)).reshape(3, ATMOS_COLUMNS)

def reference(atmosphere_level_state, atmosphere_mixing_map, sea_surface_temps, tracers, currents, ocean_advect_velocity, ocean_mixing_map, ocean_cell_mask, remap_weight_tiles, outgoing_block_table, arrival_slot_table):
    block_index = section_index(outgoing_block_table, arrival_slot_table)
    wet_pad = jnp.pad(ocean_cell_mask.astype(jnp.float32), 1)
    drift_field = ocean_advect_velocity.astype(jnp.float32)
    air_column_state = atmosphere_level_state
    ocean_now = tracers
    currents_now = currents
    for moment in range(MICRO_STEPS):
        air_column_state, surface_flux_values = advance_atmosphere(air_column_state, sea_surface_temps, atmosphere_mixing_map)
        forcing = remap_forward(lax.optimization_barrier(surface_flux_values), remap_weight_tiles, block_index)
        padded = jnp.pad(ocean_now, ((0, 0), (0, 0), (1, 1), (1, 1)))
        ocean_now, currents_now = ocean_update(padded, wet_pad, ocean_now, currents_now, forcing, drift_field, ocean_mixing_map)
    surface_fields = jnp.stack([ocean_now[0, 0], currents_now[0], currents_now[1]]).astype(jnp.bfloat16)
    returned = remap_back(lax.optimization_barrier(surface_fields), remap_weight_tiles, block_index)
    return (air_column_state, ocean_now, currents_now, returned)
```

```python
import functools

import jax
import jax.numpy as jnp
from jax import lax
from jax.experimental import pallas as pl
from jax.experimental.pallas import tpu as pltpu
from jax.sharding import PartitionSpec as P

STEPS = 6
HALO = 6
ROWS = 8
EXT = ROWS + 2 * HALO
LANES = 128
WIDE = 256
HIGHEST = lax.Precision.HIGHEST
VMEM_LIMIT = 48 * 1024 * 1024

heat_rate = 0.5
vapour_rate = 0.5
drag_rate = 0.3
saturation = 0.6
flux_gains = (0.3, 0.3, -0.3, -0.3)
diffusion = 0.15
surface_gain = (-0.3, 0.3)
surface_push = 0.3
current_drag = 0.1
coriolis = 0.2

f32 = jnp.float32
bf16 = jnp.bfloat16


def call(body, out_shape, name, smem_inputs=0, inputs=1, scratch=(), cost=None):
    specs = [pl.BlockSpec(memory_space=pltpu.SMEM)] * smem_inputs
    specs += [pl.BlockSpec(memory_space=pltpu.VMEM)] * (inputs - smem_inputs)
    return pl.pallas_call(
        body,
        out_shape=out_shape,
        in_specs=specs,
        out_specs=jax.tree.map(lambda _: pl.BlockSpec(memory_space=pltpu.VMEM), out_shape),
        scratch_shapes=list(scratch),
        compiler_params=pltpu.CompilerParams(vmem_limit_bytes=VMEM_LIMIT),
        cost_estimate=cost,
        name=name,
    )


def shape(dims, dtype=f32):
    return jax.ShapeDtypeStruct(dims, dtype)


def exact(a, b):
    return jnp.dot(a, b, precision=HIGHEST, preferred_element_type=f32)


def halves(x):
    high = x.astype(bf16)
    return high, (x - high.astype(f32)).astype(bf16)


def flux_body(a_ref, m_ref, sst_ref, pay_ref, g_ref, top_ref, edge_ref):
    levels = m_ref.shape[0]
    bottom = levels - 1
    power = {1: m_ref[...]}
    power[2] = exact(power[1], power[1])
    power[3] = exact(power[1], power[2])
    power[4] = exact(power[2], power[2])
    power[5] = exact(power[2], power[3])
    power[6] = exact(power[3], power[3])
    first = (lax.broadcasted_iota(jnp.int32, (1, levels), 1) == bottom).astype(f32)
    rows = [first] + [power[n][bottom:, :] for n in range(1, STEPS)]
    rows = jnp.concatenate(rows + [jnp.zeros((8 - STEPS, levels), f32)], axis=0)
    row_high, row_low = halves(rows)
    both = jnp.concatenate([row_high.astype(f32), row_low.astype(f32)], axis=0).astype(bf16)
    base = []
    for v in range(4):
        high, low = halves(a_ref[v])
        one = jnp.dot(both, high, preferred_element_type=f32)
        two = jnp.dot(row_high, low, preferred_element_type=f32)
        base.append(one[:8] + one[8:] + two)
    corner = {n: power[n][bottom:, bottom:] for n in range(1, STEPS)}
    sst = sst_ref[...]
    gained = []
    fluxes = []
    for n in range(STEPS):
        now = []
        for v in range(4):
            value = base[v][n : n + 1]
            for k in range(n):
                value = value + corner[n - k] * gained[k][v]
            now.append(value)
        wind = jnp.sqrt(now[2] * now[2] + now[3] * now[3] + 1.0)
        flux = (
            heat_rate * wind * (sst - now[0]),
            vapour_rate * wind * (saturation * sst - now[1]),
            drag_rate * wind * now[2],
            drag_rate * wind * now[3],
        )
        fluxes.append(flux)
        gained.append([flux_gains[v] * flux[v] for v in range(4)])
    ordered = jnp.concatenate([fluxes[n][v] for v in range(4) for n in range(STEPS)], axis=0)
    count = ordered.shape[1] // LANES
    pay_ref[...] = jnp.concatenate(
        [ordered[:, q * LANES : (q + 1) * LANES] for q in range(count)], axis=0
    ).astype(bf16)
    blank = [jnp.zeros_like(sst)] * (8 - STEPS)
    for v in range(4):
        g_ref[v] = jnp.concatenate([gained[n][v] for n in range(STEPS)] + blank, axis=0)
    top_ref[...] = power[6]
    lane = lax.broadcasted_iota(jnp.int32, (levels, 8), 1)
    edge = jnp.zeros((levels, 8), f32)
    for n in range(STEPS):
        edge = jnp.where(lane == n, power[STEPS - n][:, bottom:], edge)
    edge_ref[...] = edge


def atmosphere_body(a_ref, g_ref, top_ref, edge_ref, out_ref):
    for v in range(4):
        out_ref[v] = exact(top_ref[...], a_ref[v]) + exact(edge_ref[...], g_ref[v])


def pack_body(z_ref, first_ref, last_ref):
    depth = z_ref.shape[1]
    lane = lax.broadcasted_iota(jnp.int32, (depth, LANES), 1)
    first = jnp.zeros((depth, LANES), f32)
    last = jnp.zeros((depth, LANES), f32)
    for r in range(EXT):
        row = z_ref[r].astype(f32)
        here = (lane >= r * HALO) & (lane < (r + 1) * HALO)
        first = jnp.where(here, pltpu.roll(row, (r * HALO) % LANES, 1), first)
        last = jnp.where(here, pltpu.roll(row, (r * HALO + HALO) % LANES, 1), last)
    first_ref[...] = first.astype(bf16)
    last_ref[...] = last.astype(bf16)


def level_mix(mix, stepped):
    high, low = halves(stepped)
    return jnp.dot(mix, jnp.concatenate([high, high, low], axis=0), preferred_element_type=f32)


def coefficient_body(
    before_ref, own_ref, after_ref, west_ref, east_ref, x_ref, mix_ref, coef_ref, x1_ref, wet_ref, ext_ref, wide_ref
):
    levels = x_ref.shape[2]
    lane = lax.broadcasted_iota(jnp.int32, (1, LANES), 1)

    def row_of(r, lo, size):
        if r < HALO:
            main = before_ref[r, lo : lo + size, :]
        elif r < HALO + ROWS:
            main = own_ref[r - HALO, lo : lo + size, :]
        else:
            main = after_ref[r - HALO - ROWS, lo : lo + size, :]
        return main.astype(f32)

    def side_of(r, lo, size):
        east = pltpu.roll(east_ref[lo : lo + size, :].astype(f32), (LANES - r * HALO) % LANES, 1)
        west = pltpu.roll(
            west_ref[lo : lo + size, :].astype(f32), (LANES - HALO - r * HALO) % LANES, 1
        )
        side = jnp.where(lane < HALO, east, 0.0)
        return jnp.where(lane >= LANES - HALO, west, side)

    for r in range(EXT):
        for t in range(2):
            lo = t * levels
            if HALO <= r < HALO + ROWS:
                main = x_ref[r - HALO, t]
            else:
                main = row_of(r, lo, levels)
            ext_ref[t, r, :, :LANES] = main
            ext_ref[t, r, :, LANES:] = side_of(r, lo, levels)
            lo = (2 + t) * levels
            wide_ref[t, r, :, :LANES] = row_of(r, lo, levels)
            wide_ref[t, r, :, LANES:] = side_of(r, lo, levels)
        lo = 4 * levels
        wet_ref[r, :, :LANES] = row_of(r, lo, 16)[:8]
        wet_ref[r, :, LANES:] = side_of(r, lo, 16)[:8]

    def row(r, carry):
        wet = wet_ref[r, 0:1]
        east = wet * pltpu.roll(wet, WIDE - 1, 1)
        west = wet * pltpu.roll(wet, 1, 1)
        north = wet * wet_ref[r + 1, 0:1]
        south = wet * wet_ref[r - 1, 0:1]
        along = 0.5 * wide_ref[0, r]
        across = 0.5 * wide_ref[1, r]
        c_east = east * (diffusion - along)
        c_west = west * (diffusion + along)
        c_north = north * (diffusion - across)
        c_south = south * (diffusion + across)
        c_here = 1.0 - ((c_east + c_west) + (c_north + c_south))
        coef_ref[0, r] = c_here
        coef_ref[1, r] = c_east
        coef_ref[2, r] = c_west
        coef_ref[3, r] = c_north
        coef_ref[4, r] = c_south
        for t in range(2):
            x = ext_ref[t, r]
            stepped = (
                c_here * x
                + (c_east * pltpu.roll(x, WIDE - 1, 1) + c_west * pltpu.roll(x, 1, 1))
                + (c_north * ext_ref[t, r + 1] + c_south * ext_ref[t, r - 1])
            )
            x1_ref[t, r] = level_mix(mix_ref[...], stepped)
        return carry

    lax.fori_loop(1, EXT - 1, row, 0)


def remap_body(pick_ref, g_ref, w_ref, west_ref, east_ref, f_ref, main_ref, up_ref, down_ref):
    lane = lax.broadcasted_iota(jnp.int32, (24, LANES), 1)
    left = lane < 64

    def pick(at, half):
        t = pick_ref[at]
        window = g_ref[t >> 3, pl.ds(pl.multiple_of(((t >> 2) & 1) * 48, 16), 48), :].astype(f32)
        block = jnp.where(((t >> 1) & 1) == 1, window[24:], window[:24])
        return jnp.where((t & 1) == half, block, pltpu.roll(block, 64, 1))

    def row(r, carry):
        for part in range(2):
            start = (r * 2 + part) * 8
            sources = []
            for side in range(2):
                tiles = []
                for pair in range(2):
                    at = start + side * 4 + pair * 2
                    tiles.append(jnp.where(left, pick(at, 0), pick(at + 1, 1)))
                sources.append(jnp.concatenate(tiles, axis=1))
            sources = jnp.concatenate(sources, axis=0).astype(bf16)
            if part == 0:
                weights = w_ref[r]
            else:
                weights = jnp.concatenate(
                    [east_ref[r], jnp.zeros((96, WIDE), bf16), west_ref[r]], axis=0
                )
            product = lax.dot_general(
                sources, weights, (((1,), (1,)), ((), ())), preferred_element_type=f32
            )
            forcing = jnp.where(left, product[:24], product[24:])
            f_ref[r, :, part * LANES : (part + 1) * LANES] = forcing
            if part == 0:
                main_ref[r] = forcing
        return carry

    lax.fori_loop(0, ROWS, row, 0)
    for i in range(HALO - 1):
        up_ref[i] = f_ref[ROWS - HALO + 1 + i, :16, :].astype(bf16)
        down_ref[i] = f_ref[i, :16, :].astype(bf16)


def returned_rows(fields, w_ref, place, rows, step):
    blocks = 2 * ROWS
    block = lax.broadcasted_iota(jnp.int32, (blocks, LANES), 0)
    lane = lax.broadcasted_iota(jnp.int32, (blocks, LANES), 1)
    spread = []
    for field in fields:
        parts = []
        for r in range(ROWS):
            mine = block == 2 * r + (lane >= 64).astype(jnp.int32)
            parts.append(jnp.where(mine, field[r : r + 1], 0.0))
        spread.append(jnp.concatenate(parts, axis=1))
    spread = jnp.concatenate(spread, axis=0).astype(bf16)
    cells = w_ref[...].reshape(ROWS * LANES, WIDE)
    terms = jnp.dot(spread, cells, preferred_element_type=f32)
    high_parts, low_parts, ones = [], [], []
    target = lax.broadcasted_iota(jnp.int32, (rows, LANES), 0)
    for f in range(len(fields)):
        mine = terms[f * blocks : (f + 1) * blocks]
        pieces = []
        for half in range(2):
            for k in range(4):
                piece = mine[:, (k // 2) * LANES : (k // 2 + 1) * LANES]
                if k % 2 != half:
                    piece = pltpu.roll(piece, 64, 1)
                pieces.append(jnp.where((lane >= 64) == (half == 1), piece, 0.0))
        high, low = halves(jnp.concatenate(pieces, axis=0))
        high_parts.append(high)
        low_parts.append(low)
        ones.append((target == place + f * step).astype(f32).astype(bf16))
    return jnp.dot(
        jnp.concatenate(ones + ones, axis=1),
        jnp.concatenate(high_parts + low_parts, axis=0),
        preferred_element_type=f32,
    )


def current_body(f_ref, u_ref, wet_ref, w_ref, place_ref, u_out_ref, send_ref):
    wet = wet_ref[...].astype(f32)
    east, north = u_ref[0], u_ref[1]
    for n in range(STEPS):
        push_east = surface_push * f_ref[pl.ds(12 + n, ROWS, stride=24), :]
        push_north = surface_push * f_ref[pl.ds(18 + n, ROWS, stride=24), :]
        east, north = (
            east + wet * (push_east - current_drag * east + coriolis * north),
            north + wet * (push_north - current_drag * north - coriolis * east),
        )
    u_out_ref[0] = east
    u_out_ref[1] = north
    fields = [east.astype(bf16).astype(f32), north.astype(bf16).astype(f32)]
    send_ref[...] = returned_rows(fields, w_ref, place_ref[...], send_ref.shape[0], 4)


def tracer_body(t, with_send, *refs):
    x1_ref, coef_ref, wet_ref, mix_ref, column_ref, f_ref, before_ref, after_ref = refs[:8]
    if with_send:
        w_ref, place_ref, out_ref, send_ref, one_ref, two_ref, force_ref, sst_ref = refs[8:]
    else:
        out_ref, one_ref, two_ref, force_ref = refs[8:]
    levels = mix_ref.shape[0]
    for r in range(1, EXT - 1):
        if r < HALO:
            forcing = before_ref[r - 1, :16, :].astype(f32)
        elif r < HALO + ROWS:
            forcing = f_ref[r - HALO, :16, :]
        else:
            forcing = after_ref[r - HALO - ROWS, :16, :].astype(f32)
        gain = surface_gain[t] * wet_ref[r]
        force_ref[r] = jnp.concatenate([gain, gain], axis=0) * forcing
    column = jnp.broadcast_to(column_ref[:, 0:1], (levels, WIDE))

    def start(r, carry):
        one_ref[r] = x1_ref[t, r] + column * force_ref[r, 6 * t : 6 * t + 1]
        return carry

    lax.fori_loop(1, EXT - 1, start, 0, unroll=2)
    first_level = lax.broadcasted_iota(jnp.int32, (8, WIDE), 0) == 0
    old, new = one_ref, two_ref
    for n in range(1, STEPS):
        last = n == STEPS - 1
        width = LANES if last else WIDE

        def stepped_row(r, old=old, n=n, width=width):
            x = old[r]
            east, west = pltpu.roll(x, WIDE - 1, 1), pltpu.roll(x, 1, 1)
            stepped = (
                coef_ref[0, r, :, :width] * x[:, :width]
                + (coef_ref[1, r, :, :width] * east[:, :width]
                   + coef_ref[2, r, :, :width] * west[:, :width])
                + (coef_ref[3, r, :, :width] * old[r + 1, :, :width]
                   + coef_ref[4, r, :, :width] * old[r - 1, :, :width])
            )
            at = 6 * t + n
            gain = jnp.where(first_level[:, :width], force_ref[r, at : at + 1, :width], 0.0)
            return jnp.concatenate([stepped[:8] + gain, stepped[8:]], axis=0)

        def pair(i, carry, old=old, new=new, n=n, last=last, width=width, stepped_row=stepped_row):
            r = n + 1 + 2 * i
            mixed = level_mix(
                mix_ref[...], jnp.concatenate([stepped_row(r), stepped_row(r + 1)], axis=1)
            )
            for s in range(2):
                value = mixed[:, s * width : (s + 1) * width]
                if last:
                    row = r + s - HALO
                    out_ref[pl.ds(row, levels, stride=ROWS), :] = value
                    if with_send:
                        sst_ref[pl.ds(row, 1), :] = value[0:1]
                else:
                    new[r + s] = value
            return carry

        lax.fori_loop(0, (EXT - 2 - 2 * n) // 2, pair, 0)
        old, new = new, old
    if with_send:
        field = sst_ref[...].astype(bf16).astype(f32)
        send_ref[...] = returned_rows([field], w_ref, place_ref[...], send_ref.shape[0], 0)


def neighbours(size):
    up = [(i, i + 1) for i in range(size - 1)]
    return up, [(j, i) for i, j in up]


def on_device(
    atmosphere_level_state,
    atmosphere_mixing_map,
    sea_surface_temps,
    tracers,
    currents,
    ocean_advect_velocity,
    ocean_mixing_map,
    ocean_cell_mask,
    remap_weight_tiles,
    outgoing_block_table,
    arrival_slot_table,
):
    band = ("row", "col")
    peers = lax.axis_size(band)
    levels = tracers.shape[1]
    air_levels, air_columns = atmosphere_level_state.shape[1:]
    up, down = neighbours(lax.axis_size(("comp", "row")))
    right, leftward = neighbours(lax.axis_size("col"))
    col_count = lax.axis_size("col")
    col = lax.axis_index("col")
    me = lax.axis_index(band)

    table = jnp.concatenate(
        [
            outgoing_block_table.reshape(peers * 2),
            arrival_slot_table.reshape(64),
            jnp.zeros((-(2 * peers + 64) % LANES,), jnp.int32),
        ]
    ).reshape(-1, LANES)
    tables = lax.all_gather(table, band).reshape(peers, -1)

    payload, gained, top, edge = call(
        flux_body,
        (
            shape((24 * air_columns // LANES, LANES), bf16),
            shape((4, 8, air_columns)),
            shape((air_levels, air_levels)),
            shape((air_levels, 8)),
        ),
        "fluxes",
        inputs=3,
    )(atmosphere_level_state, atmosphere_mixing_map, sea_surface_temps[None])
    gathered = lax.all_gather(payload, band)
    atm_final = call(
        atmosphere_body, shape(atmosphere_level_state.shape), "atmosphere", inputs=4
    )(atmosphere_level_state, gained, top, edge)

    def sources(device):
        arrival = lax.dynamic_slice(tables, (device, 2 * peers), (1, 64))[0]
        blocks = lax.dynamic_slice(tables, (0, 2 * device), (peers, 2)).reshape(2 * peers)
        slot = jnp.arange(2 * peers, dtype=jnp.int32)
        block = jnp.sum(jnp.where(arrival[:, None] == slot[None], blocks[None], 0), axis=1)
        return (arrival // 2) * 8 + jnp.maximum(block, 0)

    own = sources(me)
    east_of = sources(jnp.where(col < col_count - 1, me + 1, me))
    west_of = sources(jnp.where(col > 0, me - 1, me))
    own_rows = own.reshape(ROWS, 1, 8)
    side_rows = jnp.concatenate(
        [east_of.reshape(ROWS, 1, 2, 4)[:, :, 0], west_of.reshape(ROWS, 1, 2, 4)[:, :, 1]], axis=2
    )
    picks = jnp.concatenate([own_rows, side_rows], axis=1).reshape(16 * ROWS)
    by_k = own.reshape(2 * ROWS, 4).T.reshape(64)
    half = by_k & 1
    twice = jnp.stack([jnp.where(half == 0, by_k, -1), jnp.where(half == 1, by_k, -1)]).reshape(1, LANES)
    device_of, pair_of = twice >> 3, (twice >> 1) & 3
    place_two = jnp.where(twice >= 0, device_of * 8 + pair_of, -64)
    place_one = jnp.where(twice >= 0, device_of * 4 + pair_of, -64)

    by_row = jnp.transpose(tracers, (2, 0, 1, 3))
    flow = jnp.transpose(ocean_advect_velocity, (2, 0, 1, 3))
    wet16 = jnp.broadcast_to(ocean_cell_mask.astype(bf16)[:, None, :], (ROWS, 16, LANES))
    z = jnp.concatenate(
        [
            by_row.astype(bf16).reshape(ROWS, 2 * levels, LANES),
            flow.reshape(ROWS, 2 * levels, LANES),
            wet16,
        ],
        axis=1,
    )
    rows_axis = ("comp", "row")
    before = lax.ppermute(z[ROWS - HALO :], rows_axis, up)
    after = lax.ppermute(z[:HALO], rows_axis, down)
    depth = z.shape[1]
    first, last = call(
        pack_body, (shape((depth, LANES), bf16), shape((depth, LANES), bf16)), "pack"
    )(jnp.concatenate([before, z, after], axis=0))
    cells = (
        remap_weight_tiles.reshape(2 * ROWS, 4, 64, 64)
        .transpose(0, 2, 1, 3)
        .reshape(ROWS, LANES, WIDE)
    )
    first = jnp.concatenate([first, cells[:, :16].reshape(-1, LANES)], axis=0)
    last = jnp.concatenate([last, cells[:, LANES - 16 :].reshape(-1, LANES)], axis=0)
    east_in = lax.ppermute(first, "col", leftward)
    west_in = lax.ppermute(last, "col", right)
    east_cells = east_in[depth:].reshape(ROWS, 16, WIDE)
    west_cells = west_in[depth:].reshape(ROWS, 16, WIDE)
    rounded = lax.reduce_precision(ocean_mixing_map, 8, 7)
    high, low = rounded.astype(bf16), (ocean_mixing_map - rounded).astype(bf16)
    mix = jnp.concatenate([high, low, high], axis=1)
    coef, x1, wet = call(
        coefficient_body,
        (
            shape((5, EXT, levels, WIDE)),
            shape((2, EXT, levels, WIDE)),
            shape((EXT, 8, WIDE)),
        ),
        "coefficients",
        inputs=7,
        scratch=(
            pltpu.VMEM((2, EXT, levels, WIDE), f32),
            pltpu.VMEM((2, EXT, levels, WIDE), f32),
        ),
    )(before, z, after, west_in[:depth], east_in[:depth], by_row, mix)

    forcing, own_forcing, send_up, send_down = call(
        remap_body,
        (
            shape((ROWS, 24, WIDE)),
            shape((ROWS, 24, LANES)),
            shape((HALO - 1, 16, WIDE), bf16),
            shape((HALO - 1, 16, WIDE), bf16),
        ),
        "remap",
        smem_inputs=1,
        inputs=5,
    )(picks, gathered, cells, west_cells, east_cells)
    f_before = lax.ppermute(send_up, rows_axis, up)
    f_after = lax.ppermute(send_down, rows_axis, down)

    ocean_currents, current_terms = call(
        current_body,
        (shape(currents.shape), shape((peers * 8, LANES))),
        "currents",
        inputs=5,
    )(own_forcing.reshape(ROWS * 24, LANES), currents, ocean_cell_mask, cells, place_two)
    current_back = lax.psum_scatter(
        current_terms.reshape(peers, 8, LANES), band, scatter_dimension=0, tiled=False
    )

    shared = (x1, coef, wet, mix, ocean_mixing_map, forcing, f_before, f_after)
    scratch = [
        pltpu.VMEM((EXT, levels, WIDE), f32),
        pltpu.VMEM((EXT, levels, WIDE), f32),
        pltpu.VMEM((EXT, 16, WIDE), f32),
    ]
    warm, warm_terms = call(
        functools.partial(tracer_body, 0, True),
        (shape((levels * ROWS, LANES)), shape((peers * 4, LANES))),
        "temperature",
        inputs=10,
        scratch=scratch + [pltpu.VMEM((ROWS, LANES), f32)],
    )(*shared, cells, place_one)
    warm_back = lax.psum_scatter(
        warm_terms.reshape(peers, 4, LANES), band, scatter_dimension=0, tiled=False
    )
    salt = call(
        functools.partial(tracer_body, 1, False),
        shape((levels * ROWS, LANES)),
        "salinity",
        inputs=8,
        scratch=scratch,
    )(*shared)
    ocean_tracers = jnp.stack([warm, salt]).reshape(tracers.shape)
    returned = jnp.concatenate(
        [warm_back.reshape(1, air_columns), current_back.reshape(2, air_columns)], axis=0
    )
    return (atm_final, ocean_tracers, ocean_currents, returned)


def solution(mesh):
    return jax.shard_map(
        on_device,
        mesh=mesh,
        in_specs=(
            P(None, None, ("comp", "row", "col")),
            P(),
            P(("comp", "row", "col")),
            P(None, None, ("comp", "row"), "col"),
            P(None, ("comp", "row"), "col"),
            P(None, None, ("comp", "row"), "col"),
            P(),
            P(("comp", "row"), "col"),
            P("comp", ("row", "col"), None, None),
            P("comp", ("row", "col"), None, None),
            P("comp", ("row", "col"), None),
        ),
        out_specs=(
            P(None, None, ("comp", "row", "col")),
            P(None, None, ("comp", "row"), "col"),
            P(None, ("comp", "row"), "col"),
            P(None, ("comp", "row", "col")),
        ),
        check_vma=False,
    )
```

```python
import functools

import jax
import jax.numpy as jnp
import numpy as np
from jax import lax
from jax.experimental import pallas as pl
from jax.experimental.pallas import tpu as pltpu
from jax.sharding import PartitionSpec as P

STEPS = 6
HALO = 6
ROWS = 8
EXT = ROWS + 2 * HALO
WEST, EAST = EXT, EXT + 1
STRIPS = EXT + 2
LANES = 128
WIDE = 256
HIGHEST = lax.Precision.HIGHEST
VMEM_LIMIT = 48 * 1024 * 1024

heat_rate = 0.5
vapour_rate = 0.5
drag_rate = 0.3
saturation = 0.6
flux_gains = (0.3, 0.3, -0.3, -0.3)
diffusion = 0.15
surface_gain = (-0.3, 0.3)
surface_push = 0.3
current_drag = 0.1
coriolis = 0.2
turn = np.array([[1.0 - current_drag, coriolis], [-coriolis, 1.0 - current_drag]])

f32 = jnp.float32
bf16 = jnp.bfloat16
VMEM = pl.BlockSpec(memory_space=pltpu.VMEM)
HBM = pl.BlockSpec(memory_space=pltpu.HBM)


def call(body, out_shape, name, in_specs, out_specs=None, scratch=(), aliases=None):
    if out_specs is None:
        out_specs = jax.tree.map(lambda _: VMEM, out_shape)
    return pl.pallas_call(
        body,
        out_shape=out_shape,
        in_specs=in_specs,
        out_specs=out_specs,
        scratch_shapes=list(scratch),
        input_output_aliases=aliases or {},
        compiler_params=pltpu.CompilerParams(vmem_limit_bytes=VMEM_LIMIT),
        name=name,
    )


def shape(dims, dtype=f32):
    return jax.ShapeDtypeStruct(dims, dtype)


def exact(a, b):
    return jnp.dot(a, b, precision=HIGHEST, preferred_element_type=f32)


def times(a, b):
    return jnp.dot(a, b, preferred_element_type=f32)


def times_rows(a, b):
    return lax.dot_general(a, b, (((1,), (1,)), ((), ())), preferred_element_type=f32)


def iota(dims, axis):
    return lax.broadcasted_iota(jnp.int32, dims, axis)


def one_hot(condition):
    return condition.astype(f32).astype(bf16)


def halves(x):
    high = x.astype(bf16)
    return high, (x - high.astype(f32)).astype(bf16)


def flux_body(a_hbm, m_ref, sst_ref, table_ref, pay_ref, g_ref, top_ref, edge_ref, a_ref, sem):
    copy = pltpu.make_async_copy(a_hbm, a_ref, sem)
    copy.start()
    levels = m_ref.shape[0]
    bottom = levels - 1
    power = {1: m_ref[...]}
    power[2] = exact(power[1], power[1])
    power[3] = exact(power[1], power[2])
    power[4] = exact(power[2], power[2])
    power[5] = exact(power[2], power[3])
    power[6] = exact(power[3], power[3])
    first = (iota((1, levels), 1) == bottom).astype(f32)
    rows = [first] + [power[n][bottom:, :] for n in range(1, STEPS)]
    rows = jnp.concatenate(rows + [jnp.zeros((8 - STEPS, levels), f32)], axis=0)
    row_high, row_low = halves(rows)
    both = jnp.concatenate([row_high.astype(f32), row_low.astype(f32)], axis=0).astype(bf16)
    top_ref[...] = power[6]
    lane = iota((levels, 8), 1)
    edge = jnp.zeros((levels, 8), f32)
    for n in range(STEPS):
        edge = jnp.where(lane == n, power[STEPS - n][:, bottom:], edge)
    edge_ref[...] = edge
    copy.wait()
    base = []
    for v in range(4):
        high, low = halves(a_ref[v])
        one = times(both, high)
        base.append(one[:8] + one[8:] + times(row_high, low))
    corner = {n: power[n][bottom:, bottom:] for n in range(1, STEPS)}
    sst = sst_ref[...]
    gained = []
    fluxes = []
    east, north = jnp.zeros_like(sst), jnp.zeros_like(sst)
    for n in range(STEPS):
        now = []
        for v in range(4):
            value = base[v][n : n + 1]
            for k in range(n):
                value = value + corner[n - k] * gained[k][v]
            now.append(value)
        wind = jnp.sqrt(now[2] * now[2] + now[3] * now[3] + 1.0)
        flux = (
            heat_rate * wind * (sst - now[0]),
            vapour_rate * wind * (saturation * sst - now[1]),
            drag_rate * wind * now[2],
            drag_rate * wind * now[3],
        )
        fluxes.append(flux)
        gained.append([flux_gains[v] * flux[v] for v in range(4)])
        east, north = (
            turn[0, 0] * east + turn[0, 1] * north + flux[2],
            turn[1, 0] * east + turn[1, 1] * north + flux[3],
        )
    blank = [jnp.zeros_like(sst)] * (8 - STEPS)
    for v in range(4):
        g_ref[v] = jnp.concatenate([gained[n][v] for n in range(STEPS)] + blank, axis=0)
    pairs = [(fluxes[n][0], fluxes[n][1]) for n in range(STEPS)] + [(east, north)]
    peers = table_ref.shape[0]
    block = iota((8, LANES), 0)
    left = iota((8, LANES), 1) < 64
    even = block % 2 == 0
    for i, pair in enumerate(pairs):
        parts = []
        for side in range(2):
            spread = jnp.zeros((8, LANES), f32)
            for q in range(4):
                tile = jnp.broadcast_to(pair[side][:, q * LANES : (q + 1) * LANES], (8, LANES))
                spread = jnp.where(block // 2 == q, tile, spread)
            parts.append(jnp.where(even == (side == 0), spread, pltpu.roll(spread, 64, 1)))
        tile = jnp.where(left, parts[0], parts[1])
        pay_ref[:, i * LANES : (i + 1) * LANES] = jnp.concatenate([tile] * peers, axis=0).astype(bf16)
    table = [jnp.broadcast_to(table_ref[r : r + 1, :], (8, LANES)) for r in range(peers)]
    pay_ref[:, 7 * LANES :] = jnp.concatenate(table, axis=0).astype(bf16)


def atmosphere_body(a_hbm, g_ref, top_ref, edge_ref, out_hbm, a_ref, sems, out_sems):
    loads = [pltpu.make_async_copy(a_hbm.at[v], a_ref.at[v], sems.at[v]) for v in range(4)]
    stores = [pltpu.make_async_copy(a_ref.at[v], out_hbm.at[v], out_sems.at[v]) for v in range(4)]
    for copy in loads:
        copy.start()
    for v in range(4):
        loads[v].wait()
        a_ref[v] = exact(top_ref[...], a_ref[v]) + exact(edge_ref[...], g_ref[v])
        stores[v].start()
    for copy in stores:
        copy.wait()


def select_body(in_ref, out_ref):
    slots, blocks = out_ref.shape[0], in_ref.shape[0]
    peers = blocks // 8
    row, lane = iota((slots, LANES), 0), iota((slots, LANES), 1)
    entry = (row // (2 * peers)) * 2 + row % 2
    named = times_rows(one_hot(lane == entry), in_ref[:, 7 * LANES :])
    row, lane = iota((slots, blocks), 0), iota((slots, blocks), 1)
    chosen = (named == (lane % 8).astype(f32)) & (lane // 8 == (row // 2) % peers)
    chosen = one_hot(chosen)
    out_ref[...] = times(chosen, in_ref[:, : 7 * LANES]).astype(bf16)


def gather_body(in_ref, back_ref, out_ref):
    slots, blocks = back_ref.shape[0], in_ref.shape[0]
    peers = blocks // 8
    row, lane = iota((slots, LANES), 0), iota((slots, LANES), 1)
    entry = (row // (2 * peers)) * 2 + row % 2
    named = times_rows(in_ref[:, 7 * LANES :], one_hot(lane == entry))
    row, lane = iota((blocks, slots), 0), iota((blocks, slots), 1)
    chosen = (named == (row % 8).astype(f32)) & (row // 8 == (lane // 2) % peers)
    out_ref[...] = times(one_hot(chosen), back_ref[...])


def finish_body(in_ref, out_ref):
    peers = in_ref.shape[0] // 8
    total = in_ref[:8]
    for r in range(1, peers):
        total = total + in_ref[8 * r : 8 * r + 8]
    left = iota((1, LANES), 1) < 64
    for f in range(3):
        tile = total[:, (f // 2) * LANES : (f // 2 + 1) * LANES]
        other = pltpu.roll(tile, 64, 1)
        low, high = (tile, other) if f % 2 == 0 else (other, tile)
        for q in range(4):
            out_ref[f : f + 1, q * LANES : (q + 1) * LANES] = jnp.where(
                left, low[2 * q : 2 * q + 1], high[2 * q + 1 : 2 * q + 2]
            )


def cells_body(w_hbm, out_ref, w_ref, t_ref, low_ref, high_ref, sem):
    copy = pltpu.make_async_copy(w_hbm, w_ref, sem)
    copy.start()
    copy.wait()
    left = iota((16, LANES), 1) < 64
    tiles = w_ref.shape[1] // LANES
    for i in range(tiles):
        t_ref[i * 64 : (i + 1) * 64] = w_ref[:, i * LANES : (i + 1) * LANES].astype(f32)
    for i in range(tiles):
        k = [t_ref[pl.ds(i * 64 + s, 16, stride=4), :] for s in range(4)]
        moved = [pltpu.roll(x, 64, 1) for x in k]
        low_ref[pl.ds(2 * i, 16, stride=64), :] = jnp.where(left, k[0], moved[1])
        high_ref[pl.ds(2 * i, 16, stride=64), :] = jnp.where(left, k[2], moved[3])
        low_ref[pl.ds(2 * i + 1, 16, stride=64), :] = jnp.where(left, moved[0], k[1])
        high_ref[pl.ds(2 * i + 1, 16, stride=64), :] = jnp.where(left, moved[2], k[3])
    out_ref[:, :LANES] = low_ref[...].astype(bf16)
    out_ref[:, LANES:] = high_ref[...].astype(bf16)


def rows_body(x_hbm, v_ref, wet_ref, z_ref, x_ref, f_ref, sem):
    copy = pltpu.make_async_copy(x_hbm, x_ref, sem)
    copy.start()
    levels = x_ref.shape[1] // ROWS
    for t in range(2):
        f_ref[t] = v_ref[t].astype(f32)
    for r in range(ROWS):
        for t in range(2):
            z_ref[r, (2 + t) * levels : (3 + t) * levels, :] = f_ref[
                t, pl.ds(r, levels, stride=ROWS), :
            ].astype(bf16)
        wet = jnp.broadcast_to(wet_ref[r : r + 1, :].astype(f32), (16, LANES))
        z_ref[r, 4 * levels :, :] = wet.astype(bf16)
    copy.wait()
    for r in range(ROWS):
        for t in range(2):
            z_ref[r, t * levels : (t + 1) * levels, :] = x_ref[
                t, pl.ds(r, levels, stride=ROWS), :
            ].astype(bf16)


def packed_edges(rows, depth):
    lane = iota((depth, LANES), 1)
    first = jnp.zeros((depth, LANES), f32)
    last = jnp.zeros((depth, LANES), f32)
    for r, row in rows:
        here = (lane >= r * HALO) & (lane < (r + 1) * HALO)
        first = jnp.where(here, pltpu.roll(row, (r * HALO) % LANES, 1), first)
        last = jnp.where(here, pltpu.roll(row, (r * HALO + HALO) % LANES, 1), last)
    return first.astype(bf16), last.astype(bf16)


def pack_body(before_ref, z_ref, after_ref, first_ref, last_ref):
    depth = z_ref.shape[1]

    def part(i, carry):
        at = pl.ds(pl.multiple_of(i * 16, 16), 16)
        rows = [(r, before_ref[r, at, :].astype(f32)) for r in range(HALO)]
        rows += [(HALO + r, z_ref[r, at, :].astype(f32)) for r in range(ROWS)]
        rows += [(HALO + ROWS + r, after_ref[r, at, :].astype(f32)) for r in range(HALO)]
        first_ref[at, :], last_ref[at, :] = packed_edges(rows, 16)
        return carry

    lax.fori_loop(0, depth // 16, part, 0)


def pack_forcing_body(f_ref, before_ref, after_ref, first_ref, last_ref):
    rows = [(r + 1, before_ref[r].astype(f32)) for r in range(HALO - 1)]
    rows += [(HALO + r, f_ref[16 * r : 16 * r + 16]) for r in range(ROWS)]
    rows += [(HALO + ROWS + r, after_ref[r].astype(f32)) for r in range(HALO - 1)]
    first_ref[...], last_ref[...] = packed_edges(rows, 16)


def along_row(here, west, east, r, lane):
    eastward = jnp.where(
        lane == LANES - 1, pltpu.roll(east, LANES - 1 - HALO * r, 1), pltpu.roll(here, LANES - 1, 1)
    )
    westward = jnp.where(
        lane == 0, pltpu.roll(west, LANES - HALO + 1 - HALO * r, 1), pltpu.roll(here, 1, 1)
    )
    return eastward, westward


def gathered_edges(here, r, lane, to_west, to_east):
    to_west = jnp.where(
        lane == HALO * r + HALO - 1, pltpu.roll(here, HALO * r + HALO - 1, 1), to_west
    )
    to_east = jnp.where(lane == HALO * r, pltpu.roll(here, HALO * r + 1, 1), to_east)
    return to_west, to_east


def around_strips(west, east, to_west, to_east, lane):
    north, south = LANES - HALO, HALO
    return (
        (
            jnp.where(lane % HALO == HALO - 1, to_west, pltpu.roll(west, LANES - 1, 1)),
            pltpu.roll(west, 1, 1),
            pltpu.roll(west, north, 1),
            pltpu.roll(west, south, 1),
        ),
        (
            pltpu.roll(east, LANES - 1, 1),
            jnp.where(lane % HALO == 0, to_east, pltpu.roll(east, 1, 1)),
            pltpu.roll(east, north, 1),
            pltpu.roll(east, south, 1),
        ),
    )


def ocean_step(n, x_ref, coef_ref, mix_ref, cat_ref, store, force=None):
    levels = mix_ref.shape[0]
    low, high = n + 1, EXT - 2 - n
    last = n == STEPS - 1
    rows = list(range(low, high + 1))
    lane = iota((16, LANES), 1)
    level = iota((16, LANES), 0)

    def part(c, carry):
        at = pl.multiple_of(c * 16, 16)
        here_at = pl.ds(at, 16)

        def put(i, idx, here, east, west, north, south):
            stepped = (
                coef_ref[0, idx, here_at, :] * here
                + (coef_ref[1, idx, here_at, :] * east + coef_ref[2, idx, here_at, :] * west)
                + (coef_ref[3, idx, here_at, :] * north + coef_ref[4, idx, here_at, :] * south)
            )
            if force is not None:
                stepped = stepped + jnp.where(level + at == 0, force(idx), 0.0)
            upper, lower = halves(stepped)
            cols = pl.ds(i * LANES, LANES)
            cat_ref[here_at, cols] = upper
            cat_ref[pl.ds(levels + at, 16), cols] = upper
            cat_ref[pl.ds(2 * levels + at, 16), cols] = lower

        west, east = x_ref[WEST, here_at, :], x_ref[EAST, here_at, :]
        to_west, to_east = jnp.zeros_like(west), jnp.zeros_like(east)
        south, here = x_ref[low - 1, here_at, :], x_ref[low, here_at, :]
        for i, r in enumerate(rows):
            north = x_ref[r + 1, here_at, :]
            eastward, westward = along_row(here, west, east, r, lane)
            put(i, r, here, eastward, westward, north, south)
            if not last:
                to_west, to_east = gathered_edges(here, r, lane, to_west, to_east)
            south, here = here, north
        if not last:
            of_west, of_east = around_strips(west, east, to_west, to_east, lane)
            put(len(rows), WEST, west, *of_west)
            put(len(rows) + 1, EAST, east, *of_east)
        return carry

    lax.fori_loop(0, levels // 16, part, 0)
    targets = rows + ([] if last else [WEST, EAST])
    for lo in range(0, len(targets), 4):
        some = targets[lo : lo + 4]
        mixed = times(mix_ref[...], cat_ref[:, lo * LANES : (lo + len(some)) * LANES])
        for i, idx in enumerate(some):
            store(idx, mixed[:, i * LANES : (i + 1) * LANES])


def coefficient_body(
    before_ref, z_ref, after_ref, west_ref, east_ref, x_hbm, mix_ref,
    coef_ref, x1_ref, wet_ref, x_ref, x0_ref, near_ref, cat_ref, sem,
):
    copy = pltpu.make_async_copy(x_hbm, x_ref, sem)
    copy.start()
    levels = mix_ref.shape[0]

    def of(idx, at):
        if idx == WEST:
            return west_ref[at, :].astype(f32)
        if idx == EAST:
            return east_ref[at, :].astype(f32)
        if idx < HALO:
            return before_ref[idx, at, :].astype(f32)
        if idx < HALO + ROWS:
            return z_ref[idx - HALO, at, :].astype(f32)
        return after_ref[idx - HALO - ROWS, at, :].astype(f32)

    lane = iota((8, LANES), 1)
    wets = [of(idx, pl.ds(4 * levels, 16))[:8] for idx in range(STRIPS)]
    to_west, to_east = jnp.zeros_like(lane, f32), jnp.zeros_like(lane, f32)
    for idx in range(STRIPS):
        wet_ref[idx] = wets[idx]
    sides = {}
    for r in range(1, EXT - 1):
        east, west = along_row(wets[r], wets[WEST], wets[EAST], r, lane)
        sides[r] = (east, west, wets[r + 1], wets[r - 1])
        to_west, to_east = gathered_edges(wets[r], r, lane, to_west, to_east)
    sides[WEST], sides[EAST] = around_strips(wets[WEST], wets[EAST], to_west, to_east, lane)
    for idx, near in sides.items():
        for s in range(4):
            near_ref[s, idx] = wets[idx] * near[s]

    def part(c, carry):
        at = pl.multiple_of(c * 16, 16)
        here_at = pl.ds(at, 16)
        for idx in sides:
            along = 0.5 * of(idx, pl.ds(2 * levels + at, 16))
            across = 0.5 * of(idx, pl.ds(3 * levels + at, 16))
            near = []
            for s in range(4):
                one = near_ref[s, idx]
                near.append(jnp.concatenate([one, one], axis=0))
            c_east = near[0] * (diffusion - along)
            c_west = near[1] * (diffusion + along)
            c_north = near[2] * (diffusion - across)
            c_south = near[3] * (diffusion + across)
            coef_ref[0, idx, here_at, :] = 1.0 - ((c_east + c_west) + (c_north + c_south))
            coef_ref[1, idx, here_at, :] = c_east
            coef_ref[2, idx, here_at, :] = c_west
            coef_ref[3, idx, here_at, :] = c_north
            coef_ref[4, idx, here_at, :] = c_south
        for t in range(2):
            for idx in range(STRIPS):
                if not HALO <= idx < HALO + ROWS:
                    x0_ref[t, idx, here_at, :] = of(idx, pl.ds(t * levels + at, 16))
        return carry

    lax.fori_loop(0, levels // 16, part, 0)
    copy.wait()
    for t in range(2):
        for r in range(ROWS):
            x0_ref[t, HALO + r] = x_ref[t, pl.ds(r, levels, stride=ROWS), :]
    for t in range(2):

        def store(idx, value, t=t):
            x1_ref[t, idx] = value

        ocean_step(0, x0_ref.at[t], coef_ref, mix_ref, cat_ref, store)


def remap_body(slot_ref, in_ref, w_ref, u_ref, wet_ref, f_ref, up_ref, down_ref, u_out_ref, p_ref):
    slots = in_ref.shape[0]
    picked = one_hot(iota((64, slots), 1) == slot_ref[...])
    for i in range(7):
        p_ref[i * 64 : (i + 1) * 64, :] = times(picked, in_ref[:, i * LANES : (i + 1) * LANES])
    p_ref[7 * 64 :, :] = jnp.zeros((64, LANES), f32)
    left = iota((8, LANES), 1) < 64
    left_two = iota((16, LANES), 1) < 64
    for r in range(ROWS):
        sources = []
        for side in range(2):
            even, odd = [], []
            for pair in range(2):
                j = 4 * (2 * r + side) + 2 * pair
                one = p_ref[pl.ds(j, 8, stride=64), :]
                two = p_ref[pl.ds(j + 1, 8, stride=64), :]
                even.append(jnp.where(left, one, pltpu.roll(two, 64, 1)))
                odd.append(jnp.where(left, pltpu.roll(one, 64, 1), two))
            sources.append(jnp.concatenate(even, axis=1))
            sources.append(jnp.concatenate(odd, axis=1))
        sources = jnp.concatenate(sources, axis=0).astype(bf16)
        product = times_rows(sources, w_ref[r * LANES : (r + 1) * LANES, :])
        forcing = jnp.where(left_two, product[:16], product[16:])
        f_ref[16 * r : 16 * r + 16, :] = forcing
        if r < HALO - 1:
            down_ref[r] = forcing.astype(bf16)
        if r >= ROWS - HALO + 1:
            up_ref[r - (ROWS - HALO + 1)] = forcing.astype(bf16)
    whole = np.linalg.matrix_power(turn, STEPS)
    wet = wet_ref[...].astype(f32)
    push = [surface_push * f_ref[pl.ds(6 + 8 * v, ROWS, stride=16), :] for v in range(2)]
    for v in range(2):
        ahead = float(whole[v, 0]) * u_ref[0] + float(whole[v, 1]) * u_ref[1] + push[v]
        u_out_ref[v] = u_ref[v] + wet * (ahead - u_ref[v])


def returned_slots(fields, w_ref, slot_row, slots):
    blocks = 2 * ROWS
    block, lane = iota((blocks, LANES), 0), iota((blocks, LANES), 1)
    left = lane < 64
    spread = []
    for field in fields:
        parts = []
        for r in range(ROWS):
            mine = block == 2 * r + (lane >= 64).astype(jnp.int32)
            parts.append(jnp.where(mine, field[r : r + 1], 0.0))
        spread.append(jnp.concatenate(parts, axis=1))
    terms = times(jnp.concatenate(spread, axis=0).astype(bf16), w_ref[...])
    pieces = []
    for k in range(4):
        tiles = []
        for f in range(4):
            if f == 3:
                tiles.append(jnp.zeros((blocks, LANES), f32))
                continue
            tile = terms[f * blocks : (f + 1) * blocks, (k // 2) * LANES : (k // 2 + 1) * LANES]
            tiles.append(tile if k % 2 == f % 2 else pltpu.roll(tile, 64, 1))
        pieces.append(
            jnp.concatenate(
                [jnp.where(left, tiles[0], tiles[1]), jnp.where(left, tiles[2], tiles[3])], axis=1
            )
        )
    partial = jnp.concatenate(pieces, axis=0).astype(bf16)
    placed = one_hot(iota((slots, 64), 0) == slot_row)
    return times(placed, partial).astype(bf16)


def tracer_body(t, with_send, *refs):
    x1_ref, coef_ref, wet_ref, mix_ref, column_ref, f_ref, before_ref, after_ref, west_ref, east_ref = refs[:10]
    if with_send:
        w_ref, slot_ref, u_ref, out_hbm, send_ref = refs[10:15]
        one_ref, two_ref, force_ref, cat_ref, out_ref, sem, sst_ref = refs[15:]
    else:
        _, out_hbm, one_ref, two_ref, force_ref, cat_ref, out_ref, sem = refs[10:]
    levels = mix_ref.shape[0]
    column = jnp.broadcast_to(column_ref[:, 0:1], (levels, LANES))
    for idx in range(1, STRIPS):
        if idx == EXT - 1:
            continue
        if idx == WEST:
            forcing = west_ref[...].astype(f32)[8 * t : 8 * t + 8]
        elif idx == EAST:
            forcing = east_ref[...].astype(f32)[8 * t : 8 * t + 8]
        elif idx < HALO:
            forcing = before_ref[idx - 1].astype(f32)[8 * t : 8 * t + 8]
        elif idx < HALO + ROWS:
            row = 16 * (idx - HALO) + 8 * t
            forcing = f_ref[row : row + 8, :]
        else:
            forcing = after_ref[idx - HALO - ROWS].astype(f32)[8 * t : 8 * t + 8]
        forcing = surface_gain[t] * wet_ref[idx] * forcing
        force_ref[idx] = forcing
        one_ref[idx] = x1_ref[t, idx] + column * forcing[0:1]
    old, new = one_ref, two_ref
    for n in range(1, STEPS):

        def store(idx, value, new=new, n=n):
            if n < STEPS - 1:
                new[idx] = value
            else:
                out_ref[pl.ds(idx - HALO, levels, stride=ROWS), :] = value
                if with_send:
                    sst_ref[idx - HALO : idx - HALO + 1, :] = value[0:1]

        def force(idx, n=n):
            return force_ref[idx, n : n + 1, :]

        ocean_step(n, old, coef_ref, mix_ref, cat_ref, store, force)
        old, new = new, old
    copy = pltpu.make_async_copy(out_ref, out_hbm.at[t], sem)
    copy.start()
    if with_send:
        fields = [sst_ref[...], u_ref[0], u_ref[1]]
        fields = [field.astype(bf16).astype(f32) for field in fields]
        send_ref[...] = returned_slots(fields, w_ref, slot_ref[...], send_ref.shape[0])
    copy.wait()


def neighbours(size):
    up = [(i, i + 1) for i in range(size - 1)]
    return up, [(j, i) for i, j in up]


def on_device(
    atmosphere_level_state,
    atmosphere_mixing_map,
    sea_surface_temps,
    tracers,
    currents,
    ocean_advect_velocity,
    ocean_mixing_map,
    ocean_cell_mask,
    remap_weight_tiles,
    outgoing_block_table,
    arrival_slot_table,
):
    row_count, col_count = lax.axis_size("row"), lax.axis_size("col")
    slots = row_count * col_count * 2
    levels = tracers.shape[1]
    air_levels, air_columns = atmosphere_level_state.shape[1:]
    rows_axis = ("comp", "row")
    up, down = neighbours(lax.axis_size(rows_axis))
    right, leftward = neighbours(col_count)
    dma = pltpu.SemaphoreType.DMA

    arrival = arrival_slot_table.reshape(64)
    source = arrival // 2
    slot = (source % col_count) * (2 * row_count) + (source // col_count) * 2 + arrival % 2
    slot_column = slot.reshape(64, 1)
    slot_by_k = slot.reshape(2 * ROWS, 4).T.reshape(1, 64)

    table = outgoing_block_table.reshape(row_count, col_count * 2).astype(f32)
    table = jnp.pad(table, ((0, 0), (0, LANES - col_count * 2)), constant_values=-1.0)
    payload, gained, top, edge = call(
        flux_body,
        (
            shape((row_count * 8, 8 * LANES), bf16),
            shape((4, 8, air_columns)),
            shape((air_levels, air_levels)),
            shape((air_levels, 8)),
        ),
        "fluxes",
        [HBM, VMEM, VMEM, VMEM],
        scratch=[pltpu.VMEM(atmosphere_level_state.shape, f32), dma],
    )(atmosphere_level_state, atmosphere_mixing_map, sea_surface_temps[None], table)
    row_blocks = lax.all_to_all(payload, "row", 0, 0, tiled=True)
    chosen = call(select_body, shape((slots, 7 * LANES), bf16), "select", [VMEM])(row_blocks)
    arrived = lax.all_to_all(chosen, "col", 0, 0, tiled=True)

    atm_final = call(
        atmosphere_body,
        shape(atmosphere_level_state.shape),
        "atmosphere",
        [HBM, VMEM, VMEM, VMEM],
        HBM,
        scratch=[pltpu.VMEM(atmosphere_level_state.shape, f32), dma((4,)), dma((4,))],
    )(atmosphere_level_state, gained, top, edge)

    flat = tracers.reshape(2, levels * ROWS, LANES)
    depth = 4 * levels + 16
    z = call(
        rows_body,
        shape((ROWS, depth, LANES), bf16),
        "rows",
        [HBM, VMEM, VMEM],
        scratch=[pltpu.VMEM(flat.shape, f32), pltpu.VMEM(flat.shape, f32), dma],
    )(flat, ocean_advect_velocity.reshape(flat.shape), ocean_cell_mask)
    before = lax.ppermute(z[ROWS - HALO :], rows_axis, up)
    after = lax.ppermute(z[:HALO], rows_axis, down)
    edge_shape = shape((depth, LANES), bf16)
    first, last = call(pack_body, (edge_shape, edge_shape), "pack", [VMEM] * 3)(before, z, after)
    east_in = lax.ppermute(first, "col", leftward)
    west_in = lax.ppermute(last, "col", right)
    cells = call(
        cells_body,
        shape((ROWS * LANES, WIDE), bf16),
        "cells",
        [HBM],
        scratch=[
            pltpu.VMEM((64, 4096), bf16),
            pltpu.VMEM((32 * 64, LANES), f32),
            pltpu.VMEM((ROWS * LANES, LANES), f32),
            pltpu.VMEM((ROWS * LANES, LANES), f32),
            dma,
        ],
    )(remap_weight_tiles.reshape(64, 4096))
    rounded = lax.reduce_precision(ocean_mixing_map, 8, 7)
    upper, lower = rounded.astype(bf16), (ocean_mixing_map - rounded).astype(bf16)
    mix = jnp.concatenate([upper, lower, upper], axis=1)
    wide = (STRIPS, levels, LANES)
    cat = pltpu.VMEM((3 * levels, EXT * LANES), bf16)
    coef, x1, wet = call(
        coefficient_body,
        (shape((5, *wide)), shape((2, *wide)), shape((STRIPS, 8, LANES))),
        "coefficients",
        [VMEM] * 5 + [HBM, VMEM],
        scratch=[
            pltpu.VMEM(flat.shape, f32),
            pltpu.VMEM((2, *wide), f32),
            pltpu.VMEM((4, STRIPS, 8, LANES), f32),
            cat,
            dma,
        ],
    )(before, z, after, west_in, east_in, flat, mix)

    edge_rows = shape((HALO - 1, 16, LANES), bf16)
    forcing, send_up, send_down, ocean_currents = call(
        remap_body,
        (shape((ROWS * 16, LANES)), edge_rows, edge_rows, shape(currents.shape)),
        "remap",
        [VMEM] * 5,
        scratch=[pltpu.VMEM((8 * 64, LANES), f32)],
    )(slot_column, arrived, cells, currents, ocean_cell_mask)
    f_before = lax.ppermute(send_up, rows_axis, up)
    f_after = lax.ppermute(send_down, rows_axis, down)
    strip = shape((16, LANES), bf16)
    f_first, f_last = call(pack_forcing_body, (strip, strip), "pack_forcing", [VMEM] * 3)(
        forcing, f_before, f_after
    )
    f_east = lax.ppermute(f_first, "col", leftward)
    f_west = lax.ppermute(f_last, "col", right)

    shared = (
        x1, coef, wet, mix, ocean_mixing_map, forcing, f_before, f_after, f_west, f_east,
    )
    scratch = [
        pltpu.VMEM(wide, f32),
        pltpu.VMEM(wide, f32),
        pltpu.VMEM((STRIPS, 8, LANES), f32),
        cat,
        pltpu.VMEM((levels * ROWS, LANES), f32),
        dma,
    ]
    warm, terms = call(
        functools.partial(tracer_body, 0, True),
        (shape(flat.shape), shape((slots, WIDE), bf16)),
        "temperature",
        [VMEM] * 13,
        (HBM, VMEM),
        scratch=scratch + [pltpu.VMEM((ROWS, LANES), f32)],
    )(*shared, cells, slot_by_k, ocean_currents)
    back = lax.all_to_all(terms, "col", 0, 0, tiled=True)
    sums = call(gather_body, shape((row_count * 8, WIDE)), "gather", [VMEM, VMEM])(row_blocks, back)
    home = lax.all_to_all(sums, "row", 0, 0, tiled=True)
    returned = call(finish_body, shape((3, air_columns)), "finish", [VMEM])(home)
    both = call(
        functools.partial(tracer_body, 1, False),
        shape(flat.shape),
        "salinity",
        [VMEM] * 10 + [HBM],
        HBM,
        scratch=scratch,
        aliases={10: 0},
    )(*shared, warm)
    return (atm_final, both.reshape(tracers.shape), ocean_currents, returned)


def solution(mesh):
    return jax.shard_map(
        on_device,
        mesh=mesh,
        in_specs=(
            P(None, None, ("comp", "row", "col")),
            P(),
            P(("comp", "row", "col")),
            P(None, None, ("comp", "row"), "col"),
            P(None, ("comp", "row"), "col"),
            P(None, None, ("comp", "row"), "col"),
            P(),
            P(("comp", "row"), "col"),
            P("comp", ("row", "col"), None, None),
            P("comp", ("row", "col"), None, None),
            P("comp", ("row", "col"), None),
        ),
        out_specs=(
            P(None, None, ("comp", "row", "col")),
            P(None, None, ("comp", "row"), "col"),
            P(None, ("comp", "row"), "col"),
            P(None, ("comp", "row", "col")),
        ),
        check_vma=False,
    )
```

```python
import functools

import jax
import jax.numpy as jnp
import numpy as np
from jax import lax
from jax.experimental import pallas as pl
from jax.experimental.pallas import tpu as pltpu
from jax.sharding import PartitionSpec as P

STEPS = 6
HALO = 6
ROWS = 8
EXT = ROWS + 2 * HALO
REACH = 2 * HALO
GROUP = 3
EDGES = -(-EXT // GROUP)
TILES = EXT + EDGES
SIDE = 2 * (HALO + REACH)
LANES = 128
WIDE = 256
HIGHEST = lax.Precision.HIGHEST
MIB = 1024 * 1024

heat_rate = 0.5
vapour_rate = 0.5
drag_rate = 0.3
saturation = 0.6
flux_gains = (0.3, 0.3, -0.3, -0.3)
diffusion = 0.15
surface_gain = (-0.3, 0.3)
surface_push = 0.3
current_drag = 0.1
coriolis = 0.2
turn = np.array([[1.0 - current_drag, coriolis], [-coriolis, 1.0 - current_drag]])

f32 = jnp.float32
bf16 = jnp.bfloat16
VMEM = pl.BlockSpec(memory_space=pltpu.VMEM)
HBM = pl.BlockSpec(memory_space=pltpu.HBM)
SMEM = pl.BlockSpec(memory_space=pltpu.SMEM)


def call(body, out_shape, name, in_specs, out_specs=None, scratch=(), aliases=None, limit=8, micros=1):
    if out_specs is None:
        out_specs = jax.tree.map(lambda _: VMEM, out_shape)
    return pl.pallas_call(
        body,
        out_shape=out_shape,
        in_specs=in_specs,
        out_specs=out_specs,
        scratch_shapes=list(scratch),
        input_output_aliases=aliases or {},
        compiler_params=pltpu.CompilerParams(vmem_limit_bytes=limit * MIB),
        cost_estimate=pl.CostEstimate(
            flops=int(micros * 1e9), bytes_accessed=int(micros * 3e6), transcendentals=0
        ),
        name=name,
    )


def shape(dims, dtype=f32):
    return jax.ShapeDtypeStruct(dims, dtype)


def exact(a, b):
    return jnp.dot(a, b, precision=HIGHEST, preferred_element_type=f32)


def times(a, b):
    return jnp.dot(a, b, preferred_element_type=f32)


def times_rows(a, b):
    return lax.dot_general(a, b, (((1,), (1,)), ((), ())), preferred_element_type=f32)


def iota(dims, axis):
    return lax.broadcasted_iota(jnp.int32, dims, axis)


def one_hot(condition):
    return condition.astype(f32).astype(bf16)


def halves(x):
    high = x.astype(bf16)
    return high, (x - high.astype(f32)).astype(bf16)


def moves():
    pack = np.zeros((EXT, LANES, 2, LANES), np.float32)
    spread = np.zeros((2, LANES, EDGES, LANES), np.float32)
    own = np.zeros((GROUP, LANES, LANES), np.float32)
    for r in range(EXT):
        at = SIDE * (r // EDGES)
        for c in range(HALO):
            pack[r, c, 0, HALO * r + c] = 1
            pack[r, LANES - HALO + c, 1, HALO * r + c] = 1
            spread[0, HALO * r + c, r % EDGES, at + SIDE - HALO + c] = 1
            spread[1, HALO * r + c, r % EDGES, at + c] = 1
    for k in range(GROUP):
        for c in range(REACH):
            own[k, c, SIDE * k + HALO + c] = 1
            own[k, LANES - REACH + c, SIDE * k + HALO + REACH + c] = 1
    return (
        jnp.asarray(pack.reshape(EXT * LANES, 2 * LANES), bf16),
        jnp.asarray(spread.reshape(2 * LANES, EDGES * LANES), bf16),
        jnp.asarray(own.reshape(GROUP * LANES, LANES), bf16),
    )


def flux_body(table_ref, a_ref, m_ref, sst_ref, pay_ref, g_ref, top_ref, edge_ref, block_ref):
    levels = m_ref.shape[0]
    bottom = levels - 1
    power = {1: m_ref[...]}
    power[2] = exact(power[1], power[1])
    power[3] = exact(power[1], power[2])
    power[4] = exact(power[2], power[2])
    power[5] = exact(power[2], power[3])
    power[6] = exact(power[3], power[3])
    first = (iota((1, levels), 1) == bottom).astype(f32)
    rows = [first] + [power[n][bottom:, :] for n in range(1, STEPS)]
    rows = jnp.concatenate(rows + [jnp.zeros((8 - STEPS, levels), f32)], axis=0)
    row_high, row_low = halves(rows)
    both = jnp.concatenate([row_high.astype(f32), row_low.astype(f32)], axis=0).astype(bf16)
    top_ref[...] = power[6]
    lane = iota((levels, 8), 1)
    edge = jnp.zeros((levels, 8), f32)
    for n in range(STEPS):
        edge = jnp.where(lane == n, power[STEPS - n][:, bottom:], edge)
    edge_ref[...] = edge
    base = []
    for v in range(4):
        high, low = halves(a_ref[v])
        one = times(both, high)
        base.append(one[:8] + one[8:] + times(row_high, low))
    corner = {n: power[n][bottom:, bottom:] for n in range(1, STEPS)}
    sst = sst_ref[...]
    gained = []
    fluxes = []
    east, north = jnp.zeros_like(sst), jnp.zeros_like(sst)
    for n in range(STEPS):
        now = []
        for v in range(4):
            value = base[v][n : n + 1]
            for k in range(n):
                value = value + corner[n - k] * gained[k][v]
            now.append(value)
        wind = jnp.sqrt(now[2] * now[2] + now[3] * now[3] + 1.0)
        flux = (
            heat_rate * wind * (sst - now[0]),
            vapour_rate * wind * (saturation * sst - now[1]),
            drag_rate * wind * now[2],
            drag_rate * wind * now[3],
        )
        fluxes.append(flux)
        gained.append([flux_gains[v] * flux[v] for v in range(4)])
        east, north = (
            turn[0, 0] * east + turn[0, 1] * north + flux[2],
            turn[1, 0] * east + turn[1, 1] * north + flux[3],
        )
    blank = [jnp.zeros_like(sst)] * (8 - STEPS)
    for v in range(4):
        g_ref[v] = jnp.concatenate([gained[n][v] for n in range(STEPS)] + blank, axis=0)
    pairs = [(fluxes[n][0], fluxes[n][1]) for n in range(STEPS)] + [(east, north)]
    block = iota((8, LANES), 0)
    left = iota((8, LANES), 1) < 64
    even = block % 2 == 0
    for i, pair in enumerate(pairs):
        parts = []
        for side in range(2):
            spread = jnp.zeros((8, LANES), f32)
            for q in range(4):
                tile = jnp.broadcast_to(pair[side][:, q * LANES : (q + 1) * LANES], (8, LANES))
                spread = jnp.where(block // 2 == q, tile, spread)
            parts.append(jnp.where(even == (side == 0), spread, pltpu.roll(spread, 64, 1)))
        block_ref[pl.ds(i, 8, stride=8), :] = jnp.where(left, parts[0], parts[1])
    block_ref[pl.ds(7, 8, stride=8), :] = jnp.zeros((8, LANES), f32)
    for d in range(pay_ref.shape[0] // 16):
        chosen = []
        for side in range(2):
            at = jnp.maximum(table_ref[side, d], 0) * 8
            chosen.append(block_ref[pl.ds(pl.multiple_of(at, 8), 8), :])
        pay_ref[16 * d : 16 * d + 16, :] = jnp.concatenate(chosen, axis=0).astype(bf16)


def atmosphere_body(a_ref, g_ref, top_ref, edge_ref, out_ref):
    for v in range(4):
        out_ref[v] = exact(top_ref[...], a_ref[v]) + exact(edge_ref[...], g_ref[v])


def finish_body(table_ref, in_ref, out_ref):
    rows = in_ref.shape[0]
    block, lane = iota((8, rows), 0), iota((8, rows), 1)
    ones = []
    for side in range(2):
        named = table_ref[side : side + 1, :] == block
        for f in range(3):
            ones.append((named & (lane % 4 == f)).astype(f32))
    ones = jnp.concatenate(ones, axis=0).astype(bf16)
    high, low = halves(in_ref[...])
    sums = times(ones, high) + times(ones, low)
    left = iota((1, LANES), 1) < 64
    for f in range(3):
        low = sums[8 * f : 8 * f + 8] + pltpu.roll(sums[24 + 8 * f : 32 + 8 * f], 64, 1)
        high = pltpu.roll(low, 64, 1)
        for q in range(4):
            out_ref[f : f + 1, q * LANES : (q + 1) * LANES] = jnp.where(
                left, low[2 * q : 2 * q + 1], high[2 * q + 1 : 2 * q + 2]
            )


def cells_body(w_ref, out_ref, t_ref, low_ref, high_ref):
    left = iota((16, LANES), 1) < 64
    tiles = w_ref.shape[1] // LANES
    for i in range(tiles):
        t_ref[i * 64 : (i + 1) * 64] = w_ref[:, i * LANES : (i + 1) * LANES].astype(f32)
    for i in range(tiles):
        k = [t_ref[pl.ds(i * 64 + s, 16, stride=4), :] for s in range(4)]
        moved = [pltpu.roll(x, 64, 1) for x in k]
        low_ref[pl.ds(2 * i, 16, stride=64), :] = jnp.where(left, k[0], moved[1])
        high_ref[pl.ds(2 * i, 16, stride=64), :] = jnp.where(left, k[2], moved[3])
        low_ref[pl.ds(2 * i + 1, 16, stride=64), :] = jnp.where(left, moved[0], k[1])
        high_ref[pl.ds(2 * i + 1, 16, stride=64), :] = jnp.where(left, moved[2], k[3])
    out_ref[:, :LANES] = low_ref[...].astype(bf16)
    out_ref[:, LANES:] = high_ref[...].astype(bf16)


def rows_body(x_ref, v_ref, wet_ref, z_ref, f_ref):
    levels = x_ref.shape[1] // ROWS
    for t in range(2):
        f_ref[t] = v_ref[t].astype(f32)
    for r in range(ROWS):
        for t in range(2):
            z_ref[r, (2 + t) * levels : (3 + t) * levels, :] = f_ref[
                t, pl.ds(r, levels, stride=ROWS), :
            ].astype(bf16)
        wet = jnp.broadcast_to(wet_ref[r : r + 1, :].astype(f32), (16, LANES))
        z_ref[r, 4 * levels :, :] = wet.astype(bf16)
    for r in range(ROWS):
        for t in range(2):
            z_ref[r, t * levels : (t + 1) * levels, :] = x_ref[
                t, pl.ds(r, levels, stride=ROWS), :
            ].astype(bf16)


def widened(before_ref, own_ref, after_ref):
    rows = [before_ref[r] for r in range(HALO)]
    rows += [own_ref[r] for r in range(ROWS)]
    return rows + [after_ref[r] for r in range(HALO)]


def pack_body(before_ref, z_ref, after_ref, pack_ref, first_ref, last_ref):
    rows = widened(before_ref, z_ref, after_ref)
    packed = times(jnp.concatenate(rows, axis=1), pack_ref[...]).astype(bf16)
    first_ref[...] = packed[:, :LANES]
    last_ref[...] = packed[:, LANES:]


def forcing_rows(f_ref, before_ref, after_ref):
    blank = [jnp.zeros((16, LANES), bf16)]
    rows = blank + [before_ref[r] for r in range(HALO - 1)]
    rows += [f_ref[16 * r : 16 * r + 16].astype(bf16) for r in range(ROWS)]
    return rows + [after_ref[r] for r in range(HALO - 1)] + blank


def pack_forcing_body(f_ref, before_ref, after_ref, pack_ref, first_ref, last_ref):
    rows = forcing_rows(f_ref, before_ref, after_ref)
    packed = times(jnp.concatenate(rows, axis=1), pack_ref[...]).astype(bf16)
    first_ref[...] = packed[:, :LANES]
    last_ref[...] = packed[:, LANES:]


def edge_tile(g, rows, sides, spread_ref, own_ref):
    mine = [rows[r] for r in range(g, EXT, EDGES)]
    return times(jnp.concatenate(mine, axis=1), own_ref[: len(mine) * LANES, :]) + times(
        sides, spread_ref[:, g * LANES : (g + 1) * LANES]
    )


def around(idx, get):
    here = get(idx)
    if idx < EXT:
        north, south = get(idx + 1), get(idx - 1)
    else:
        north = get(idx + 1) if idx + 1 < TILES else pltpu.roll(get(EXT), LANES - SIDE, 1)
        south = get(idx - 1) if idx > EXT else pltpu.roll(get(TILES - 1), SIDE, 1)
    return here, pltpu.roll(here, LANES - 1, 1), pltpu.roll(here, 1, 1), north, south


def ocean_step(n, x_ref, coef_ref, mix_ref, cat_ref, store, force=None):
    levels = mix_ref.shape[0]
    tiles = list(range(n + 1, EXT - 1 - n)) + list(range(EXT, TILES))
    first = iota((8, LANES), 0) == 0
    for lo in range(0, len(tiles), 4):
        some = tiles[lo : lo + 4]
        slot = (lo // 4) % 2
        for at in range(0, levels, 16):
            for i, idx in enumerate(some):
                here, east, west, north, south = around(idx, lambda j: x_ref[j, at : at + 16, :])
                stepped = (
                    coef_ref[0, idx, at : at + 16, :] * here
                    + (coef_ref[1, idx, at : at + 16, :] * east
                       + coef_ref[2, idx, at : at + 16, :] * west)
                    + (coef_ref[3, idx, at : at + 16, :] * north
                       + coef_ref[4, idx, at : at + 16, :] * south)
                )
                if force is not None and at == 0:
                    top = stepped[:8] + jnp.where(first, force(idx), 0.0)
                    stepped = jnp.concatenate([top, stepped[8:]], axis=0)
                upper, lower = halves(stepped)
                cols = slice(i * LANES, (i + 1) * LANES)
                cat_ref[slot, at : at + 16, cols] = upper
                cat_ref[slot, levels + at : levels + at + 16, cols] = upper
                cat_ref[slot, 2 * levels + at : 2 * levels + at + 16, cols] = lower
        mixed = times(mix_ref[...], cat_ref[slot, :, : len(some) * LANES])
        for i, idx in enumerate(some):
            store(idx, mixed[:, i * LANES : (i + 1) * LANES])


def coefficient_body(
    before_ref, z_ref, after_ref, west_ref, east_ref, x_ref, mix_ref, spread_ref, own_ref,
    coef_ref, x1_ref, salt_ref, wet_ref, x0_ref, near_ref, edge_ref, cat_ref,
):
    levels = mix_ref.shape[0]
    rows = widened(before_ref, z_ref, after_ref)
    sides = jnp.concatenate([east_ref[...], west_ref[...]], axis=1)
    for g in range(EDGES):
        edge_ref[g] = edge_tile(g, rows, sides, spread_ref, own_ref).astype(bf16)

    def of(idx, at):
        if idx >= EXT:
            return edge_ref[idx - EXT, at, :].astype(f32)
        if idx < HALO:
            return before_ref[idx, at, :].astype(f32)
        if idx < HALO + ROWS:
            return z_ref[idx - HALO, at, :].astype(f32)
        return after_ref[idx - HALO - ROWS, at, :].astype(f32)

    wets = [of(idx, pl.ds(4 * levels, 16))[:8] for idx in range(TILES)]
    for idx in range(TILES):
        wet_ref[idx] = wets[idx]
    inner = list(range(1, EXT - 1)) + list(range(EXT, TILES))
    for idx in inner:
        here, *near = around(idx, lambda j: wets[j])
        for s in range(4):
            near_ref[s, idx] = here * near[s]

    def part(c, carry):
        at = pl.multiple_of(c * 16, 16)
        here_at = pl.ds(at, 16)
        for idx in inner:
            along = 0.5 * of(idx, pl.ds(2 * levels + at, 16))
            across = 0.5 * of(idx, pl.ds(3 * levels + at, 16))
            near = []
            for s in range(4):
                one = near_ref[s, idx]
                near.append(jnp.concatenate([one, one], axis=0))
            c_east = near[0] * (diffusion - along)
            c_west = near[1] * (diffusion + along)
            c_north = near[2] * (diffusion - across)
            c_south = near[3] * (diffusion + across)
            coef_ref[0, idx, here_at, :] = 1.0 - ((c_east + c_west) + (c_north + c_south))
            coef_ref[1, idx, here_at, :] = c_east
            coef_ref[2, idx, here_at, :] = c_west
            coef_ref[3, idx, here_at, :] = c_north
            coef_ref[4, idx, here_at, :] = c_south
        for t, to_ref in enumerate((x0_ref, salt_ref)):
            for idx in range(TILES):
                if not HALO <= idx < HALO + ROWS:
                    to_ref[idx, here_at, :] = of(idx, pl.ds(t * levels + at, 16))
        return carry

    lax.fori_loop(0, levels // 16, part, 0)
    for t, to_ref in enumerate((x0_ref, salt_ref)):
        for r in range(ROWS):
            to_ref[HALO + r] = x_ref[t, pl.ds(r, levels, stride=ROWS), :]

    def store(idx, value):
        x1_ref[idx] = value

    ocean_step(0, x0_ref, coef_ref, mix_ref, cat_ref, store)


def remap_body(arrival_ref, in_ref, w_ref, u_ref, wet_ref, f_ref, up_ref, down_ref, u_out_ref):
    def pick(j):
        t = arrival_ref[0, j]
        at = pl.multiple_of((t >> 1) * 16, 16)
        window = in_ref[pl.ds(at, 16), :].astype(f32)
        return jnp.where((t & 1) == 1, window[8:], window[:8])

    left = iota((8, LANES), 1) < 64
    left_two = iota((16, LANES), 1) < 64
    for r in range(ROWS):
        sources = []
        for side in range(2):
            even, odd = [], []
            for pair in range(2):
                j = 4 * (2 * r + side) + 2 * pair
                one, two = pick(j), pick(j + 1)
                even.append(jnp.where(left, one, pltpu.roll(two, 64, 1)))
                odd.append(jnp.where(left, pltpu.roll(one, 64, 1), two))
            sources.append(jnp.concatenate(even, axis=1))
            sources.append(jnp.concatenate(odd, axis=1))
        sources = jnp.concatenate(sources, axis=0).astype(bf16)
        product = times_rows(sources, w_ref[r * LANES : (r + 1) * LANES, :])
        forcing = jnp.where(left_two, product[:16], product[16:])
        f_ref[16 * r : 16 * r + 16, :] = forcing
        if r < HALO - 1:
            down_ref[r] = forcing.astype(bf16)
        if r >= ROWS - HALO + 1:
            up_ref[r - (ROWS - HALO + 1)] = forcing.astype(bf16)
    whole = np.linalg.matrix_power(turn, STEPS)
    wet = wet_ref[...].astype(f32)
    push = [surface_push * f_ref[pl.ds(6 + 8 * v, ROWS, stride=16), :] for v in range(2)]
    for v in range(2):
        ahead = float(whole[v, 0]) * u_ref[0] + float(whole[v, 1]) * u_ref[1] + push[v]
        u_out_ref[v] = u_ref[v] + wet * (ahead - u_ref[v])


def returned_rows(fields, w_ref, place, rows):
    blocks = 2 * ROWS
    block, lane = iota((blocks, LANES), 0), iota((blocks, LANES), 1)
    spread = []
    for field in fields:
        parts = []
        for r in range(ROWS):
            mine = block == 2 * r + (lane >= 64).astype(jnp.int32)
            parts.append(jnp.where(mine, field[r : r + 1], 0.0))
        spread.append(jnp.concatenate(parts, axis=1))
    terms = times(jnp.concatenate(spread, axis=0).astype(bf16), w_ref[...])
    high_parts, low_parts, ones = [], [], []
    target = iota((rows, LANES), 0)
    for f in range(len(fields)):
        mine = terms[f * blocks : (f + 1) * blocks]
        pieces = []
        for half in range(2):
            for k in range(4):
                piece = mine[:, (k // 2) * LANES : (k // 2 + 1) * LANES]
                if k % 2 != half:
                    piece = pltpu.roll(piece, 64, 1)
                pieces.append(jnp.where((lane >= 64) == (half == 1), piece, 0.0))
        high, low = halves(jnp.concatenate(pieces, axis=0))
        high_parts.append(high)
        low_parts.append(low)
        ones.append(one_hot(target == place + f))
    return times(
        jnp.concatenate(ones + ones, axis=1), jnp.concatenate(high_parts + low_parts, axis=0)
    )


def tracer_body(t, *refs):
    x_ref, coef_ref, wet_ref, mix_ref, f_ref, before_ref, after_ref, west_ref, east_ref = refs[:9]
    spread_ref, own_ref = refs[9:11]
    if t == 0:
        column_ref, w_ref, place_ref, u_ref, out_ref, send_ref = refs[11:17]
        one_ref, two_ref, force_ref, cat_ref, sst_ref = refs[17:]
    else:
        out_ref, one_ref, two_ref, force_ref, cat_ref = refs[11:]
    levels = mix_ref.shape[0]
    rows = forcing_rows(f_ref, before_ref, after_ref)
    sides = jnp.concatenate([east_ref[...], west_ref[...]], axis=1)
    for idx in range(1, TILES):
        if idx == EXT - 1:
            continue
        if HALO <= idx < HALO + ROWS:
            row = 16 * (idx - HALO)
            forcing = f_ref[row : row + 16, :]
        elif idx < EXT:
            forcing = rows[idx].astype(f32)
        else:
            forcing = edge_tile(idx - EXT, rows, sides, spread_ref, own_ref)
        force_ref[idx] = surface_gain[t] * wet_ref[idx] * forcing[8 * t : 8 * t + 8]
    if t == 0:
        column = jnp.broadcast_to(column_ref[:, 0:1], (levels, LANES))
        for idx in range(1, TILES):
            if idx != EXT - 1:
                one_ref[idx] = x_ref[idx] + column * force_ref[idx, 0:1, :]
        old, new = one_ref, two_ref
    else:
        old, new = x_ref, one_ref
    for n in range(1 if t == 0 else 0, STEPS):

        def store(idx, value, new=new):
            new[idx] = value

        def force(idx, n=n):
            return force_ref[idx, n : n + 1, :]

        ocean_step(n, old, coef_ref, mix_ref, cat_ref, store, force)
        if t == 1 and n == 0:
            old, new = one_ref, two_ref
        else:
            old, new = new, old
    lane = iota((16, LANES), 1)
    for r in range(ROWS):
        idx = HALO + r
        at = SIDE * (idx // EDGES) + HALO
        edge = EXT + idx % EDGES
        for lo in range(0, levels, 16):
            side = old[edge, lo : lo + 16, :]
            value = jnp.where(
                lane < HALO, pltpu.roll(side, (LANES - at) % LANES, 1), old[idx, lo : lo + 16, :]
            )
            here = at + REACH + HALO
            value = jnp.where(
                lane >= LANES - HALO, pltpu.roll(side, (LANES - HALO - here) % LANES, 1), value
            )
            out_ref[pl.ds(lo * ROWS + r, 16, stride=ROWS), :] = value
            if t == 0 and lo == 0:
                sst_ref[r : r + 1, :] = value[0:1]
    if t == 0:
        fields = [sst_ref[...], u_ref[0], u_ref[1]]
        fields = [field.astype(bf16).astype(f32) for field in fields]
        send_ref[...] = returned_rows(fields, w_ref, place_ref[...], send_ref.shape[0])


def neighbours(size):
    up = [(i, i + 1) for i in range(size - 1)]
    return up, [(j, i) for i, j in up]


def on_device(
    atmosphere_level_state,
    atmosphere_mixing_map,
    sea_surface_temps,
    tracers,
    currents,
    ocean_advect_velocity,
    ocean_mixing_map,
    ocean_cell_mask,
    remap_weight_tiles,
    outgoing_block_table,
    arrival_slot_table,
):
    band = ("row", "col")
    peers = lax.axis_size(band)
    levels = tracers.shape[1]
    air_levels, air_columns = atmosphere_level_state.shape[1:]
    rows_axis = ("comp", "row")
    up, down = neighbours(lax.axis_size(rows_axis))
    right, leftward = neighbours(lax.axis_size("col"))
    pack_moves, spread_moves, own_moves = moves()

    table = outgoing_block_table.reshape(peers, 2).T
    arrival = arrival_slot_table.reshape(1, 64)
    by_k = arrival.reshape(2 * ROWS, 4).T.reshape(1, 64)
    place = jnp.concatenate(
        [jnp.where(by_k % 2 == side, (by_k // 2) * 4, -64) for side in range(2)], axis=1
    )

    payload, gained, top, edge = call(
        flux_body,
        (
            shape((peers * 16, LANES), bf16),
            shape((4, 8, air_columns)),
            shape((air_levels, air_levels)),
            shape((air_levels, 8)),
        ),
        "fluxes",
        [SMEM, VMEM, VMEM, VMEM],
        scratch=[pltpu.VMEM((64, LANES), f32)],
        micros=2,
    )(table, atmosphere_level_state, atmosphere_mixing_map, sea_surface_temps[None])
    arrived = lax.all_to_all(payload, band, 0, 0, tiled=True)

    flat = tracers.reshape(2, levels * ROWS, LANES)
    depth = 4 * levels + 16
    z = call(
        rows_body,
        shape((ROWS, depth, LANES), bf16),
        "rows",
        [VMEM] * 3,
        scratch=[pltpu.VMEM(flat.shape, f32)],
    )(flat, ocean_advect_velocity.reshape(flat.shape), ocean_cell_mask)
    before = lax.ppermute(z[ROWS - HALO :], rows_axis, up)
    after = lax.ppermute(z[:HALO], rows_axis, down)
    edge_shape = shape((depth, LANES), bf16)
    first, last = call(pack_body, (edge_shape, edge_shape), "pack", [VMEM] * 4)(
        before, z, after, pack_moves
    )
    east_in = lax.ppermute(first, "col", leftward)
    west_in = lax.ppermute(last, "col", right)
    cells = call(
        cells_body,
        shape((ROWS * LANES, WIDE), bf16),
        "cells",
        [VMEM],
        scratch=[
            pltpu.VMEM((32 * 64, LANES), f32),
            pltpu.VMEM((ROWS * LANES, LANES), f32),
            pltpu.VMEM((ROWS * LANES, LANES), f32),
        ],
    )(remap_weight_tiles.reshape(64, 4096))
    rounded = lax.reduce_precision(ocean_mixing_map, 8, 7)
    upper, lower = rounded.astype(bf16), (ocean_mixing_map - rounded).astype(bf16)
    mix = jnp.concatenate([upper, lower, upper], axis=1)
    wide = (TILES, levels, LANES)
    cat = pltpu.VMEM((2, 3 * levels, 4 * LANES), bf16)
    coef, x1, salt, wet = call(
        coefficient_body,
        (shape((5, *wide)), shape(wide), shape(wide), shape((TILES, 8, LANES))),
        "coefficients",
        [VMEM] * 9,
        scratch=[
            pltpu.VMEM(wide, f32),
            pltpu.VMEM((4, TILES, 8, LANES), f32),
            pltpu.VMEM((EDGES, depth, LANES), bf16),
            cat,
        ],
        limit=24,
        micros=4,
    )(before, z, after, west_in, east_in, flat, mix, spread_moves, own_moves)
    arrived, coef = lax.optimization_barrier((arrived, coef))

    edge_rows = shape((HALO - 1, 16, LANES), bf16)
    forcing, send_up, send_down, ocean_currents = call(
        remap_body,
        (shape((ROWS * 16, LANES)), edge_rows, edge_rows, shape(currents.shape)),
        "remap",
        [SMEM] + [VMEM] * 4,
    )(arrival, arrived, cells, currents, ocean_cell_mask)
    f_before = lax.ppermute(send_up, rows_axis, up)
    f_after = lax.ppermute(send_down, rows_axis, down)
    strip = shape((16, LANES), bf16)
    f_first, f_last = call(pack_forcing_body, (strip, strip), "pack_forcing", [VMEM] * 4)(
        forcing, f_before, f_after, pack_moves
    )
    f_east = lax.ppermute(f_first, "col", leftward)
    f_west = lax.ppermute(f_last, "col", right)

    shared = (coef, wet, mix, forcing, f_before, f_after, f_west, f_east, spread_moves, own_moves)
    scratch = [
        pltpu.VMEM(wide, f32),
        pltpu.VMEM(wide, f32),
        pltpu.VMEM((TILES, 8, LANES), f32),
        cat,
    ]
    warm, terms = call(
        functools.partial(tracer_body, 0),
        (shape(flat.shape[1:]), shape((peers * 4, LANES))),
        "temperature",
        [VMEM] * 15,
        scratch=scratch + [pltpu.VMEM((ROWS, LANES), f32)],
        limit=24,
        micros=6,
    )(x1, *shared, ocean_mixing_map, cells, place, ocean_currents)
    home = lax.all_to_all(terms, band, 0, 0, tiled=True)
    gained, terms = lax.optimization_barrier((gained, terms))
    atm_final = call(
        atmosphere_body,
        shape(atmosphere_level_state.shape),
        "atmosphere",
        [VMEM] * 4,
        micros=3,
    )(atmosphere_level_state, gained, top, edge)
    cold = call(
        functools.partial(tracer_body, 1),
        shape(flat.shape[1:]),
        "salinity",
        [VMEM] * 11,
        scratch=scratch,
        limit=24,
        micros=6,
    )(salt, *shared)
    returned = call(finish_body, shape((3, air_columns)), "finish", [VMEM, VMEM])(
        jnp.repeat(table, 4, axis=1), home
    )
    ocean_tracers = jnp.stack([warm, cold]).reshape(tracers.shape)
    return (atm_final, ocean_tracers, ocean_currents, returned)


def solution(mesh):
    return jax.shard_map(
        on_device,
        mesh=mesh,
        in_specs=(
            P(None, None, ("comp", "row", "col")),
            P(),
            P(("comp", "row", "col")),
            P(None, None, ("comp", "row"), "col"),
            P(None, ("comp", "row"), "col"),
            P(None, None, ("comp", "row"), "col"),
            P(),
            P(("comp", "row"), "col"),
            P("comp", ("row", "col"), None, None),
            P("comp", ("row", "col"), None, None),
            P("comp", ("row", "col"), None),
        ),
        out_specs=(
            P(None, None, ("comp", "row", "col")),
            P(None, None, ("comp", "row"), "col"),
            P(None, ("comp", "row"), "col"),
            P(None, ("comp", "row", "col")),
        ),
        check_vma=False,
    )
```

```python
import functools

import jax
import jax.numpy as jnp
import numpy as np
from jax import lax
from jax.experimental import pallas as pl
from jax.experimental.pallas import tpu as pltpu
from jax.sharding import PartitionSpec as P

STEPS = 6
HALO = 6
ROWS = 8
EXT = ROWS + 2 * HALO
REACH = 2 * HALO
GROUP = 3
EDGES = -(-EXT // GROUP)
TILES = EXT + EDGES
SIDE = 2 * (HALO + REACH)
LANES = 128
WIDE = 256
HIGHEST = lax.Precision.HIGHEST
MIB = 1024 * 1024

heat_rate = 0.5
vapour_rate = 0.5
drag_rate = 0.3
saturation = 0.6
flux_gains = (0.3, 0.3, -0.3, -0.3)
diffusion = 0.15
surface_gain = (-0.3, 0.3)
surface_push = 0.3
current_drag = 0.1
coriolis = 0.2
turn = np.array([[1.0 - current_drag, coriolis], [-coriolis, 1.0 - current_drag]])

f32 = jnp.float32
bf16 = jnp.bfloat16
VMEM = pl.BlockSpec(memory_space=pltpu.VMEM)
HBM = pl.BlockSpec(memory_space=pltpu.HBM)
SMEM = pl.BlockSpec(memory_space=pltpu.SMEM)


def call(body, out_shape, name, in_specs, out_specs=None, scratch=(), aliases=None, limit=8, micros=1):
    if out_specs is None:
        out_specs = jax.tree.map(lambda _: VMEM, out_shape)
    return pl.pallas_call(
        body,
        out_shape=out_shape,
        in_specs=in_specs,
        out_specs=out_specs,
        scratch_shapes=list(scratch),
        input_output_aliases=aliases or {},
        compiler_params=pltpu.CompilerParams(vmem_limit_bytes=limit * MIB),
        cost_estimate=pl.CostEstimate(
            flops=int(micros * 1e9), bytes_accessed=int(micros * 3e6), transcendentals=0
        ),
        name=name,
    )


def shape(dims, dtype=f32):
    return jax.ShapeDtypeStruct(dims, dtype)


def exact(a, b):
    return jnp.dot(a, b, precision=HIGHEST, preferred_element_type=f32)


def times(a, b):
    return jnp.dot(a, b, preferred_element_type=f32)


def times_rows(a, b):
    return lax.dot_general(a, b, (((1,), (1,)), ((), ())), preferred_element_type=f32)


def iota(dims, axis):
    return lax.broadcasted_iota(jnp.int32, dims, axis)


def one_hot(condition):
    return condition.astype(f32).astype(bf16)


def halves(x):
    high = x.astype(bf16)
    return high, (x - high.astype(f32)).astype(bf16)


def moves():
    pack = np.zeros((EXT, LANES, 2, LANES), np.float32)
    spread = np.zeros((2, LANES, EDGES, LANES), np.float32)
    own = np.zeros((GROUP, LANES, LANES), np.float32)
    for r in range(EXT):
        at = SIDE * (r // EDGES)
        for c in range(HALO):
            pack[r, c, 0, HALO * r + c] = 1
            pack[r, LANES - HALO + c, 1, HALO * r + c] = 1
            spread[0, HALO * r + c, r % EDGES, at + SIDE - HALO + c] = 1
            spread[1, HALO * r + c, r % EDGES, at + c] = 1
    for k in range(GROUP):
        for c in range(REACH):
            own[k, c, SIDE * k + HALO + c] = 1
            own[k, LANES - REACH + c, SIDE * k + HALO + REACH + c] = 1
    return (
        jnp.asarray(pack.reshape(EXT * LANES, 2 * LANES), bf16),
        jnp.asarray(spread.reshape(2 * LANES, EDGES * LANES), bf16),
        jnp.asarray(own.reshape(GROUP * LANES, LANES), bf16),
    )


def mixing_powers(m_ref):
    power = {1: m_ref[...]}
    power[2] = exact(power[1], power[1])
    power[3] = exact(power[1], power[2])
    power[4] = exact(power[2], power[2])
    power[5] = exact(power[2], power[3])
    power[6] = exact(power[3], power[3])
    return power


def flux_body(table_ref, a_ref, m_ref, sst_ref, pay_ref, g_hbm, block_ref, g_ref, sem):
    levels = m_ref.shape[0]
    bottom = levels - 1
    power = mixing_powers(m_ref)
    first = (iota((1, levels), 1) == bottom).astype(f32)
    rows = [first] + [power[n][bottom:, :] for n in range(1, STEPS)]
    rows = jnp.concatenate(rows + [jnp.zeros((8 - STEPS, levels), f32)], axis=0)
    row_high, row_low = halves(rows)
    both = jnp.concatenate([row_high.astype(f32), row_low.astype(f32)], axis=0).astype(bf16)
    base = []
    for v in range(4):
        high, low = halves(a_ref[v])
        one = times(both, high)
        base.append(one[:8] + one[8:] + times(row_high, low))
    corner = {n: power[n][bottom:, bottom:] for n in range(1, STEPS)}
    sst = sst_ref[...]
    gained = []
    fluxes = []
    east, north = jnp.zeros_like(sst), jnp.zeros_like(sst)
    for n in range(STEPS):
        now = []
        for v in range(4):
            value = base[v][n : n + 1]
            for k in range(n):
                value = value + corner[n - k] * gained[k][v]
            now.append(value)
        wind = jnp.sqrt(now[2] * now[2] + now[3] * now[3] + 1.0)
        flux = (
            heat_rate * wind * (sst - now[0]),
            vapour_rate * wind * (saturation * sst - now[1]),
            drag_rate * wind * now[2],
            drag_rate * wind * now[3],
        )
        fluxes.append(flux)
        gained.append([flux_gains[v] * flux[v] for v in range(4)])
        east, north = (
            turn[0, 0] * east + turn[0, 1] * north + flux[2],
            turn[1, 0] * east + turn[1, 1] * north + flux[3],
        )
    blank = [jnp.zeros_like(sst)] * (8 - STEPS)
    for v in range(4):
        g_ref[v] = jnp.concatenate([gained[n][v] for n in range(STEPS)] + blank, axis=0)
    copy = pltpu.make_async_copy(g_ref, g_hbm, sem)
    copy.start()
    pairs = [(fluxes[n][0], fluxes[n][1]) for n in range(STEPS)] + [(east, north)]
    block = iota((8, LANES), 0)
    left = iota((8, LANES), 1) < 64
    even = block % 2 == 0
    for i, pair in enumerate(pairs):
        parts = []
        for side in range(2):
            spread = jnp.zeros((8, LANES), f32)
            for q in range(4):
                tile = jnp.broadcast_to(pair[side][:, q * LANES : (q + 1) * LANES], (8, LANES))
                spread = jnp.where(block // 2 == q, tile, spread)
            parts.append(jnp.where(even == (side == 0), spread, pltpu.roll(spread, 64, 1)))
        block_ref[pl.ds(i, 8, stride=8), :] = jnp.where(left, parts[0], parts[1])
    block_ref[pl.ds(7, 8, stride=8), :] = jnp.zeros((8, LANES), f32)
    for d in range(pay_ref.shape[0] // 16):
        chosen = []
        for side in range(2):
            at = jnp.maximum(table_ref[side, d], 0) * 8
            chosen.append(block_ref[pl.ds(pl.multiple_of(at, 8), 8), :])
        pay_ref[16 * d : 16 * d + 16, :] = jnp.concatenate(chosen, axis=0).astype(bf16)
    copy.wait()


def atmosphere_body(a_ref, g_ref, m_ref, out_ref):
    levels = m_ref.shape[0]
    power = mixing_powers(m_ref)
    lane = iota((levels, 8), 1)
    edge = jnp.zeros((levels, 8), f32)
    for n in range(STEPS):
        edge = jnp.where(lane == n, power[STEPS - n][:, levels - 1 :], edge)
    for v in range(4):
        out_ref[v] = exact(power[STEPS], a_ref[v]) + exact(edge, g_ref[v])


def finish_body(table_ref, in_ref, out_ref):
    rows = in_ref.shape[0]
    block, lane = iota((8, rows), 0), iota((8, rows), 1)
    ones = []
    for side in range(2):
        named = table_ref[side : side + 1, :] == block
        for f in range(3):
            ones.append((named & (lane % 4 == f)).astype(f32))
    ones = jnp.concatenate(ones, axis=0).astype(bf16)
    high, low = halves(in_ref[...])
    sums = times(ones, high) + times(ones, low)
    left = iota((1, LANES), 1) < 64
    for f in range(3):
        low = sums[8 * f : 8 * f + 8] + pltpu.roll(sums[24 + 8 * f : 32 + 8 * f], 64, 1)
        high = pltpu.roll(low, 64, 1)
        for q in range(4):
            out_ref[f : f + 1, q * LANES : (q + 1) * LANES] = jnp.where(
                left, low[2 * q : 2 * q + 1], high[2 * q + 1 : 2 * q + 2]
            )


def cells_body(w_ref, out_ref, t_ref, low_ref, high_ref):
    left = iota((16, LANES), 1) < 64
    tiles = w_ref.shape[1] // LANES
    for i in range(tiles):
        t_ref[i * 64 : (i + 1) * 64] = w_ref[:, i * LANES : (i + 1) * LANES].astype(f32)
    for i in range(tiles):
        k = [t_ref[pl.ds(i * 64 + s, 16, stride=4), :] for s in range(4)]
        moved = [pltpu.roll(x, 64, 1) for x in k]
        low_ref[pl.ds(2 * i, 16, stride=64), :] = jnp.where(left, k[0], moved[1])
        high_ref[pl.ds(2 * i, 16, stride=64), :] = jnp.where(left, k[2], moved[3])
        low_ref[pl.ds(2 * i + 1, 16, stride=64), :] = jnp.where(left, moved[0], k[1])
        high_ref[pl.ds(2 * i + 1, 16, stride=64), :] = jnp.where(left, moved[2], k[3])
    out_ref[:, :LANES] = low_ref[...].astype(bf16)
    out_ref[:, LANES:] = high_ref[...].astype(bf16)


def rows_body(x_ref, v_ref, wet_ref, z_ref, f_ref):
    levels = x_ref.shape[1] // ROWS
    for t in range(2):
        f_ref[t] = v_ref[t].astype(f32)
    for r in range(ROWS):
        for t in range(2):
            z_ref[r, (2 + t) * levels : (3 + t) * levels, :] = f_ref[
                t, pl.ds(r, levels, stride=ROWS), :
            ].astype(bf16)
        wet = jnp.broadcast_to(wet_ref[r : r + 1, :].astype(f32), (16, LANES))
        z_ref[r, 4 * levels :, :] = wet.astype(bf16)
    for r in range(ROWS):
        for t in range(2):
            z_ref[r, t * levels : (t + 1) * levels, :] = x_ref[
                t, pl.ds(r, levels, stride=ROWS), :
            ].astype(bf16)


def widened(before_ref, own_ref, after_ref):
    rows = [before_ref[r] for r in range(HALO)]
    rows += [own_ref[r] for r in range(ROWS)]
    return rows + [after_ref[r] for r in range(HALO)]


def pack_body(before_ref, z_ref, after_ref, pack_ref, first_ref, last_ref):
    rows = widened(before_ref, z_ref, after_ref)
    packed = times(jnp.concatenate(rows, axis=1), pack_ref[...]).astype(bf16)
    first_ref[...] = packed[:, :LANES]
    last_ref[...] = packed[:, LANES:]


def forcing_rows(f_ref, before_ref, after_ref):
    blank = [jnp.zeros((16, LANES), bf16)]
    rows = blank + [before_ref[r] for r in range(HALO - 1)]
    rows += [f_ref[16 * r : 16 * r + 16].astype(bf16) for r in range(ROWS)]
    return rows + [after_ref[r] for r in range(HALO - 1)] + blank


def pack_forcing_body(f_ref, before_ref, after_ref, pack_ref, first_ref, last_ref):
    rows = forcing_rows(f_ref, before_ref, after_ref)
    packed = times(jnp.concatenate(rows, axis=1), pack_ref[...]).astype(bf16)
    first_ref[...] = packed[:, :LANES]
    last_ref[...] = packed[:, LANES:]


def edge_tile(g, rows, sides, spread_ref, own_ref):
    mine = [rows[r] for r in range(g, EXT, EDGES)]
    return times(jnp.concatenate(mine, axis=1), own_ref[: len(mine) * LANES, :]) + times(
        sides, spread_ref[:, g * LANES : (g + 1) * LANES]
    )


def around(idx, get):
    here = get(idx)
    if idx < EXT:
        north, south = get(idx + 1), get(idx - 1)
    else:
        north = get(idx + 1) if idx + 1 < TILES else pltpu.roll(get(EXT), LANES - SIDE, 1)
        south = get(idx - 1) if idx > EXT else pltpu.roll(get(TILES - 1), SIDE, 1)
    return here, pltpu.roll(here, LANES - 1, 1), pltpu.roll(here, 1, 1), north, south


def ocean_step(n, x_ref, coef_ref, mix_ref, cat_ref, store, force=None):
    levels = mix_ref.shape[0]
    tiles = list(range(n + 1, EXT - 1 - n)) + list(range(EXT, TILES))
    first = iota((8, LANES), 0) == 0
    for lo in range(0, len(tiles), 4):
        some = tiles[lo : lo + 4]
        slot = (lo // 4) % 2
        for at in range(0, levels, 16):
            for i, idx in enumerate(some):
                here, east, west, north, south = around(idx, lambda j: x_ref[j, at : at + 16, :])
                stepped = (
                    coef_ref[0, idx, at : at + 16, :] * here
                    + (coef_ref[1, idx, at : at + 16, :] * east
                       + coef_ref[2, idx, at : at + 16, :] * west)
                    + (coef_ref[3, idx, at : at + 16, :] * north
                       + coef_ref[4, idx, at : at + 16, :] * south)
                )
                if force is not None and at == 0:
                    top = stepped[:8] + jnp.where(first, force(idx), 0.0)
                    stepped = jnp.concatenate([top, stepped[8:]], axis=0)
                upper, lower = halves(stepped)
                cols = slice(i * LANES, (i + 1) * LANES)
                cat_ref[slot, at : at + 16, cols] = upper
                cat_ref[slot, levels + at : levels + at + 16, cols] = upper
                cat_ref[slot, 2 * levels + at : 2 * levels + at + 16, cols] = lower
        mixed = times(mix_ref[...], cat_ref[slot, :, : len(some) * LANES])
        for i, idx in enumerate(some):
            store(idx, mixed[:, i * LANES : (i + 1) * LANES])


def coefficient_body(
    before_ref, z_ref, after_ref, west_ref, east_ref, x_ref, mix_ref, spread_ref, own_ref,
    coef_ref, x1_ref, salt_ref, wet_ref, x0_ref, near_ref, edge_ref, cat_ref,
):
    levels = mix_ref.shape[0]
    rows = widened(before_ref, z_ref, after_ref)
    sides = jnp.concatenate([east_ref[...], west_ref[...]], axis=1)
    for g in range(EDGES):
        edge_ref[g] = edge_tile(g, rows, sides, spread_ref, own_ref).astype(bf16)

    def of(idx, at):
        if idx >= EXT:
            return edge_ref[idx - EXT, at, :].astype(f32)
        if idx < HALO:
            return before_ref[idx, at, :].astype(f32)
        if idx < HALO + ROWS:
            return z_ref[idx - HALO, at, :].astype(f32)
        return after_ref[idx - HALO - ROWS, at, :].astype(f32)

    wets = [of(idx, pl.ds(4 * levels, 16))[:8] for idx in range(TILES)]
    for idx in range(TILES):
        wet_ref[idx] = wets[idx]
    inner = list(range(1, EXT - 1)) + list(range(EXT, TILES))
    for idx in inner:
        here, *near = around(idx, lambda j: wets[j])
        for s in range(4):
            near_ref[s, idx] = here * near[s]

    def part(c, carry):
        at = pl.multiple_of(c * 16, 16)
        here_at = pl.ds(at, 16)
        for idx in inner:
            along = 0.5 * of(idx, pl.ds(2 * levels + at, 16))
            across = 0.5 * of(idx, pl.ds(3 * levels + at, 16))
            near = []
            for s in range(4):
                one = near_ref[s, idx]
                near.append(jnp.concatenate([one, one], axis=0))
            c_east = near[0] * (diffusion - along)
            c_west = near[1] * (diffusion + along)
            c_north = near[2] * (diffusion - across)
            c_south = near[3] * (diffusion + across)
            coef_ref[0, idx, here_at, :] = 1.0 - ((c_east + c_west) + (c_north + c_south))
            coef_ref[1, idx, here_at, :] = c_east
            coef_ref[2, idx, here_at, :] = c_west
            coef_ref[3, idx, here_at, :] = c_north
            coef_ref[4, idx, here_at, :] = c_south
        for t, to_ref in enumerate((x0_ref, salt_ref)):
            for idx in range(TILES):
                if not HALO <= idx < HALO + ROWS:
                    to_ref[idx, here_at, :] = of(idx, pl.ds(t * levels + at, 16))
        return carry

    lax.fori_loop(0, levels // 16, part, 0)
    for t, to_ref in enumerate((x0_ref, salt_ref)):
        for r in range(ROWS):
            to_ref[HALO + r] = x_ref[t, pl.ds(r, levels, stride=ROWS), :]

    def store(idx, value):
        x1_ref[idx] = value

    ocean_step(0, x0_ref, coef_ref, mix_ref, cat_ref, store)


def remap_body(arrival_ref, in_ref, w_ref, u_ref, wet_ref, f_ref, up_ref, down_ref, u_out_ref):
    def pick(j):
        t = arrival_ref[0, j]
        at = pl.multiple_of((t >> 1) * 16, 16)
        window = in_ref[pl.ds(at, 16), :].astype(f32)
        return jnp.where((t & 1) == 1, window[8:], window[:8])

    left = iota((8, LANES), 1) < 64
    left_two = iota((16, LANES), 1) < 64
    for r in range(ROWS):
        sources = []
        for side in range(2):
            even, odd = [], []
            for pair in range(2):
                j = 4 * (2 * r + side) + 2 * pair
                one, two = pick(j), pick(j + 1)
                even.append(jnp.where(left, one, pltpu.roll(two, 64, 1)))
                odd.append(jnp.where(left, pltpu.roll(one, 64, 1), two))
            sources.append(jnp.concatenate(even, axis=1))
            sources.append(jnp.concatenate(odd, axis=1))
        sources = jnp.concatenate(sources, axis=0).astype(bf16)
        product = times_rows(sources, w_ref[r * LANES : (r + 1) * LANES, :])
        forcing = jnp.where(left_two, product[:16], product[16:])
        f_ref[16 * r : 16 * r + 16, :] = forcing
        if r < HALO - 1:
            down_ref[r] = forcing.astype(bf16)
        if r >= ROWS - HALO + 1:
            up_ref[r - (ROWS - HALO + 1)] = forcing.astype(bf16)
    whole = np.linalg.matrix_power(turn, STEPS)
    wet = wet_ref[...].astype(f32)
    push = [surface_push * f_ref[pl.ds(6 + 8 * v, ROWS, stride=16), :] for v in range(2)]
    for v in range(2):
        ahead = float(whole[v, 0]) * u_ref[0] + float(whole[v, 1]) * u_ref[1] + push[v]
        u_out_ref[v] = u_ref[v] + wet * (ahead - u_ref[v])


def returned_rows(fields, w_ref, place, rows):
    blocks = 2 * ROWS
    block, lane = iota((blocks, LANES), 0), iota((blocks, LANES), 1)
    spread = []
    for field in fields:
        parts = []
        for r in range(ROWS):
            mine = block == 2 * r + (lane >= 64).astype(jnp.int32)
            parts.append(jnp.where(mine, field[r : r + 1], 0.0))
        spread.append(jnp.concatenate(parts, axis=1))
    terms = times(jnp.concatenate(spread, axis=0).astype(bf16), w_ref[...])
    high_parts, low_parts, ones = [], [], []
    target = iota((rows, LANES), 0)
    for f in range(len(fields)):
        mine = terms[f * blocks : (f + 1) * blocks]
        pieces = []
        for half in range(2):
            for k in range(4):
                piece = mine[:, (k // 2) * LANES : (k // 2 + 1) * LANES]
                if k % 2 != half:
                    piece = pltpu.roll(piece, 64, 1)
                pieces.append(jnp.where((lane >= 64) == (half == 1), piece, 0.0))
        high, low = halves(jnp.concatenate(pieces, axis=0))
        high_parts.append(high)
        low_parts.append(low)
        ones.append(one_hot(target == place + f))
    return times(
        jnp.concatenate(ones + ones, axis=1), jnp.concatenate(high_parts + low_parts, axis=0)
    )


def tracer_body(t, *refs):
    x_ref, coef_ref, wet_ref, mix_ref, f_ref, before_ref, after_ref, west_ref, east_ref = refs[:9]
    spread_ref, own_ref = refs[9:11]
    if t == 0:
        column_ref, w_ref, place_ref, u_ref, out_ref, send_ref = refs[11:17]
        one_ref, two_ref, force_ref, cat_ref, sst_ref = refs[17:]
    else:
        out_ref, one_ref, two_ref, force_ref, cat_ref = refs[11:]
    levels = mix_ref.shape[0]
    rows = forcing_rows(f_ref, before_ref, after_ref)
    sides = jnp.concatenate([east_ref[...], west_ref[...]], axis=1)
    for idx in range(1, TILES):
        if idx == EXT - 1:
            continue
        if HALO <= idx < HALO + ROWS:
            row = 16 * (idx - HALO)
            forcing = f_ref[row : row + 16, :]
        elif idx < EXT:
            forcing = rows[idx].astype(f32)
        else:
            forcing = edge_tile(idx - EXT, rows, sides, spread_ref, own_ref)
        force_ref[idx] = surface_gain[t] * wet_ref[idx] * forcing[8 * t : 8 * t + 8]
    if t == 0:
        column = jnp.broadcast_to(column_ref[:, 0:1], (levels, LANES))
        for idx in range(1, TILES):
            if idx != EXT - 1:
                one_ref[idx] = x_ref[idx] + column * force_ref[idx, 0:1, :]
        old, new = one_ref, two_ref
    else:
        old, new = x_ref, one_ref
    for n in range(1 if t == 0 else 0, STEPS):

        def store(idx, value, new=new):
            new[idx] = value

        def force(idx, n=n):
            return force_ref[idx, n : n + 1, :]

        ocean_step(n, old, coef_ref, mix_ref, cat_ref, store, force)
        if t == 1 and n == 0:
            old, new = one_ref, two_ref
        else:
            old, new = new, old
    lane = iota((16, LANES), 1)
    for r in range(ROWS):
        idx = HALO + r
        at = SIDE * (idx // EDGES) + HALO
        edge = EXT + idx % EDGES
        for lo in range(0, levels, 16):
            side = old[edge, lo : lo + 16, :]
            value = jnp.where(
                lane < HALO, pltpu.roll(side, (LANES - at) % LANES, 1), old[idx, lo : lo + 16, :]
            )
            here = at + REACH + HALO
            value = jnp.where(
                lane >= LANES - HALO, pltpu.roll(side, (LANES - HALO - here) % LANES, 1), value
            )
            out_ref[pl.ds(lo * ROWS + r, 16, stride=ROWS), :] = value
            if t == 0 and lo == 0:
                sst_ref[r : r + 1, :] = value[0:1]
    if t == 0:
        fields = [sst_ref[...], u_ref[0], u_ref[1]]
        fields = [field.astype(bf16).astype(f32) for field in fields]
        send_ref[...] = returned_rows(fields, w_ref, place_ref[...], send_ref.shape[0])


def neighbours(size):
    up = [(i, i + 1) for i in range(size - 1)]
    return up, [(j, i) for i, j in up]


def on_device(
    atmosphere_level_state,
    atmosphere_mixing_map,
    sea_surface_temps,
    tracers,
    currents,
    ocean_advect_velocity,
    ocean_mixing_map,
    ocean_cell_mask,
    remap_weight_tiles,
    outgoing_block_table,
    arrival_slot_table,
):
    band = ("row", "col")
    peers = lax.axis_size(band)
    levels = tracers.shape[1]
    air_levels, air_columns = atmosphere_level_state.shape[1:]
    rows_axis = ("comp", "row")
    up, down = neighbours(lax.axis_size(rows_axis))
    right, leftward = neighbours(lax.axis_size("col"))
    pack_moves, spread_moves, own_moves = moves()

    table = outgoing_block_table.reshape(peers, 2).T
    arrival = arrival_slot_table.reshape(1, 64)
    by_k = arrival.reshape(2 * ROWS, 4).T.reshape(1, 64)
    place = jnp.concatenate(
        [jnp.where(by_k % 2 == side, (by_k // 2) * 4, -64) for side in range(2)], axis=1
    )

    payload, gained = call(
        flux_body,
        (shape((peers * 16, LANES), bf16), shape((4, 8, air_columns))),
        "fluxes",
        [SMEM, VMEM, VMEM, VMEM],
        (VMEM, HBM),
        scratch=[
            pltpu.VMEM((64, LANES), f32),
            pltpu.VMEM((4, 8, air_columns), f32),
            pltpu.SemaphoreType.DMA,
        ],
        micros=3,
    )(table, atmosphere_level_state, atmosphere_mixing_map, sea_surface_temps[None])
    payload, wet_rows = lax.optimization_barrier((payload, ocean_cell_mask))
    arrived = lax.all_to_all(payload, band, 0, 0, tiled=True)

    flat = tracers.reshape(2, levels * ROWS, LANES)
    depth = 4 * levels + 16
    z = call(
        rows_body,
        shape((ROWS, depth, LANES), bf16),
        "rows",
        [VMEM] * 3,
        scratch=[pltpu.VMEM(flat.shape, f32)],
    )(flat, ocean_advect_velocity.reshape(flat.shape), wet_rows)
    before = lax.ppermute(z[ROWS - HALO :], rows_axis, up)
    after = lax.ppermute(z[:HALO], rows_axis, down)
    edge_shape = shape((depth, LANES), bf16)
    first, last = call(pack_body, (edge_shape, edge_shape), "pack", [VMEM] * 4)(
        before, z, after, pack_moves
    )
    east_in = lax.ppermute(first, "col", leftward)
    west_in = lax.ppermute(last, "col", right)
    cells = call(
        cells_body,
        shape((ROWS * LANES, WIDE), bf16),
        "cells",
        [VMEM],
        scratch=[
            pltpu.VMEM((32 * 64, LANES), f32),
            pltpu.VMEM((ROWS * LANES, LANES), f32),
            pltpu.VMEM((ROWS * LANES, LANES), f32),
        ],
    )(remap_weight_tiles.reshape(64, 4096))
    rounded = lax.reduce_precision(ocean_mixing_map, 8, 7)
    upper, lower = rounded.astype(bf16), (ocean_mixing_map - rounded).astype(bf16)
    mix = jnp.concatenate([upper, lower, upper], axis=1)
    wide = (TILES, levels, LANES)
    cat = pltpu.VMEM((2, 3 * levels, 4 * LANES), bf16)
    edge_rows = shape((HALO - 1, 16, LANES), bf16)
    forcing, send_up, send_down, ocean_currents = call(
        remap_body,
        (shape((ROWS * 16, LANES)), edge_rows, edge_rows, shape(currents.shape)),
        "remap",
        [SMEM] + [VMEM] * 4,
    )(arrival, arrived, cells, currents, ocean_cell_mask)
    f_before = lax.ppermute(send_up, rows_axis, up)
    f_after = lax.ppermute(send_down, rows_axis, down)
    strip = shape((16, LANES), bf16)
    f_first, f_last = call(pack_forcing_body, (strip, strip), "pack_forcing", [VMEM] * 4)(
        forcing, f_before, f_after, pack_moves
    )
    f_first, f_last, mix = lax.optimization_barrier((f_first, f_last, mix))
    f_east = lax.ppermute(f_first, "col", leftward)
    f_west = lax.ppermute(f_last, "col", right)

    coef, x1, salt, wet = call(
        coefficient_body,
        (shape((5, *wide)), shape(wide), shape(wide), shape((TILES, 8, LANES))),
        "coefficients",
        [VMEM] * 9,
        scratch=[
            pltpu.VMEM(wide, f32),
            pltpu.VMEM((4, TILES, 8, LANES), f32),
            pltpu.VMEM((EDGES, depth, LANES), bf16),
            cat,
        ],
        limit=24,
        micros=4,
    )(before, z, after, west_in, east_in, flat, mix, spread_moves, own_moves)
    shared = (coef, wet, mix, forcing, f_before, f_after, f_west, f_east, spread_moves, own_moves)
    scratch = [
        pltpu.VMEM(wide, f32),
        pltpu.VMEM(wide, f32),
        pltpu.VMEM((TILES, 8, LANES), f32),
        cat,
    ]
    warm, terms = call(
        functools.partial(tracer_body, 0),
        (shape(flat.shape[1:]), shape((peers * 4, LANES))),
        "temperature",
        [VMEM] * 15,
        scratch=scratch + [pltpu.VMEM((ROWS, LANES), f32)],
        limit=24,
        micros=6,
    )(x1, *shared, ocean_mixing_map, cells, place, ocean_currents)
    home = lax.all_to_all(terms, band, 0, 0, tiled=True)
    gained, terms = lax.optimization_barrier((gained, terms))
    atm_final = call(
        atmosphere_body,
        shape(atmosphere_level_state.shape),
        "atmosphere",
        [VMEM] * 3,
        micros=3,
    )(atmosphere_level_state, gained, atmosphere_mixing_map)
    cold = call(
        functools.partial(tracer_body, 1),
        shape(flat.shape[1:]),
        "salinity",
        [VMEM] * 11,
        scratch=scratch,
        limit=24,
        micros=6,
    )(salt, *shared)
    returned = call(finish_body, shape((3, air_columns)), "finish", [VMEM, VMEM])(
        jnp.repeat(table, 4, axis=1), home
    )
    ocean_tracers = jnp.stack([warm, cold]).reshape(tracers.shape)
    return (atm_final, ocean_tracers, ocean_currents, returned)


def solution(mesh):
    return jax.shard_map(
        on_device,
        mesh=mesh,
        in_specs=(
            P(None, None, ("comp", "row", "col")),
            P(),
            P(("comp", "row", "col")),
            P(None, None, ("comp", "row"), "col"),
            P(None, ("comp", "row"), "col"),
            P(None, None, ("comp", "row"), "col"),
            P(),
            P(("comp", "row"), "col"),
            P("comp", ("row", "col"), None, None),
            P("comp", ("row", "col"), None, None),
            P("comp", ("row", "col"), None),
        ),
        out_specs=(
            P(None, None, ("comp", "row", "col")),
            P(None, None, ("comp", "row"), "col"),
            P(None, ("comp", "row"), "col"),
            P(None, ("comp", "row", "col")),
        ),
        check_vma=False,
    )
```

```python
import functools

import jax
import jax.numpy as jnp
import numpy as np
from jax import lax
from jax.experimental import pallas as pl
from jax.experimental.pallas import tpu as pltpu
from jax.sharding import PartitionSpec as P

STEPS = 6
HALO = 6
ROWS = 8
EXT = ROWS + 2 * HALO
REACH = 2 * HALO
GROUP = 3
EDGES = -(-EXT // GROUP)
TILES = EXT + EDGES
SIDE = 2 * (HALO + REACH)
LANES = 128
WIDE = 256
HIGHEST = lax.Precision.HIGHEST
MIB = 1024 * 1024

heat_rate = 0.5
vapour_rate = 0.5
drag_rate = 0.3
saturation = 0.6
flux_gains = (0.3, 0.3, -0.3, -0.3)
diffusion = 0.15
surface_gain = (-0.3, 0.3)
surface_push = 0.3
current_drag = 0.1
coriolis = 0.2
turn = np.array([[1.0 - current_drag, coriolis], [-coriolis, 1.0 - current_drag]])

f32 = jnp.float32
bf16 = jnp.bfloat16
VMEM = pl.BlockSpec(memory_space=pltpu.VMEM)
HBM = pl.BlockSpec(memory_space=pltpu.HBM)
SMEM = pl.BlockSpec(memory_space=pltpu.SMEM)


def call(body, out_shape, name, in_specs, out_specs=None, scratch=(), aliases=None, limit=8, micros=1):
    if out_specs is None:
        out_specs = jax.tree.map(lambda _: VMEM, out_shape)
    return pl.pallas_call(
        body,
        out_shape=out_shape,
        in_specs=in_specs,
        out_specs=out_specs,
        scratch_shapes=list(scratch),
        input_output_aliases=aliases or {},
        compiler_params=pltpu.CompilerParams(vmem_limit_bytes=limit * MIB),
        cost_estimate=pl.CostEstimate(
            flops=int(micros * 1e9), bytes_accessed=int(micros * 3e6), transcendentals=0
        ),
        name=name,
    )


def shape(dims, dtype=f32):
    return jax.ShapeDtypeStruct(dims, dtype)


def exact(a, b):
    return jnp.dot(a, b, precision=HIGHEST, preferred_element_type=f32)


def times(a, b):
    return jnp.dot(a, b, preferred_element_type=f32)


def times_rows(a, b):
    return lax.dot_general(a, b, (((1,), (1,)), ((), ())), preferred_element_type=f32)


def iota(dims, axis):
    return lax.broadcasted_iota(jnp.int32, dims, axis)


def one_hot(condition):
    return condition.astype(f32).astype(bf16)


def halves(x):
    high = x.astype(bf16)
    return high, (x - high.astype(f32)).astype(bf16)


def moves():
    pack = np.zeros((EXT, LANES, 2, LANES), np.float32)
    spread = np.zeros((2, LANES, EDGES, LANES), np.float32)
    own = np.zeros((GROUP, LANES, LANES), np.float32)
    for r in range(EXT):
        at = SIDE * (r // EDGES)
        for c in range(HALO):
            pack[r, c, 0, HALO * r + c] = 1
            pack[r, LANES - HALO + c, 1, HALO * r + c] = 1
            spread[0, HALO * r + c, r % EDGES, at + SIDE - HALO + c] = 1
            spread[1, HALO * r + c, r % EDGES, at + c] = 1
    for k in range(GROUP):
        for c in range(REACH):
            own[k, c, SIDE * k + HALO + c] = 1
            own[k, LANES - REACH + c, SIDE * k + HALO + REACH + c] = 1
    return (
        jnp.asarray(pack.reshape(EXT * LANES, 2 * LANES), bf16),
        jnp.asarray(spread.reshape(2 * LANES, EDGES * LANES), bf16),
        jnp.asarray(own.reshape(GROUP * LANES, LANES), bf16),
    )


def mixing_powers(m_ref):
    power = {1: m_ref[...]}
    power[2] = exact(power[1], power[1])
    power[3] = exact(power[1], power[2])
    power[4] = exact(power[2], power[2])
    power[5] = exact(power[2], power[3])
    power[6] = exact(power[3], power[3])
    return power


def flux_body(
    table_ref, a_hbm, m_hbm, sst_hbm, pay_ref, g_hbm, block_ref, g_ref, a_ref, m_ref, sst_ref, sems, sem
):
    loads = [
        pltpu.make_async_copy(m_hbm, m_ref, sems.at[0]),
        pltpu.make_async_copy(sst_hbm, sst_ref, sems.at[1]),
        pltpu.make_async_copy(a_hbm, a_ref, sems.at[2]),
    ]
    for load in loads:
        load.start()
    loads[0].wait()
    levels = m_ref.shape[0]
    bottom = levels - 1
    power = mixing_powers(m_ref)
    first = (iota((1, levels), 1) == bottom).astype(f32)
    rows = [first] + [power[n][bottom:, :] for n in range(1, STEPS)]
    rows = jnp.concatenate(rows + [jnp.zeros((8 - STEPS, levels), f32)], axis=0)
    row_high, row_low = halves(rows)
    both = jnp.concatenate([row_high.astype(f32), row_low.astype(f32)], axis=0).astype(bf16)
    loads[1].wait()
    loads[2].wait()
    base = []
    for v in range(4):
        high, low = halves(a_ref[v])
        one = times(both, high)
        base.append(one[:8] + one[8:] + times(row_high, low))
    corner = {n: power[n][bottom:, bottom:] for n in range(1, STEPS)}
    sst = sst_ref[...]
    gained = []
    fluxes = []
    east, north = jnp.zeros_like(sst), jnp.zeros_like(sst)
    for n in range(STEPS):
        now = []
        for v in range(4):
            value = base[v][n : n + 1]
            for k in range(n):
                value = value + corner[n - k] * gained[k][v]
            now.append(value)
        wind = jnp.sqrt(now[2] * now[2] + now[3] * now[3] + 1.0)
        flux = (
            heat_rate * wind * (sst - now[0]),
            vapour_rate * wind * (saturation * sst - now[1]),
            drag_rate * wind * now[2],
            drag_rate * wind * now[3],
        )
        fluxes.append(flux)
        gained.append([flux_gains[v] * flux[v] for v in range(4)])
        east, north = (
            turn[0, 0] * east + turn[0, 1] * north + flux[2],
            turn[1, 0] * east + turn[1, 1] * north + flux[3],
        )
    blank = [jnp.zeros_like(sst)] * (8 - STEPS)
    for v in range(4):
        g_ref[v] = jnp.concatenate([gained[n][v] for n in range(STEPS)] + blank, axis=0)
    copy = pltpu.make_async_copy(g_ref, g_hbm, sem)
    copy.start()
    pairs = [(fluxes[n][0], fluxes[n][1]) for n in range(STEPS)] + [(east, north)]
    block = iota((8, LANES), 0)
    left = iota((8, LANES), 1) < 64
    even = block % 2 == 0
    for i, pair in enumerate(pairs):
        parts = []
        for side in range(2):
            spread = jnp.zeros((8, LANES), f32)
            for q in range(4):
                tile = jnp.broadcast_to(pair[side][:, q * LANES : (q + 1) * LANES], (8, LANES))
                spread = jnp.where(block // 2 == q, tile, spread)
            parts.append(jnp.where(even == (side == 0), spread, pltpu.roll(spread, 64, 1)))
        block_ref[pl.ds(i, 8, stride=8), :] = jnp.where(left, parts[0], parts[1])
    block_ref[pl.ds(7, 8, stride=8), :] = jnp.zeros((8, LANES), f32)
    for d in range(pay_ref.shape[0] // 16):
        chosen = []
        for side in range(2):
            at = jnp.maximum(table_ref[side, d], 0) * 8
            chosen.append(block_ref[pl.ds(pl.multiple_of(at, 8), 8), :])
        pay_ref[16 * d : 16 * d + 16, :] = jnp.concatenate(chosen, axis=0).astype(bf16)
    copy.wait()


def atmosphere_body(a_ref, g_ref, m_ref, out_ref):
    levels = m_ref.shape[0]
    power = mixing_powers(m_ref)
    lane = iota((levels, 8), 1)
    edge = jnp.zeros((levels, 8), f32)
    for n in range(STEPS):
        edge = jnp.where(lane == n, power[STEPS - n][:, levels - 1 :], edge)
    for v in range(4):
        out_ref[v] = exact(power[STEPS], a_ref[v]) + exact(edge, g_ref[v])


def finish_body(table_ref, in_ref, out_ref):
    rows = in_ref.shape[0]
    block, lane = iota((8, rows), 0), iota((8, rows), 1)
    ones = []
    for side in range(2):
        named = table_ref[side : side + 1, :] == block
        for f in range(3):
            ones.append((named & (lane % 4 == f)).astype(f32))
    ones = jnp.concatenate(ones, axis=0).astype(bf16)
    high, low = halves(in_ref[...])
    sums = times(ones, high) + times(ones, low)
    left = iota((1, LANES), 1) < 64
    for f in range(3):
        low = sums[8 * f : 8 * f + 8] + pltpu.roll(sums[24 + 8 * f : 32 + 8 * f], 64, 1)
        high = pltpu.roll(low, 64, 1)
        for q in range(4):
            out_ref[f : f + 1, q * LANES : (q + 1) * LANES] = jnp.where(
                left, low[2 * q : 2 * q + 1], high[2 * q + 1 : 2 * q + 2]
            )


def cells_body(w_ref, out_ref, t_ref, low_ref, high_ref):
    left = iota((16, LANES), 1) < 64
    tiles = w_ref.shape[1] // LANES
    for i in range(tiles):
        t_ref[i * 64 : (i + 1) * 64] = w_ref[:, i * LANES : (i + 1) * LANES].astype(f32)
    for i in range(tiles):
        k = [t_ref[pl.ds(i * 64 + s, 16, stride=4), :] for s in range(4)]
        moved = [pltpu.roll(x, 64, 1) for x in k]
        low_ref[pl.ds(2 * i, 16, stride=64), :] = jnp.where(left, k[0], moved[1])
        high_ref[pl.ds(2 * i, 16, stride=64), :] = jnp.where(left, k[2], moved[3])
        low_ref[pl.ds(2 * i + 1, 16, stride=64), :] = jnp.where(left, moved[0], k[1])
        high_ref[pl.ds(2 * i + 1, 16, stride=64), :] = jnp.where(left, moved[2], k[3])
    out_ref[:, :LANES] = low_ref[...].astype(bf16)
    out_ref[:, LANES:] = high_ref[...].astype(bf16)


def rows_body(x_ref, v_ref, wet_ref, z_ref, f_ref):
    levels = x_ref.shape[1] // ROWS
    for t in range(2):
        f_ref[t] = v_ref[t].astype(f32)
    for r in range(ROWS):
        for t in range(2):
            z_ref[r, (2 + t) * levels : (3 + t) * levels, :] = f_ref[
                t, pl.ds(r, levels, stride=ROWS), :
            ].astype(bf16)
        wet = jnp.broadcast_to(wet_ref[r : r + 1, :].astype(f32), (16, LANES))
        z_ref[r, 4 * levels :, :] = wet.astype(bf16)
    for r in range(ROWS):
        for t in range(2):
            z_ref[r, t * levels : (t + 1) * levels, :] = x_ref[
                t, pl.ds(r, levels, stride=ROWS), :
            ].astype(bf16)


def widened(before_ref, own_ref, after_ref):
    rows = [before_ref[r] for r in range(HALO)]
    rows += [own_ref[r] for r in range(ROWS)]
    return rows + [after_ref[r] for r in range(HALO)]


def pack_body(before_ref, z_ref, after_ref, pack_ref, first_ref, last_ref):
    rows = widened(before_ref, z_ref, after_ref)
    packed = times(jnp.concatenate(rows, axis=1), pack_ref[...]).astype(bf16)
    first_ref[...] = packed[:, :LANES]
    last_ref[...] = packed[:, LANES:]


def forcing_rows(f_ref, before_ref, after_ref):
    blank = [jnp.zeros((16, LANES), bf16)]
    rows = blank + [before_ref[r] for r in range(HALO - 1)]
    rows += [f_ref[16 * r : 16 * r + 16].astype(bf16) for r in range(ROWS)]
    return rows + [after_ref[r] for r in range(HALO - 1)] + blank


def pack_forcing_body(f_ref, before_ref, after_ref, pack_ref, first_ref, last_ref):
    rows = forcing_rows(f_ref, before_ref, after_ref)
    packed = times(jnp.concatenate(rows, axis=1), pack_ref[...]).astype(bf16)
    first_ref[...] = packed[:, :LANES]
    last_ref[...] = packed[:, LANES:]


def edge_tile(g, rows, sides, spread_ref, own_ref):
    mine = [rows[r] for r in range(g, EXT, EDGES)]
    return times(jnp.concatenate(mine, axis=1), own_ref[: len(mine) * LANES, :]) + times(
        sides, spread_ref[:, g * LANES : (g + 1) * LANES]
    )


def around(idx, get):
    here = get(idx)
    if idx < EXT:
        north, south = get(idx + 1), get(idx - 1)
    else:
        north = get(idx + 1) if idx + 1 < TILES else pltpu.roll(get(EXT), LANES - SIDE, 1)
        south = get(idx - 1) if idx > EXT else pltpu.roll(get(TILES - 1), SIDE, 1)
    return here, pltpu.roll(here, LANES - 1, 1), pltpu.roll(here, 1, 1), north, south


def ocean_step(n, x_ref, coef_ref, mix_ref, cat_ref, store, force=None):
    levels = mix_ref.shape[0]
    tiles = list(range(n + 1, EXT - 1 - n)) + list(range(EXT, TILES))
    first = iota((8, LANES), 0) == 0
    for lo in range(0, len(tiles), 4):
        some = tiles[lo : lo + 4]
        slot = (lo // 4) % 2
        for at in range(0, levels, 16):
            for i, idx in enumerate(some):
                here, east, west, north, south = around(idx, lambda j: x_ref[j, at : at + 16, :])
                stepped = (
                    coef_ref[0, idx, at : at + 16, :] * here
                    + (coef_ref[1, idx, at : at + 16, :] * east
                       + coef_ref[2, idx, at : at + 16, :] * west)
                    + (coef_ref[3, idx, at : at + 16, :] * north
                       + coef_ref[4, idx, at : at + 16, :] * south)
                )
                if force is not None and at == 0:
                    top = stepped[:8] + jnp.where(first, force(idx), 0.0)
                    stepped = jnp.concatenate([top, stepped[8:]], axis=0)
                upper, lower = halves(stepped)
                cols = slice(i * LANES, (i + 1) * LANES)
                cat_ref[slot, at : at + 16, cols] = upper
                cat_ref[slot, levels + at : levels + at + 16, cols] = upper
                cat_ref[slot, 2 * levels + at : 2 * levels + at + 16, cols] = lower
        mixed = times(mix_ref[...], cat_ref[slot, :, : len(some) * LANES])
        for i, idx in enumerate(some):
            store(idx, mixed[:, i * LANES : (i + 1) * LANES])


def coefficient_body(
    before_ref, z_ref, after_ref, west_ref, east_ref, x_ref, mix_ref, spread_ref, own_ref,
    coef_ref, x1_ref, salt_ref, wet_ref, x0_ref, near_ref, edge_ref, cat_ref,
):
    levels = mix_ref.shape[0]
    rows = widened(before_ref, z_ref, after_ref)
    sides = jnp.concatenate([east_ref[...], west_ref[...]], axis=1)
    for g in range(EDGES):
        edge_ref[g] = edge_tile(g, rows, sides, spread_ref, own_ref).astype(bf16)

    def of(idx, at):
        if idx >= EXT:
            return edge_ref[idx - EXT, at, :].astype(f32)
        if idx < HALO:
            return before_ref[idx, at, :].astype(f32)
        if idx < HALO + ROWS:
            return z_ref[idx - HALO, at, :].astype(f32)
        return after_ref[idx - HALO - ROWS, at, :].astype(f32)

    wets = [of(idx, pl.ds(4 * levels, 16))[:8] for idx in range(TILES)]
    for idx in range(TILES):
        wet_ref[idx] = wets[idx]
    inner = list(range(1, EXT - 1)) + list(range(EXT, TILES))
    for idx in inner:
        here, *near = around(idx, lambda j: wets[j])
        for s in range(4):
            near_ref[s, idx] = here * near[s]

    def part(c, carry):
        at = pl.multiple_of(c * 16, 16)
        here_at = pl.ds(at, 16)
        for idx in inner:
            along = 0.5 * of(idx, pl.ds(2 * levels + at, 16))
            across = 0.5 * of(idx, pl.ds(3 * levels + at, 16))
            near = []
            for s in range(4):
                one = near_ref[s, idx]
                near.append(jnp.concatenate([one, one], axis=0))
            c_east = near[0] * (diffusion - along)
            c_west = near[1] * (diffusion + along)
            c_north = near[2] * (diffusion - across)
            c_south = near[3] * (diffusion + across)
            coef_ref[0, idx, here_at, :] = 1.0 - ((c_east + c_west) + (c_north + c_south))
            coef_ref[1, idx, here_at, :] = c_east
            coef_ref[2, idx, here_at, :] = c_west
            coef_ref[3, idx, here_at, :] = c_north
            coef_ref[4, idx, here_at, :] = c_south
        for t, to_ref in enumerate((x0_ref, salt_ref)):
            for idx in range(TILES):
                if not HALO <= idx < HALO + ROWS:
                    to_ref[idx, here_at, :] = of(idx, pl.ds(t * levels + at, 16))
        return carry

    lax.fori_loop(0, levels // 16, part, 0)
    for t, to_ref in enumerate((x0_ref, salt_ref)):
        for r in range(ROWS):
            to_ref[HALO + r] = x_ref[t, pl.ds(r, levels, stride=ROWS), :]

    def store(idx, value):
        x1_ref[idx] = value

    ocean_step(0, x0_ref, coef_ref, mix_ref, cat_ref, store)


def remap_body(arrival_ref, in_ref, w_ref, u_ref, wet_ref, f_ref, up_ref, down_ref, u_out_ref):
    def pick(j):
        t = arrival_ref[0, j]
        at = pl.multiple_of((t >> 1) * 16, 16)
        window = in_ref[pl.ds(at, 16), :].astype(f32)
        return jnp.where((t & 1) == 1, window[8:], window[:8])

    left = iota((8, LANES), 1) < 64
    left_two = iota((16, LANES), 1) < 64
    for r in range(ROWS):
        sources = []
        for side in range(2):
            even, odd = [], []
            for pair in range(2):
                j = 4 * (2 * r + side) + 2 * pair
                one, two = pick(j), pick(j + 1)
                even.append(jnp.where(left, one, pltpu.roll(two, 64, 1)))
                odd.append(jnp.where(left, pltpu.roll(one, 64, 1), two))
            sources.append(jnp.concatenate(even, axis=1))
            sources.append(jnp.concatenate(odd, axis=1))
        sources = jnp.concatenate(sources, axis=0).astype(bf16)
        product = times_rows(sources, w_ref[r * LANES : (r + 1) * LANES, :])
        forcing = jnp.where(left_two, product[:16], product[16:])
        f_ref[16 * r : 16 * r + 16, :] = forcing
        if r < HALO - 1:
            down_ref[r] = forcing.astype(bf16)
        if r >= ROWS - HALO + 1:
            up_ref[r - (ROWS - HALO + 1)] = forcing.astype(bf16)
    whole = np.linalg.matrix_power(turn, STEPS)
    wet = wet_ref[...].astype(f32)
    push = [surface_push * f_ref[pl.ds(6 + 8 * v, ROWS, stride=16), :] for v in range(2)]
    for v in range(2):
        ahead = float(whole[v, 0]) * u_ref[0] + float(whole[v, 1]) * u_ref[1] + push[v]
        u_out_ref[v] = u_ref[v] + wet * (ahead - u_ref[v])


def returned_rows(fields, w_ref, place, rows):
    blocks = 2 * ROWS
    block, lane = iota((blocks, LANES), 0), iota((blocks, LANES), 1)
    spread = []
    for field in fields:
        parts = []
        for r in range(ROWS):
            mine = block == 2 * r + (lane >= 64).astype(jnp.int32)
            parts.append(jnp.where(mine, field[r : r + 1], 0.0))
        spread.append(jnp.concatenate(parts, axis=1))
    terms = times(jnp.concatenate(spread, axis=0).astype(bf16), w_ref[...])
    high_parts, low_parts, ones = [], [], []
    target = iota((rows, LANES), 0)
    for f in range(len(fields)):
        mine = terms[f * blocks : (f + 1) * blocks]
        pieces = []
        for half in range(2):
            for k in range(4):
                piece = mine[:, (k // 2) * LANES : (k // 2 + 1) * LANES]
                if k % 2 != half:
                    piece = pltpu.roll(piece, 64, 1)
                pieces.append(jnp.where((lane >= 64) == (half == 1), piece, 0.0))
        high, low = halves(jnp.concatenate(pieces, axis=0))
        high_parts.append(high)
        low_parts.append(low)
        ones.append(one_hot(target == place + f))
    return times(
        jnp.concatenate(ones + ones, axis=1), jnp.concatenate(high_parts + low_parts, axis=0)
    )


def tracer_body(t, *refs):
    x_ref, coef_ref, wet_ref, mix_ref, f_ref, before_ref, after_ref, west_ref, east_ref = refs[:9]
    spread_ref, own_ref = refs[9:11]
    if t == 0:
        column_ref, w_ref, place_ref, u_ref, out_hbm, send_ref = refs[11:17]
        one_ref, two_ref, force_ref, cat_ref, out_ref, sem, sst_ref = refs[17:]
    else:
        _, out_hbm, one_ref, two_ref, force_ref, cat_ref, out_ref, sem = refs[11:]
    levels = mix_ref.shape[0]
    rows = forcing_rows(f_ref, before_ref, after_ref)
    sides = jnp.concatenate([east_ref[...], west_ref[...]], axis=1)
    for idx in range(1, TILES):
        if idx == EXT - 1:
            continue
        if HALO <= idx < HALO + ROWS:
            row = 16 * (idx - HALO)
            forcing = f_ref[row : row + 16, :]
        elif idx < EXT:
            forcing = rows[idx].astype(f32)
        else:
            forcing = edge_tile(idx - EXT, rows, sides, spread_ref, own_ref)
        force_ref[idx] = surface_gain[t] * wet_ref[idx] * forcing[8 * t : 8 * t + 8]
    if t == 0:
        column = jnp.broadcast_to(column_ref[:, 0:1], (levels, LANES))
        for idx in range(1, TILES):
            if idx != EXT - 1:
                one_ref[idx] = x_ref[idx] + column * force_ref[idx, 0:1, :]
        old, new = one_ref, two_ref
    else:
        old, new = x_ref, one_ref
    for n in range(1 if t == 0 else 0, STEPS):

        def store(idx, value, new=new):
            new[idx] = value

        def force(idx, n=n):
            return force_ref[idx, n : n + 1, :]

        ocean_step(n, old, coef_ref, mix_ref, cat_ref, store, force)
        if t == 1 and n == 0:
            old, new = one_ref, two_ref
        else:
            old, new = new, old
    lane = iota((16, LANES), 1)
    for r in range(ROWS):
        idx = HALO + r
        at = SIDE * (idx // EDGES) + HALO
        edge = EXT + idx % EDGES
        for lo in range(0, levels, 16):
            side = old[edge, lo : lo + 16, :]
            value = jnp.where(
                lane < HALO, pltpu.roll(side, (LANES - at) % LANES, 1), old[idx, lo : lo + 16, :]
            )
            here = at + REACH + HALO
            value = jnp.where(
                lane >= LANES - HALO, pltpu.roll(side, (LANES - HALO - here) % LANES, 1), value
            )
            out_ref[pl.ds(lo * ROWS + r, 16, stride=ROWS), :] = value
            if t == 0 and lo == 0:
                sst_ref[r : r + 1, :] = value[0:1]
    copy = pltpu.make_async_copy(out_ref, out_hbm.at[t], sem)
    copy.start()
    if t == 0:
        fields = [sst_ref[...], u_ref[0], u_ref[1]]
        fields = [field.astype(bf16).astype(f32) for field in fields]
        send_ref[...] = returned_rows(fields, w_ref, place_ref[...], send_ref.shape[0])
    copy.wait()


def neighbours(size):
    up = [(i, i + 1) for i in range(size - 1)]
    return up, [(j, i) for i, j in up]


def on_device(
    atmosphere_level_state,
    atmosphere_mixing_map,
    sea_surface_temps,
    tracers,
    currents,
    ocean_advect_velocity,
    ocean_mixing_map,
    ocean_cell_mask,
    remap_weight_tiles,
    outgoing_block_table,
    arrival_slot_table,
):
    band = ("row", "col")
    peers = lax.axis_size(band)
    levels = tracers.shape[1]
    air_levels, air_columns = atmosphere_level_state.shape[1:]
    rows_axis = ("comp", "row")
    up, down = neighbours(lax.axis_size(rows_axis))
    right, leftward = neighbours(lax.axis_size("col"))
    pack_moves, spread_moves, own_moves = moves()

    table = outgoing_block_table.reshape(peers, 2).T
    arrival = arrival_slot_table.reshape(1, 64)
    by_k = arrival.reshape(2 * ROWS, 4).T.reshape(1, 64)
    place = jnp.concatenate(
        [jnp.where(by_k % 2 == side, (by_k // 2) * 4, -64) for side in range(2)], axis=1
    )

    payload, gained = call(
        flux_body,
        (shape((peers * 16, LANES), bf16), shape((4, 8, air_columns))),
        "fluxes",
        [SMEM, HBM, HBM, HBM],
        (VMEM, HBM),
        scratch=[
            pltpu.VMEM((64, LANES), f32),
            pltpu.VMEM((4, 8, air_columns), f32),
            pltpu.VMEM(atmosphere_level_state.shape, f32),
            pltpu.VMEM(atmosphere_mixing_map.shape, f32),
            pltpu.VMEM((1, air_columns), f32),
            pltpu.SemaphoreType.DMA((3,)),
            pltpu.SemaphoreType.DMA,
        ],
        limit=56,
        micros=3,
    )(table, atmosphere_level_state, atmosphere_mixing_map, sea_surface_temps[None])
    payload, wet_rows = lax.optimization_barrier((payload, ocean_cell_mask))
    arrived = lax.all_to_all(payload, band, 0, 0, tiled=True)

    flat = tracers.reshape(2, levels * ROWS, LANES)
    depth = 4 * levels + 16
    z = call(
        rows_body,
        shape((ROWS, depth, LANES), bf16),
        "rows",
        [VMEM] * 3,
        scratch=[pltpu.VMEM(flat.shape, f32)],
    )(flat, ocean_advect_velocity.reshape(flat.shape), wet_rows)
    before = lax.ppermute(z[ROWS - HALO :], rows_axis, up)
    after = lax.ppermute(z[:HALO], rows_axis, down)
    edge_shape = shape((depth, LANES), bf16)
    first, last = call(pack_body, (edge_shape, edge_shape), "pack", [VMEM] * 4)(
        before, z, after, pack_moves
    )
    east_in = lax.ppermute(first, "col", leftward)
    west_in = lax.ppermute(last, "col", right)
    cells = call(
        cells_body,
        shape((ROWS * LANES, WIDE), bf16),
        "cells",
        [VMEM],
        scratch=[
            pltpu.VMEM((32 * 64, LANES), f32),
            pltpu.VMEM((ROWS * LANES, LANES), f32),
            pltpu.VMEM((ROWS * LANES, LANES), f32),
        ],
    )(remap_weight_tiles.reshape(64, 4096))
    rounded = lax.reduce_precision(ocean_mixing_map, 8, 7)
    upper, lower = rounded.astype(bf16), (ocean_mixing_map - rounded).astype(bf16)
    mix = jnp.concatenate([upper, lower, upper], axis=1)
    wide = (TILES, levels, LANES)
    cat = pltpu.VMEM((2, 3 * levels, 4 * LANES), bf16)
    arrived, east_in, west_in = lax.optimization_barrier((arrived, east_in, west_in))

    edge_rows = shape((HALO - 1, 16, LANES), bf16)
    forcing, send_up, send_down, ocean_currents = call(
        remap_body,
        (shape((ROWS * 16, LANES)), edge_rows, edge_rows, shape(currents.shape)),
        "remap",
        [SMEM] + [VMEM] * 4,
    )(arrival, arrived, cells, currents, ocean_cell_mask)
    f_before = lax.ppermute(send_up, rows_axis, up)
    f_after = lax.ppermute(send_down, rows_axis, down)
    strip = shape((16, LANES), bf16)
    f_first, f_last = call(pack_forcing_body, (strip, strip), "pack_forcing", [VMEM] * 4)(
        forcing, f_before, f_after, pack_moves
    )
    f_first, f_last, mix = lax.optimization_barrier((f_first, f_last, mix))
    f_east = lax.ppermute(f_first, "col", leftward)
    f_west = lax.ppermute(f_last, "col", right)

    coef, x1, salt, wet = call(
        coefficient_body,
        (shape((5, *wide)), shape(wide), shape(wide), shape((TILES, 8, LANES))),
        "coefficients",
        [VMEM] * 9,
        scratch=[
            pltpu.VMEM(wide, f32),
            pltpu.VMEM((4, TILES, 8, LANES), f32),
            pltpu.VMEM((EDGES, depth, LANES), bf16),
            cat,
        ],
        limit=24,
        micros=4,
    )(before, z, after, west_in, east_in, flat, mix, spread_moves, own_moves)
    shared = (coef, wet, mix, forcing, f_before, f_after, f_west, f_east, spread_moves, own_moves)
    scratch = [
        pltpu.VMEM(wide, f32),
        pltpu.VMEM(wide, f32),
        pltpu.VMEM((TILES, 8, LANES), f32),
        cat,
        pltpu.VMEM(flat.shape[1:], f32),
        pltpu.SemaphoreType.DMA,
    ]
    warm, terms = call(
        functools.partial(tracer_body, 0),
        (shape(flat.shape), shape((peers * 4, LANES))),
        "temperature",
        [VMEM] * 15,
        (HBM, VMEM),
        scratch=scratch + [pltpu.VMEM((ROWS, LANES), f32)],
        limit=24,
        micros=6,
    )(x1, *shared, ocean_mixing_map, cells, place, ocean_currents)
    home = lax.all_to_all(terms, band, 0, 0, tiled=True)
    gained, terms = lax.optimization_barrier((gained, terms))
    atm_final = call(
        atmosphere_body,
        shape(atmosphere_level_state.shape),
        "atmosphere",
        [VMEM] * 3,
        micros=3,
    )(atmosphere_level_state, gained, atmosphere_mixing_map)
    both = call(
        functools.partial(tracer_body, 1),
        shape(flat.shape),
        "salinity",
        [VMEM] * 11 + [HBM],
        HBM,
        scratch=scratch,
        aliases={11: 0},
        limit=24,
        micros=6,
    )(salt, *shared, warm)
    returned = call(finish_body, shape((3, air_columns)), "finish", [VMEM, VMEM])(
        jnp.repeat(table, 4, axis=1), home
    )
    return (atm_final, both.reshape(tracers.shape), ocean_currents, returned)


def solution(mesh):
    return jax.shard_map(
        on_device,
        mesh=mesh,
        in_specs=(
            P(None, None, ("comp", "row", "col")),
            P(),
            P(("comp", "row", "col")),
            P(None, None, ("comp", "row"), "col"),
            P(None, ("comp", "row"), "col"),
            P(None, None, ("comp", "row"), "col"),
            P(),
            P(("comp", "row"), "col"),
            P("comp", ("row", "col"), None, None),
            P("comp", ("row", "col"), None, None),
            P("comp", ("row", "col"), None),
        ),
        out_specs=(
            P(None, None, ("comp", "row", "col")),
            P(None, None, ("comp", "row"), "col"),
            P(None, ("comp", "row"), "col"),
            P(None, ("comp", "row", "col")),
        ),
        check_vma=False,
    )
```

```python
import functools

import jax
import jax.numpy as jnp
import numpy as np
from jax import lax
from jax.experimental import pallas as pl
from jax.experimental.pallas import tpu as pltpu
from jax.sharding import PartitionSpec as P

STEPS = 6
HALO = 6
ROWS = 8
EXT = ROWS + 2 * HALO
REACH = 2 * HALO
GROUP = 3
EDGES = -(-EXT // GROUP)
TILES = EXT + EDGES
SIDE = 2 * (HALO + REACH)
LANES = 128
WIDE = 256
HIGHEST = lax.Precision.HIGHEST
MIB = 1024 * 1024

heat_rate = 0.5
vapour_rate = 0.5
drag_rate = 0.3
saturation = 0.6
flux_gains = (0.3, 0.3, -0.3, -0.3)
diffusion = 0.15
surface_gain = (-0.3, 0.3)
surface_push = 0.3
current_drag = 0.1
coriolis = 0.2
turn = np.array([[1.0 - current_drag, coriolis], [-coriolis, 1.0 - current_drag]])

f32 = jnp.float32
bf16 = jnp.bfloat16
VMEM = pl.BlockSpec(memory_space=pltpu.VMEM)
HBM = pl.BlockSpec(memory_space=pltpu.HBM)
SMEM = pl.BlockSpec(memory_space=pltpu.SMEM)


def call(body, out_shape, name, in_specs, out_specs=None, scratch=(), aliases=None, limit=8, micros=1):
    if out_specs is None:
        out_specs = jax.tree.map(lambda _: VMEM, out_shape)
    return pl.pallas_call(
        body,
        out_shape=out_shape,
        in_specs=in_specs,
        out_specs=out_specs,
        scratch_shapes=list(scratch),
        input_output_aliases=aliases or {},
        compiler_params=pltpu.CompilerParams(vmem_limit_bytes=limit * MIB),
        cost_estimate=pl.CostEstimate(
            flops=int(micros * 1e9), bytes_accessed=int(micros * 3e6), transcendentals=0
        ),
        name=name,
    )


def shape(dims, dtype=f32):
    return jax.ShapeDtypeStruct(dims, dtype)


def exact(a, b):
    return jnp.dot(a, b, precision=HIGHEST, preferred_element_type=f32)


def times(a, b):
    return jnp.dot(a, b, preferred_element_type=f32)


def times_rows(a, b):
    return lax.dot_general(a, b, (((1,), (1,)), ((), ())), preferred_element_type=f32)


def iota(dims, axis):
    return lax.broadcasted_iota(jnp.int32, dims, axis)


def one_hot(condition):
    return condition.astype(f32).astype(bf16)


def halves(x):
    high = x.astype(bf16)
    return high, (x - high.astype(f32)).astype(bf16)


def moves():
    pack = np.zeros((EXT, LANES, 2, LANES), np.float32)
    spread = np.zeros((2, LANES, EDGES, LANES), np.float32)
    own = np.zeros((GROUP, LANES, LANES), np.float32)
    for r in range(EXT):
        at = SIDE * (r // EDGES)
        for c in range(HALO):
            pack[r, c, 0, HALO * r + c] = 1
            pack[r, LANES - HALO + c, 1, HALO * r + c] = 1
            spread[0, HALO * r + c, r % EDGES, at + SIDE - HALO + c] = 1
            spread[1, HALO * r + c, r % EDGES, at + c] = 1
    for k in range(GROUP):
        for c in range(REACH):
            own[k, c, SIDE * k + HALO + c] = 1
            own[k, LANES - REACH + c, SIDE * k + HALO + REACH + c] = 1
    return (
        jnp.asarray(pack.reshape(EXT * LANES, 2 * LANES), bf16),
        jnp.asarray(spread.reshape(2 * LANES, EDGES * LANES), bf16),
        jnp.asarray(own.reshape(GROUP * LANES, LANES), bf16),
    )


def mixing_powers(m_ref):
    power = {1: m_ref[...]}
    power[2] = exact(power[1], power[1])
    power[3] = exact(power[1], power[2])
    power[4] = exact(power[2], power[2])
    power[5] = exact(power[2], power[3])
    power[6] = exact(power[3], power[3])
    return power


def flux_body(
    table_ref, a_hbm, m_hbm, sst_hbm, pay_ref, g_hbm, block_ref, g_ref, a_ref, m_ref, sst_ref, sems, sem
):
    loads = [
        pltpu.make_async_copy(m_hbm, m_ref, sems.at[0]),
        pltpu.make_async_copy(sst_hbm, sst_ref, sems.at[1]),
        pltpu.make_async_copy(a_hbm, a_ref, sems.at[2]),
    ]
    for load in loads:
        load.start()
    loads[0].wait()
    levels = m_ref.shape[0]
    bottom = levels - 1
    power = mixing_powers(m_ref)
    first = (iota((1, levels), 1) == bottom).astype(f32)
    rows = [first] + [power[n][bottom:, :] for n in range(1, STEPS)]
    rows = jnp.concatenate(rows + [jnp.zeros((8 - STEPS, levels), f32)], axis=0)
    row_high, row_low = halves(rows)
    both = jnp.concatenate([row_high.astype(f32), row_low.astype(f32)], axis=0).astype(bf16)
    loads[1].wait()
    loads[2].wait()
    base = []
    for v in range(4):
        high, low = halves(a_ref[v])
        one = times(both, high)
        base.append(one[:8] + one[8:] + times(row_high, low))
    corner = {n: power[n][bottom:, bottom:] for n in range(1, STEPS)}
    sst = sst_ref[...]
    gained = []
    fluxes = []
    east, north = jnp.zeros_like(sst), jnp.zeros_like(sst)
    for n in range(STEPS):
        now = []
        for v in range(4):
            value = base[v][n : n + 1]
            for k in range(n):
                value = value + corner[n - k] * gained[k][v]
            now.append(value)
        wind = jnp.sqrt(now[2] * now[2] + now[3] * now[3] + 1.0)
        flux = (
            heat_rate * wind * (sst - now[0]),
            vapour_rate * wind * (saturation * sst - now[1]),
            drag_rate * wind * now[2],
            drag_rate * wind * now[3],
        )
        fluxes.append(flux)
        gained.append([flux_gains[v] * flux[v] for v in range(4)])
        east, north = (
            turn[0, 0] * east + turn[0, 1] * north + flux[2],
            turn[1, 0] * east + turn[1, 1] * north + flux[3],
        )
    blank = [jnp.zeros_like(sst)] * (8 - STEPS)
    for v in range(4):
        g_ref[v] = jnp.concatenate([gained[n][v] for n in range(STEPS)] + blank, axis=0)
    copy = pltpu.make_async_copy(g_ref, g_hbm, sem)
    copy.start()
    pairs = [(fluxes[n][0], fluxes[n][1]) for n in range(STEPS)] + [(east, north)]
    block = iota((8, LANES), 0)
    left = iota((8, LANES), 1) < 64
    even = block % 2 == 0
    for i, pair in enumerate(pairs):
        parts = []
        for side in range(2):
            spread = jnp.zeros((8, LANES), f32)
            for q in range(4):
                tile = jnp.broadcast_to(pair[side][:, q * LANES : (q + 1) * LANES], (8, LANES))
                spread = jnp.where(block // 2 == q, tile, spread)
            parts.append(jnp.where(even == (side == 0), spread, pltpu.roll(spread, 64, 1)))
        block_ref[pl.ds(i, 8, stride=8), :] = jnp.where(left, parts[0], parts[1])
    block_ref[pl.ds(7, 8, stride=8), :] = jnp.zeros((8, LANES), f32)
    for d in range(pay_ref.shape[0] // 16):
        chosen = []
        for side in range(2):
            at = jnp.maximum(table_ref[side, d], 0) * 8
            chosen.append(block_ref[pl.ds(pl.multiple_of(at, 8), 8), :])
        pay_ref[16 * d : 16 * d + 16, :] = jnp.concatenate(chosen, axis=0).astype(bf16)
    copy.wait()


def atmosphere_body(a_ref, g_ref, m_ref, out_ref, token_ref):
    token_ref[...] = jnp.zeros_like(token_ref)
    levels = m_ref.shape[0]
    power = mixing_powers(m_ref)
    lane = iota((levels, 8), 1)
    edge = jnp.zeros((levels, 8), f32)
    for n in range(STEPS):
        edge = jnp.where(lane == n, power[STEPS - n][:, levels - 1 :], edge)
    for v in range(4):
        out_ref[v] = exact(power[STEPS], a_ref[v]) + exact(edge, g_ref[v])


def finish_body(table_ref, in_ref, out_ref):
    rows = in_ref.shape[0]
    block, lane = iota((8, rows), 0), iota((8, rows), 1)
    ones = []
    for side in range(2):
        named = table_ref[side : side + 1, :] == block
        for f in range(3):
            ones.append((named & (lane % 4 == f)).astype(f32))
    ones = jnp.concatenate(ones, axis=0).astype(bf16)
    high, low = halves(in_ref[...])
    sums = times(ones, high) + times(ones, low)
    left = iota((1, LANES), 1) < 64
    for f in range(3):
        low = sums[8 * f : 8 * f + 8] + pltpu.roll(sums[24 + 8 * f : 32 + 8 * f], 64, 1)
        high = pltpu.roll(low, 64, 1)
        for q in range(4):
            out_ref[f : f + 1, q * LANES : (q + 1) * LANES] = jnp.where(
                left, low[2 * q : 2 * q + 1], high[2 * q + 1 : 2 * q + 2]
            )


def cells_body(w_ref, out_ref, t_ref, low_ref, high_ref):
    left = iota((16, LANES), 1) < 64
    tiles = w_ref.shape[1] // LANES
    for i in range(tiles):
        t_ref[i * 64 : (i + 1) * 64] = w_ref[:, i * LANES : (i + 1) * LANES].astype(f32)
    for i in range(tiles):
        k = [t_ref[pl.ds(i * 64 + s, 16, stride=4), :] for s in range(4)]
        moved = [pltpu.roll(x, 64, 1) for x in k]
        low_ref[pl.ds(2 * i, 16, stride=64), :] = jnp.where(left, k[0], moved[1])
        high_ref[pl.ds(2 * i, 16, stride=64), :] = jnp.where(left, k[2], moved[3])
        low_ref[pl.ds(2 * i + 1, 16, stride=64), :] = jnp.where(left, moved[0], k[1])
        high_ref[pl.ds(2 * i + 1, 16, stride=64), :] = jnp.where(left, moved[2], k[3])
    out_ref[:, :LANES] = low_ref[...].astype(bf16)
    out_ref[:, LANES:] = high_ref[...].astype(bf16)


def rows_body(x_ref, v_ref, wet_ref, z_ref, f_ref):
    levels = x_ref.shape[1] // ROWS
    for t in range(2):
        f_ref[t] = v_ref[t].astype(f32)
    for r in range(ROWS):
        for t in range(2):
            z_ref[r, (2 + t) * levels : (3 + t) * levels, :] = f_ref[
                t, pl.ds(r, levels, stride=ROWS), :
            ].astype(bf16)
        wet = jnp.broadcast_to(wet_ref[r : r + 1, :].astype(f32), (16, LANES))
        z_ref[r, 4 * levels :, :] = wet.astype(bf16)
    for r in range(ROWS):
        for t in range(2):
            z_ref[r, t * levels : (t + 1) * levels, :] = x_ref[
                t, pl.ds(r, levels, stride=ROWS), :
            ].astype(bf16)


def widened(before_ref, own_ref, after_ref):
    rows = [before_ref[r] for r in range(HALO)]
    rows += [own_ref[r] for r in range(ROWS)]
    return rows + [after_ref[r] for r in range(HALO)]


def forcing_rows(f_ref, before_ref, after_ref):
    blank = [jnp.zeros((16, LANES), bf16)]
    rows = blank + [before_ref[r] for r in range(HALO - 1)]
    rows += [f_ref[16 * r : 16 * r + 16].astype(bf16) for r in range(ROWS)]
    return rows + [after_ref[r] for r in range(HALO - 1)] + blank


def pack_body(before_ref, z_ref, after_ref, f_ref, f_before_ref, f_after_ref, pack_ref, first_ref, last_ref):
    rows = jnp.concatenate(widened(before_ref, z_ref, after_ref), axis=1)
    forcing = jnp.concatenate(forcing_rows(f_ref, f_before_ref, f_after_ref), axis=1)
    packed = times(jnp.concatenate([rows, forcing], axis=0), pack_ref[...]).astype(bf16)
    first_ref[...] = packed[:, :LANES]
    last_ref[...] = packed[:, LANES:]


def edge_tile(g, rows, sides, spread_ref, own_ref):
    mine = [rows[r] for r in range(g, EXT, EDGES)]
    return times(jnp.concatenate(mine, axis=1), own_ref[: len(mine) * LANES, :]) + times(
        sides, spread_ref[:, g * LANES : (g + 1) * LANES]
    )


def around(idx, get):
    here = get(idx)
    if idx < EXT:
        north, south = get(idx + 1), get(idx - 1)
    else:
        north = get(idx + 1) if idx + 1 < TILES else pltpu.roll(get(EXT), LANES - SIDE, 1)
        south = get(idx - 1) if idx > EXT else pltpu.roll(get(TILES - 1), SIDE, 1)
    return here, pltpu.roll(here, LANES - 1, 1), pltpu.roll(here, 1, 1), north, south


def ocean_step(tiles, x, coef, mix_ref, cat_ref, store, force=None):
    levels = mix_ref.shape[0]
    first = iota((8, LANES), 0) == 0
    for lo in range(0, len(tiles), 4):
        some = tiles[lo : lo + 4]
        slot = (lo // 4) % 2
        for at in range(0, levels, 16):
            for i, idx in enumerate(some):
                here, east, west, north, south = around(idx, lambda j: x(j, at))
                stepped = (
                    coef(0, idx, at) * here
                    + (coef(1, idx, at) * east + coef(2, idx, at) * west)
                    + (coef(3, idx, at) * north + coef(4, idx, at) * south)
                )
                if force is not None and at == 0:
                    top = stepped[:8] + jnp.where(first, force(idx), 0.0)
                    stepped = jnp.concatenate([top, stepped[8:]], axis=0)
                upper, lower = halves(stepped)
                cols = slice(i * LANES, (i + 1) * LANES)
                cat_ref[slot, at : at + 16, cols] = upper
                cat_ref[slot, levels + at : levels + at + 16, cols] = upper
                cat_ref[slot, 2 * levels + at : 2 * levels + at + 16, cols] = lower
        mixed = times(mix_ref[...], cat_ref[slot, :, : len(some) * LANES])
        for i, idx in enumerate(some):
            store(idx, mixed[:, i * LANES : (i + 1) * LANES])


def step_tiles(n):
    return list(range(n + 1, EXT - 1 - n)), list(range(EXT, TILES))


def two_refs(main_ref, edge_ref):
    def get(idx, at):
        if idx < EXT:
            return main_ref[idx, at : at + 16, :]
        return edge_ref[idx - EXT, at : at + 16, :]

    return get


def two_coefs(main_ref, edge_ref):
    def get(s, idx, at):
        if idx < EXT:
            return main_ref[s, idx, at : at + 16, :]
        return edge_ref[s, idx - EXT, at : at + 16, :]

    return get


def coefficients(inner, base, of, wets, levels, near_ref, coef_ref):
    for idx in inner:
        here, *near = around(idx, lambda j: wets[j])
        for s in range(4):
            near_ref[s, idx - base] = here * near[s]

    def part(c, carry):
        at = pl.multiple_of(c * 16, 16)
        here_at = pl.ds(at, 16)
        for idx in inner:
            along = 0.5 * of(idx, pl.ds(2 * levels + at, 16))
            across = 0.5 * of(idx, pl.ds(3 * levels + at, 16))
            near = []
            for s in range(4):
                one = near_ref[s, idx - base]
                near.append(jnp.concatenate([one, one], axis=0))
            c_east = near[0] * (diffusion - along)
            c_west = near[1] * (diffusion + along)
            c_north = near[2] * (diffusion - across)
            c_south = near[3] * (diffusion + across)
            coef_ref[0, idx - base, here_at, :] = 1.0 - ((c_east + c_west) + (c_north + c_south))
            coef_ref[1, idx - base, here_at, :] = c_east
            coef_ref[2, idx - base, here_at, :] = c_west
            coef_ref[3, idx - base, here_at, :] = c_north
            coef_ref[4, idx - base, here_at, :] = c_south
        return carry

    lax.fori_loop(0, levels // 16, part, 0)


def rows_step_body(
    before_ref, z_ref, after_ref, x_ref, mix_ref,
    coef_ref, x1_ref, salt_ref, wet_ref, x0_ref, near_ref, cat_ref,
):
    levels = mix_ref.shape[0]

    def of(idx, at):
        if idx < HALO:
            return before_ref[idx, at, :].astype(f32)
        if idx < HALO + ROWS:
            return z_ref[idx - HALO, at, :].astype(f32)
        return after_ref[idx - HALO - ROWS, at, :].astype(f32)

    wets = [of(idx, pl.ds(4 * levels, 16))[:8] for idx in range(EXT)]
    for idx in range(EXT):
        wet_ref[idx] = wets[idx]
    inner = step_tiles(0)[0]
    coefficients(inner, 0, of, wets, levels, near_ref, coef_ref)
    for t, to_ref in enumerate((x0_ref, salt_ref)):
        for idx in range(EXT):
            if HALO <= idx < HALO + ROWS:
                to_ref[idx] = x_ref[t, pl.ds(idx - HALO, levels, stride=ROWS), :]
            else:
                to_ref[idx] = of(idx, pl.ds(t * levels, levels))

    def store(idx, value):
        x1_ref[idx] = value

    ocean_step(inner, two_refs(x0_ref, None), two_coefs(coef_ref, None), mix_ref, cat_ref, store)


def edges_step_body(
    before_ref, z_ref, after_ref, west_ref, east_ref, f_ref, f_before_ref, f_after_ref,
    mix_ref, spread_ref, own_ref,
    coef_ref, x1_ref, salt_ref, wet_ref, force_ref, x0_ref, near_ref, edge_ref, cat_ref,
):
    levels = mix_ref.shape[0]
    depth = z_ref.shape[1]
    rows = widened(before_ref, z_ref, after_ref)
    forcing = forcing_rows(f_ref, f_before_ref, f_after_ref)
    rows = [jnp.concatenate(pair, axis=0) for pair in zip(rows, forcing)]
    sides = jnp.concatenate([east_ref[...], west_ref[...]], axis=1)
    for g in range(EDGES):
        tile = edge_tile(g, rows, sides, spread_ref, own_ref)
        edge_ref[g] = tile[:depth].astype(bf16)
        force_ref[g] = tile[depth:]
        x0_ref[g] = tile[:levels]
        salt_ref[g] = tile[levels : 2 * levels]
        wet_ref[g] = tile[4 * levels : 4 * levels + 8]

    def of(idx, at):
        return edge_ref[idx - EXT, at, :].astype(f32)

    inner = step_tiles(0)[1]
    wets = {idx: wet_ref[idx - EXT] for idx in inner}
    coefficients(inner, EXT, of, wets, levels, near_ref, coef_ref)

    def store(idx, value):
        x1_ref[idx - EXT] = value

    ocean_step(inner, two_refs(None, x0_ref), two_coefs(None, coef_ref), mix_ref, cat_ref, store)


def remap_body(arrival_ref, in_ref, w_ref, u_ref, wet_ref, _, f_ref, up_ref, down_ref, u_out_ref):
    def pick(j):
        t = arrival_ref[0, j]
        at = pl.multiple_of((t >> 1) * 16, 16)
        window = in_ref[pl.ds(at, 16), :].astype(f32)
        return jnp.where((t & 1) == 1, window[8:], window[:8])

    left = iota((8, LANES), 1) < 64
    left_two = iota((16, LANES), 1) < 64
    for r in range(ROWS):
        sources = []
        for side in range(2):
            even, odd = [], []
            for pair in range(2):
                j = 4 * (2 * r + side) + 2 * pair
                one, two = pick(j), pick(j + 1)
                even.append(jnp.where(left, one, pltpu.roll(two, 64, 1)))
                odd.append(jnp.where(left, pltpu.roll(one, 64, 1), two))
            sources.append(jnp.concatenate(even, axis=1))
            sources.append(jnp.concatenate(odd, axis=1))
        sources = jnp.concatenate(sources, axis=0).astype(bf16)
        product = times_rows(sources, w_ref[r * LANES : (r + 1) * LANES, :])
        forcing = jnp.where(left_two, product[:16], product[16:])
        f_ref[16 * r : 16 * r + 16, :] = forcing
        if r < HALO - 1:
            down_ref[r] = forcing.astype(bf16)
        if r >= ROWS - HALO + 1:
            up_ref[r - (ROWS - HALO + 1)] = forcing.astype(bf16)
    whole = np.linalg.matrix_power(turn, STEPS)
    wet = wet_ref[...].astype(f32)
    push = [surface_push * f_ref[pl.ds(6 + 8 * v, ROWS, stride=16), :] for v in range(2)]
    for v in range(2):
        ahead = float(whole[v, 0]) * u_ref[0] + float(whole[v, 1]) * u_ref[1] + push[v]
        u_out_ref[v] = u_ref[v] + wet * (ahead - u_ref[v])


def returned_rows(fields, w_ref, place, rows):
    blocks = 2 * ROWS
    block, lane = iota((blocks, LANES), 0), iota((blocks, LANES), 1)
    spread = []
    for field in fields:
        parts = []
        for r in range(ROWS):
            mine = block == 2 * r + (lane >= 64).astype(jnp.int32)
            parts.append(jnp.where(mine, field[r : r + 1], 0.0))
        spread.append(jnp.concatenate(parts, axis=1))
    terms = times(jnp.concatenate(spread, axis=0).astype(bf16), w_ref[...])
    high_parts, low_parts, ones = [], [], []
    target = iota((rows, LANES), 0)
    for f in range(len(fields)):
        mine = terms[f * blocks : (f + 1) * blocks]
        pieces = []
        for half in range(2):
            for k in range(4):
                piece = mine[:, (k // 2) * LANES : (k // 2 + 1) * LANES]
                if k % 2 != half:
                    piece = pltpu.roll(piece, 64, 1)
                pieces.append(jnp.where((lane >= 64) == (half == 1), piece, 0.0))
        high, low = halves(jnp.concatenate(pieces, axis=0))
        high_parts.append(high)
        low_parts.append(low)
        ones.append(one_hot(target == place + f))
    return times(
        jnp.concatenate(ones + ones, axis=1), jnp.concatenate(high_parts + low_parts, axis=0)
    )


def tracer_body(t, *refs):
    x_ref, edge_x_ref, coef_ref, edge_coef_ref, wet_ref, edge_wet_ref = refs[:6]
    mix_ref, f_ref, before_ref, after_ref, edge_force_ref = refs[6:11]
    if t == 0:
        column_ref, w_ref, place_ref, u_ref, out_hbm, send_ref = refs[11:17]
        one_ref, two_ref, force_ref, cat_ref, out_ref, sem, sst_ref = refs[17:]
    else:
        _, out_hbm, one_ref, two_ref, force_ref, cat_ref, out_ref, sem = refs[11:]
    levels = mix_ref.shape[0]
    for idx in range(1, TILES):
        if idx == EXT - 1:
            continue
        if idx >= EXT:
            wet, forcing = edge_wet_ref[idx - EXT], edge_force_ref[idx - EXT]
        else:
            wet = wet_ref[idx]
            if idx < HALO:
                forcing = before_ref[idx - 1].astype(f32)
            elif idx < HALO + ROWS:
                forcing = f_ref[16 * (idx - HALO) : 16 * (idx - HALO) + 16, :]
            else:
                forcing = after_ref[idx - HALO - ROWS].astype(f32)
        force_ref[idx] = surface_gain[t] * wet * forcing[8 * t : 8 * t + 8]
    if t == 0:
        column = jnp.broadcast_to(column_ref[:, 0:1], (levels, LANES))
        for idx in range(1, TILES):
            if idx != EXT - 1:
                first = x_ref[idx] if idx < EXT else edge_x_ref[idx - EXT]
                one_ref[idx] = first + column * force_ref[idx, 0:1, :]
        old, new = one_ref, two_ref
    else:
        old, new = None, one_ref
    for n in range(1 if t == 0 else 0, STEPS):

        def store(idx, value, new=new):
            new[idx] = value

        def force(idx, n=n):
            return force_ref[idx, n : n + 1, :]

        if old is None:
            x = two_refs(x_ref, edge_x_ref)
        else:

            def x(idx, at, old=old):
                return old[idx, at : at + 16, :]

        main, edges = step_tiles(n)
        coef = two_coefs(coef_ref, edge_coef_ref)
        ocean_step(main + edges, x, coef, mix_ref, cat_ref, store, force)
        if t == 1 and n == 0:
            old, new = one_ref, two_ref
        else:
            old, new = new, old
    lane = iota((16, LANES), 1)
    for r in range(ROWS):
        idx = HALO + r
        at = SIDE * (idx // EDGES) + HALO
        edge = EXT + idx % EDGES
        for lo in range(0, levels, 16):
            side = old[edge, lo : lo + 16, :]
            value = jnp.where(
                lane < HALO, pltpu.roll(side, (LANES - at) % LANES, 1), old[idx, lo : lo + 16, :]
            )
            here = at + REACH + HALO
            value = jnp.where(
                lane >= LANES - HALO, pltpu.roll(side, (LANES - HALO - here) % LANES, 1), value
            )
            out_ref[pl.ds(lo * ROWS + r, 16, stride=ROWS), :] = value
            if t == 0 and lo == 0:
                sst_ref[r : r + 1, :] = value[0:1]
    copy = pltpu.make_async_copy(out_ref, out_hbm.at[t], sem)
    copy.start()
    if t == 0:
        fields = [sst_ref[...], u_ref[0], u_ref[1]]
        fields = [field.astype(bf16).astype(f32) for field in fields]
        send_ref[...] = returned_rows(fields, w_ref, place_ref[...], send_ref.shape[0])
    copy.wait()


def neighbours(size):
    up = [(i, i + 1) for i in range(size - 1)]
    return up, [(j, i) for i, j in up]


def on_device(
    atmosphere_level_state,
    atmosphere_mixing_map,
    sea_surface_temps,
    tracers,
    currents,
    ocean_advect_velocity,
    ocean_mixing_map,
    ocean_cell_mask,
    remap_weight_tiles,
    outgoing_block_table,
    arrival_slot_table,
):
    band = ("row", "col")
    peers = lax.axis_size(band)
    levels = tracers.shape[1]
    air_levels, air_columns = atmosphere_level_state.shape[1:]
    rows_axis = ("comp", "row")
    up, down = neighbours(lax.axis_size(rows_axis))
    right, leftward = neighbours(lax.axis_size("col"))
    pack_moves, spread_moves, own_moves = moves()

    table = outgoing_block_table.reshape(peers, 2).T
    arrival = arrival_slot_table.reshape(1, 64)
    by_k = arrival.reshape(2 * ROWS, 4).T.reshape(1, 64)
    place = jnp.concatenate(
        [jnp.where(by_k % 2 == side, (by_k // 2) * 4, -64) for side in range(2)], axis=1
    )

    payload, gained = call(
        flux_body,
        (shape((peers * 16, LANES), bf16), shape((4, 8, air_columns))),
        "fluxes",
        [SMEM, HBM, HBM, HBM],
        (VMEM, HBM),
        scratch=[
            pltpu.VMEM((64, LANES), f32),
            pltpu.VMEM((4, 8, air_columns), f32),
            pltpu.VMEM(atmosphere_level_state.shape, f32),
            pltpu.VMEM(atmosphere_mixing_map.shape, f32),
            pltpu.VMEM((1, air_columns), f32),
            pltpu.SemaphoreType.DMA((3,)),
            pltpu.SemaphoreType.DMA,
        ],
        limit=56,
        micros=3,
    )(table, atmosphere_level_state, atmosphere_mixing_map, sea_surface_temps[None])
    payload, wet_rows = lax.optimization_barrier((payload, ocean_cell_mask))
    arrived = lax.all_to_all(payload, band, 0, 0, tiled=True)

    flat = tracers.reshape(2, levels * ROWS, LANES)
    depth = 4 * levels + 16
    z = call(
        rows_body,
        shape((ROWS, depth, LANES), bf16),
        "rows",
        [VMEM] * 3,
        scratch=[pltpu.VMEM(flat.shape, f32)],
    )(flat, ocean_advect_velocity.reshape(flat.shape), wet_rows)
    before = lax.ppermute(z[ROWS - HALO :], rows_axis, up)
    after = lax.ppermute(z[:HALO], rows_axis, down)
    gained, wet_rows = lax.optimization_barrier((gained, wet_rows))
    atm_final, token = call(
        atmosphere_body,
        (shape(atmosphere_level_state.shape), shape((8, LANES))),
        "atmosphere",
        [VMEM] * 3,
        micros=3,
    )(atmosphere_level_state, gained, atmosphere_mixing_map)
    cells = call(
        cells_body,
        shape((ROWS * LANES, WIDE), bf16),
        "cells",
        [VMEM],
        scratch=[
            pltpu.VMEM((32 * 64, LANES), f32),
            pltpu.VMEM((ROWS * LANES, LANES), f32),
            pltpu.VMEM((ROWS * LANES, LANES), f32),
        ],
    )(remap_weight_tiles.reshape(64, 4096))
    rounded = lax.reduce_precision(ocean_mixing_map, 8, 7)
    upper, lower = rounded.astype(bf16), (ocean_mixing_map - rounded).astype(bf16)
    mix = jnp.concatenate([upper, lower, upper], axis=1)
    cat = pltpu.VMEM((2, 3 * levels, 4 * LANES), bf16)

    edge_rows = shape((HALO - 1, 16, LANES), bf16)
    forcing, send_up, send_down, ocean_currents = call(
        remap_body,
        (shape((ROWS * 16, LANES)), edge_rows, edge_rows, shape(currents.shape)),
        "remap",
        [SMEM] + [VMEM] * 4 + [HBM],
    )(arrival, arrived, cells, currents, ocean_cell_mask, token)
    f_before = lax.ppermute(send_up, rows_axis, up)
    f_after = lax.ppermute(send_down, rows_axis, down)
    strip = shape((depth + 16, LANES), bf16)
    first, last = call(pack_body, (strip, strip), "pack", [VMEM] * 7)(
        before, z, after, forcing, f_before, f_after, pack_moves
    )
    first, last, mix = lax.optimization_barrier((first, last, mix))
    east_in = lax.ppermute(first, "col", leftward)
    west_in = lax.ppermute(last, "col", right)
    main, side = (EXT, levels, LANES), (EDGES, levels, LANES)
    coef, x1, salt, wet = call(
        rows_step_body,
        (shape((5, *main)), shape(main), shape(main), shape((EXT, 8, LANES))),
        "rows_step",
        [VMEM] * 5,
        scratch=[pltpu.VMEM(main, f32), pltpu.VMEM((4, EXT, 8, LANES), f32), cat],
        limit=24,
        micros=2,
    )(before, z, after, flat, mix)
    side_coef, side_x1, side_salt, side_wet, side_force = call(
        edges_step_body,
        (
            shape((5, *side)),
            shape(side),
            shape(side),
            shape((EDGES, 8, LANES)),
            shape((EDGES, 16, LANES)),
        ),
        "edges_step",
        [VMEM] * 11,
        scratch=[
            pltpu.VMEM(side, f32),
            pltpu.VMEM((4, EDGES, 8, LANES), f32),
            pltpu.VMEM((EDGES, depth, LANES), bf16),
            cat,
        ],
        limit=16,
        micros=1,
    )(
        before, z, after, west_in, east_in, forcing, f_before, f_after,
        mix, spread_moves, own_moves,
    )

    shared = (coef, side_coef, wet, side_wet, mix, forcing, f_before, f_after, side_force)
    wide = (TILES, levels, LANES)
    scratch = [
        pltpu.VMEM(wide, f32),
        pltpu.VMEM(wide, f32),
        pltpu.VMEM((TILES, 8, LANES), f32),
        cat,
        pltpu.VMEM(flat.shape[1:], f32),
        pltpu.SemaphoreType.DMA,
    ]
    warm, terms = call(
        functools.partial(tracer_body, 0),
        (shape(flat.shape), shape((peers * 4, LANES))),
        "temperature",
        [VMEM] * 15,
        (HBM, VMEM),
        scratch=scratch + [pltpu.VMEM((ROWS, LANES), f32)],
        limit=24,
        micros=6,
    )(x1, side_x1, *shared, ocean_mixing_map, cells, place, ocean_currents)
    home = lax.all_to_all(terms, band, 0, 0, tiled=True)
    both = call(
        functools.partial(tracer_body, 1),
        shape(flat.shape),
        "salinity",
        [VMEM] * 11 + [HBM],
        HBM,
        scratch=scratch,
        aliases={11: 0},
        limit=24,
        micros=6,
    )(salt, side_salt, *shared, warm)
    returned = call(finish_body, shape((3, air_columns)), "finish", [VMEM, VMEM])(
        jnp.repeat(table, 4, axis=1), home
    )
    return (atm_final, both.reshape(tracers.shape), ocean_currents, returned)


def solution(mesh):
    return jax.shard_map(
        on_device,
        mesh=mesh,
        in_specs=(
            P(None, None, ("comp", "row", "col")),
            P(),
            P(("comp", "row", "col")),
            P(None, None, ("comp", "row"), "col"),
            P(None, ("comp", "row"), "col"),
            P(None, None, ("comp", "row"), "col"),
            P(),
            P(("comp", "row"), "col"),
            P("comp", ("row", "col"), None, None),
            P("comp", ("row", "col"), None, None),
            P("comp", ("row", "col"), None),
        ),
        out_specs=(
            P(None, None, ("comp", "row", "col")),
            P(None, None, ("comp", "row"), "col"),
            P(None, ("comp", "row"), "col"),
            P(None, ("comp", "row", "col")),
        ),
        check_vma=False,
    )
```

```python
import functools

import jax
import jax.numpy as jnp
import numpy as np
from jax import lax
from jax.experimental import pallas as pl
from jax.experimental.pallas import tpu as pltpu
from jax.sharding import PartitionSpec as P

STEPS = 6
HALO = 6
ROWS = 8
EXT = ROWS + 2 * HALO
REACH = 2 * HALO
GROUP = 3
EDGES = -(-EXT // GROUP)
TILES = EXT + EDGES
SIDE = 2 * (HALO + REACH)
LANES = 128
WIDE = 256
HIGHEST = lax.Precision.HIGHEST
MIB = 1024 * 1024

heat_rate = 0.5
vapour_rate = 0.5
drag_rate = 0.3
saturation = 0.6
flux_gains = (0.3, 0.3, -0.3, -0.3)
diffusion = 0.15
surface_gain = (-0.3, 0.3)
surface_push = 0.3
current_drag = 0.1
coriolis = 0.2
turn = np.array([[1.0 - current_drag, coriolis], [-coriolis, 1.0 - current_drag]])

f32 = jnp.float32
bf16 = jnp.bfloat16
VMEM = pl.BlockSpec(memory_space=pltpu.VMEM)
HBM = pl.BlockSpec(memory_space=pltpu.HBM)
SMEM = pl.BlockSpec(memory_space=pltpu.SMEM)


def call(body, out_shape, name, in_specs, out_specs=None, scratch=(), aliases=None, limit=8, micros=1):
    if out_specs is None:
        out_specs = jax.tree.map(lambda _: VMEM, out_shape)
    return pl.pallas_call(
        body,
        out_shape=out_shape,
        in_specs=in_specs,
        out_specs=out_specs,
        scratch_shapes=list(scratch),
        input_output_aliases=aliases or {},
        compiler_params=pltpu.CompilerParams(vmem_limit_bytes=limit * MIB),
        cost_estimate=pl.CostEstimate(
            flops=int(micros * 1e9), bytes_accessed=int(micros * 3e6), transcendentals=0
        ),
        name=name,
    )


def shape(dims, dtype=f32):
    return jax.ShapeDtypeStruct(dims, dtype)


def exact(a, b):
    return jnp.dot(a, b, precision=HIGHEST, preferred_element_type=f32)


def times(a, b):
    return jnp.dot(a, b, preferred_element_type=f32)


def times_rows(a, b):
    return lax.dot_general(a, b, (((1,), (1,)), ((), ())), preferred_element_type=f32)


def iota(dims, axis):
    return lax.broadcasted_iota(jnp.int32, dims, axis)


def one_hot(condition):
    return condition.astype(f32).astype(bf16)


def halves(x):
    high = x.astype(bf16)
    return high, (x - high.astype(f32)).astype(bf16)


def moves():
    spread = np.zeros((2, LANES, EDGES, LANES), np.float32)
    own = np.zeros((GROUP, LANES, LANES), np.float32)
    for r in range(EXT):
        at = SIDE * (r // EDGES)
        for c in range(HALO):
            spread[0, HALO * r + c, r % EDGES, at + SIDE - HALO + c] = 1
            spread[1, HALO * r + c, r % EDGES, at + c] = 1
    for k in range(GROUP):
        for c in range(REACH):
            own[k, c, SIDE * k + HALO + c] = 1
            own[k, LANES - REACH + c, SIDE * k + HALO + REACH + c] = 1
    return (
        jnp.asarray(spread.reshape(2 * LANES, EDGES * LANES), bf16),
        jnp.asarray(own.reshape(GROUP * LANES, LANES), bf16),
    )


def mixing_powers(m_ref):
    power = {1: m_ref[...]}
    power[2] = exact(power[1], power[1])
    power[3] = exact(power[1], power[2])
    power[4] = exact(power[2], power[2])
    power[5] = exact(power[2], power[3])
    power[6] = exact(power[3], power[3])
    return power


def flux_body(
    table_ref, a_hbm, m_hbm, sst_hbm, pay_ref, g_hbm, block_ref, g_ref, a_ref, m_ref, sst_ref, sems, sem
):
    loads = [
        pltpu.make_async_copy(m_hbm, m_ref, sems.at[0]),
        pltpu.make_async_copy(sst_hbm, sst_ref, sems.at[1]),
        pltpu.make_async_copy(a_hbm, a_ref, sems.at[2]),
    ]
    for load in loads:
        load.start()
    loads[0].wait()
    levels = m_ref.shape[0]
    bottom = levels - 1
    power = mixing_powers(m_ref)
    first = (iota((1, levels), 1) == bottom).astype(f32)
    rows = [first] + [power[n][bottom:, :] for n in range(1, STEPS)]
    rows = jnp.concatenate(rows + [jnp.zeros((8 - STEPS, levels), f32)], axis=0)
    row_high, row_low = halves(rows)
    both = jnp.concatenate([row_high.astype(f32), row_low.astype(f32)], axis=0).astype(bf16)
    loads[1].wait()
    loads[2].wait()
    base = []
    for v in range(4):
        high, low = halves(a_ref[v])
        one = times(both, high)
        base.append(one[:8] + one[8:] + times(row_high, low))
    corner = {n: power[n][bottom:, bottom:] for n in range(1, STEPS)}
    sst = sst_ref[...]
    gained = []
    fluxes = []
    east, north = jnp.zeros_like(sst), jnp.zeros_like(sst)
    for n in range(STEPS):
        now = []
        for v in range(4):
            value = base[v][n : n + 1]
            for k in range(n):
                value = value + corner[n - k] * gained[k][v]
            now.append(value)
        wind = jnp.sqrt(now[2] * now[2] + now[3] * now[3] + 1.0)
        flux = (
            heat_rate * wind * (sst - now[0]),
            vapour_rate * wind * (saturation * sst - now[1]),
            drag_rate * wind * now[2],
            drag_rate * wind * now[3],
        )
        fluxes.append(flux)
        gained.append([flux_gains[v] * flux[v] for v in range(4)])
        east, north = (
            turn[0, 0] * east + turn[0, 1] * north + flux[2],
            turn[1, 0] * east + turn[1, 1] * north + flux[3],
        )
    blank = [jnp.zeros_like(sst)] * (8 - STEPS)
    for v in range(4):
        g_ref[v] = jnp.concatenate([gained[n][v] for n in range(STEPS)] + blank, axis=0)
    copy = pltpu.make_async_copy(g_ref, g_hbm, sem)
    copy.start()
    pairs = [(fluxes[n][0], fluxes[n][1]) for n in range(STEPS)] + [(east, north)]
    block = iota((8, LANES), 0)
    left = iota((8, LANES), 1) < 64
    even = block % 2 == 0
    for i, pair in enumerate(pairs):
        parts = []
        for side in range(2):
            spread = jnp.zeros((8, LANES), f32)
            for q in range(4):
                tile = jnp.broadcast_to(pair[side][:, q * LANES : (q + 1) * LANES], (8, LANES))
                spread = jnp.where(block // 2 == q, tile, spread)
            parts.append(jnp.where(even == (side == 0), spread, pltpu.roll(spread, 64, 1)))
        block_ref[pl.ds(i, 8, stride=8), :] = jnp.where(left, parts[0], parts[1])
    block_ref[pl.ds(7, 8, stride=8), :] = jnp.zeros((8, LANES), f32)
    for d in range(pay_ref.shape[0] // 16):
        chosen = []
        for side in range(2):
            at = jnp.maximum(table_ref[side, d], 0) * 8
            chosen.append(block_ref[pl.ds(pl.multiple_of(at, 8), 8), :])
        pay_ref[16 * d : 16 * d + 16, :] = jnp.concatenate(chosen, axis=0).astype(bf16)
    copy.wait()


def atmosphere_body(a_ref, g_ref, m_ref, out_ref, token_ref):
    token_ref[...] = jnp.zeros_like(token_ref)
    levels = m_ref.shape[0]
    power = mixing_powers(m_ref)
    lane = iota((levels, 8), 1)
    edge = jnp.zeros((levels, 8), f32)
    for n in range(STEPS):
        edge = jnp.where(lane == n, power[STEPS - n][:, levels - 1 :], edge)
    for v in range(4):
        out_ref[v] = exact(power[STEPS], a_ref[v]) + exact(edge, g_ref[v])


def finish_body(table_ref, in_ref, out_ref):
    rows = in_ref.shape[0]
    block, lane = iota((8, rows), 0), iota((8, rows), 1)
    ones = []
    for side in range(2):
        named = table_ref[side : side + 1, :] == block
        for f in range(3):
            ones.append((named & (lane % 4 == f)).astype(f32))
    ones = jnp.concatenate(ones, axis=0).astype(bf16)
    high, low = halves(in_ref[...])
    sums = times(ones, high) + times(ones, low)
    left = iota((1, LANES), 1) < 64
    for f in range(3):
        low = sums[8 * f : 8 * f + 8] + pltpu.roll(sums[24 + 8 * f : 32 + 8 * f], 64, 1)
        high = pltpu.roll(low, 64, 1)
        for q in range(4):
            out_ref[f : f + 1, q * LANES : (q + 1) * LANES] = jnp.where(
                left, low[2 * q : 2 * q + 1], high[2 * q + 1 : 2 * q + 2]
            )


def cells_body(w_ref, out_ref, t_ref, low_ref, high_ref):
    left = iota((16, LANES), 1) < 64
    tiles = w_ref.shape[1] // LANES
    for i in range(tiles):
        t_ref[i * 64 : (i + 1) * 64] = w_ref[:, i * LANES : (i + 1) * LANES].astype(f32)
    for i in range(tiles):
        k = [t_ref[pl.ds(i * 64 + s, 16, stride=4), :] for s in range(4)]
        moved = [pltpu.roll(x, 64, 1) for x in k]
        low_ref[pl.ds(2 * i, 16, stride=64), :] = jnp.where(left, k[0], moved[1])
        high_ref[pl.ds(2 * i, 16, stride=64), :] = jnp.where(left, k[2], moved[3])
        low_ref[pl.ds(2 * i + 1, 16, stride=64), :] = jnp.where(left, moved[0], k[1])
        high_ref[pl.ds(2 * i + 1, 16, stride=64), :] = jnp.where(left, moved[2], k[3])
    out_ref[:, :LANES] = low_ref[...].astype(bf16)
    out_ref[:, LANES:] = high_ref[...].astype(bf16)


def rows_body(x_ref, v_ref, wet_ref, z_ref, f_ref):
    levels = x_ref.shape[1] // ROWS
    for t in range(2):
        f_ref[t] = v_ref[t].astype(f32)
    for r in range(ROWS):
        for t in range(2):
            z_ref[r, (2 + t) * levels : (3 + t) * levels, :] = f_ref[
                t, pl.ds(r, levels, stride=ROWS), :
            ].astype(bf16)
        wet = jnp.broadcast_to(wet_ref[r : r + 1, :].astype(f32), (16, LANES))
        z_ref[r, 4 * levels :, :] = wet.astype(bf16)
    for r in range(ROWS):
        for t in range(2):
            z_ref[r, t * levels : (t + 1) * levels, :] = x_ref[
                t, pl.ds(r, levels, stride=ROWS), :
            ].astype(bf16)


def widened(before_ref, own_ref, after_ref):
    rows = [before_ref[r] for r in range(HALO)]
    rows += [own_ref[r] for r in range(ROWS)]
    return rows + [after_ref[r] for r in range(HALO)]


def forcing_rows(f_ref, before_ref, after_ref):
    blank = [jnp.zeros((16, LANES), bf16)]
    rows = blank + [before_ref[r] for r in range(HALO - 1)]
    rows += [f_ref[16 * r : 16 * r + 16].astype(bf16) for r in range(ROWS)]
    return rows + [after_ref[r] for r in range(HALO - 1)] + blank


def pack_matrix():
    row, lane = iota((LANES, LANES), 0), iota((LANES, LANES), 1)
    first = jnp.where(row < HALO, lane - row, -LANES)
    last = jnp.where(row >= LANES - HALO, lane - row + LANES - HALO, -LANES)
    both = [
        jnp.concatenate([one_hot(first == HALO * r), one_hot(last == HALO * r)], axis=1)
        for r in range(EXT)
    ]
    return jnp.concatenate(both, axis=0)


def pack_body(
    odd_ref, before_ref, z_ref, after_ref, f_ref, one_ref, two_ref,
    send_one_ref, send_two_ref, f_before_ref, f_after_ref,
):
    odd_row, odd_col = odd_ref[0, 0] == 1, odd_ref[0, 1] == 1
    for i in range(HALO - 1):
        one, two = one_ref[i].astype(f32), two_ref[i].astype(f32)
        f_before_ref[i] = jnp.where(odd_row, two, one).astype(bf16)
        f_after_ref[i] = jnp.where(odd_row, one, two).astype(bf16)
    rows = jnp.concatenate(widened(before_ref, z_ref, after_ref), axis=1)
    forcing = jnp.concatenate(forcing_rows(f_ref, f_before_ref, f_after_ref), axis=1)
    packed = times(jnp.concatenate([rows, forcing], axis=0), pack_matrix())
    first, last = packed[:, :LANES], packed[:, LANES:]
    send_one_ref[...] = jnp.where(odd_col, last, first).astype(bf16)
    send_two_ref[...] = jnp.where(odd_col, first, last).astype(bf16)


def edge_tile(g, rows, sides, spread_ref, own_ref):
    mine = [rows[r] for r in range(g, EXT, EDGES)]
    return times(jnp.concatenate(mine, axis=1), own_ref[: len(mine) * LANES, :]) + times(
        sides, spread_ref[:, g * LANES : (g + 1) * LANES]
    )


def around(idx, get):
    here = get(idx)
    if idx < EXT:
        north, south = get(idx + 1), get(idx - 1)
    else:
        north = get(idx + 1) if idx + 1 < TILES else pltpu.roll(get(EXT), LANES - SIDE, 1)
        south = get(idx - 1) if idx > EXT else pltpu.roll(get(TILES - 1), SIDE, 1)
    return here, pltpu.roll(here, LANES - 1, 1), pltpu.roll(here, 1, 1), north, south


def ocean_step(tiles, x, coef, mix_ref, cat_ref, store, force=None):
    levels = mix_ref.shape[0]
    first = iota((8, LANES), 0) == 0
    for lo in range(0, len(tiles), 4):
        some = tiles[lo : lo + 4]
        slot = (lo // 4) % 2
        for at in range(0, levels, 16):
            for i, idx in enumerate(some):
                here, east, west, north, south = around(idx, lambda j: x(j, at))
                stepped = (
                    coef(0, idx, at) * here
                    + (coef(1, idx, at) * east + coef(2, idx, at) * west)
                    + (coef(3, idx, at) * north + coef(4, idx, at) * south)
                )
                if force is not None and at == 0:
                    top = stepped[:8] + jnp.where(first, force(idx), 0.0)
                    stepped = jnp.concatenate([top, stepped[8:]], axis=0)
                upper, lower = halves(stepped)
                cols = slice(i * LANES, (i + 1) * LANES)
                cat_ref[slot, at : at + 16, cols] = upper
                cat_ref[slot, levels + at : levels + at + 16, cols] = upper
                cat_ref[slot, 2 * levels + at : 2 * levels + at + 16, cols] = lower
        mixed = times(mix_ref[...], cat_ref[slot, :, : len(some) * LANES])
        for i, idx in enumerate(some):
            store(idx, mixed[:, i * LANES : (i + 1) * LANES])


def step_tiles(n):
    return list(range(n + 1, EXT - 1 - n)), list(range(EXT, TILES))


def two_refs(main_ref, edge_ref):
    def get(idx, at):
        if idx < EXT:
            return main_ref[idx, at : at + 16, :]
        return edge_ref[idx - EXT, at : at + 16, :]

    return get


def two_coefs(main_ref, edge_ref):
    def get(s, idx, at):
        if idx < EXT:
            return main_ref[s, idx, at : at + 16, :]
        return edge_ref[s, idx - EXT, at : at + 16, :]

    return get


def coefficients(inner, base, of, wets, levels, near_ref, coef_ref):
    for idx in inner:
        here, *near = around(idx, lambda j: wets[j])
        for s in range(4):
            near_ref[s, idx - base] = here * near[s]

    def part(c, carry):
        at = pl.multiple_of(c * 16, 16)
        here_at = pl.ds(at, 16)
        for idx in inner:
            along = 0.5 * of(idx, pl.ds(2 * levels + at, 16))
            across = 0.5 * of(idx, pl.ds(3 * levels + at, 16))
            near = []
            for s in range(4):
                one = near_ref[s, idx - base]
                near.append(jnp.concatenate([one, one], axis=0))
            c_east = near[0] * (diffusion - along)
            c_west = near[1] * (diffusion + along)
            c_north = near[2] * (diffusion - across)
            c_south = near[3] * (diffusion + across)
            coef_ref[0, idx - base, here_at, :] = 1.0 - ((c_east + c_west) + (c_north + c_south))
            coef_ref[1, idx - base, here_at, :] = c_east
            coef_ref[2, idx - base, here_at, :] = c_west
            coef_ref[3, idx - base, here_at, :] = c_north
            coef_ref[4, idx - base, here_at, :] = c_south
        return carry

    lax.fori_loop(0, levels // 16, part, 0)


def rows_step_body(
    before_ref, z_ref, after_ref, x_ref, mix_ref,
    coef_ref, x1_ref, wet_ref, coef_hbm, salt_hbm, x0_ref, near_ref, cat_ref, salt_ref, sems,
):
    levels = mix_ref.shape[0]

    def of(idx, at):
        if idx < HALO:
            return before_ref[idx, at, :].astype(f32)
        if idx < HALO + ROWS:
            return z_ref[idx - HALO, at, :].astype(f32)
        return after_ref[idx - HALO - ROWS, at, :].astype(f32)

    wets = [of(idx, pl.ds(4 * levels, 16))[:8] for idx in range(EXT)]
    for idx in range(EXT):
        wet_ref[idx] = wets[idx]
    inner = step_tiles(0)[0]
    coefficients(inner, 0, of, wets, levels, near_ref, coef_ref)
    stores = [
        pltpu.make_async_copy(coef_ref, coef_hbm, sems.at[0]),
        pltpu.make_async_copy(salt_ref, salt_hbm, sems.at[1]),
    ]
    stores[0].start()
    for t, to_ref in enumerate((x0_ref, salt_ref)):
        for idx in range(EXT):
            if HALO <= idx < HALO + ROWS:
                to_ref[idx] = x_ref[t, pl.ds(idx - HALO, levels, stride=ROWS), :]
            else:
                to_ref[idx] = of(idx, pl.ds(t * levels, levels))
    stores[1].start()

    def store(idx, value):
        x1_ref[idx] = value

    ocean_step(inner, two_refs(x0_ref, None), two_coefs(coef_ref, None), mix_ref, cat_ref, store)
    for copy in stores:
        copy.wait()


def edges_step_body(
    odd_ref, before_ref, z_ref, after_ref, one_ref, two_ref, f_ref, f_before_ref, f_after_ref,
    mix_ref, spread_ref, own_ref,
    coef_ref, x1_ref, salt_ref, wet_ref, force_ref, x0_ref, near_ref, edge_ref, cat_ref,
):
    levels = mix_ref.shape[0]
    depth = z_ref.shape[1]
    rows = widened(before_ref, z_ref, after_ref)
    forcing = forcing_rows(f_ref, f_before_ref, f_after_ref)
    rows = [jnp.concatenate(pair, axis=0) for pair in zip(rows, forcing)]
    odd = odd_ref[0, 1] == 1
    one, two = one_ref[...].astype(f32), two_ref[...].astype(f32)
    sides = jnp.concatenate([jnp.where(odd, one, two), jnp.where(odd, two, one)], axis=1)
    sides = sides.astype(bf16)
    for g in range(EDGES):
        tile = edge_tile(g, rows, sides, spread_ref, own_ref)
        edge_ref[g] = tile[:depth].astype(bf16)
        force_ref[g] = tile[depth:]
        x0_ref[g] = tile[:levels]
        salt_ref[g] = tile[levels : 2 * levels]
        wet_ref[g] = tile[4 * levels : 4 * levels + 8]

    def of(idx, at):
        return edge_ref[idx - EXT, at, :].astype(f32)

    inner = step_tiles(0)[1]
    wets = {idx: wet_ref[idx - EXT] for idx in inner}
    coefficients(inner, EXT, of, wets, levels, near_ref, coef_ref)

    def store(idx, value):
        x1_ref[idx - EXT] = value

    ocean_step(inner, two_refs(None, x0_ref), two_coefs(None, coef_ref), mix_ref, cat_ref, store)


def remap_body(arrival_ref, odd_ref, in_ref, w_ref, u_ref, wet_ref, _, f_ref, one_ref, two_ref, u_out_ref):
    def pick(j):
        t = arrival_ref[0, j]
        at = pl.multiple_of((t >> 1) * 16, 16)
        window = in_ref[pl.ds(at, 16), :].astype(f32)
        return jnp.where((t & 1) == 1, window[8:], window[:8])

    left = iota((8, LANES), 1) < 64
    left_two = iota((16, LANES), 1) < 64
    for r in range(ROWS):
        sources = []
        for side in range(2):
            even, odd = [], []
            for pair in range(2):
                j = 4 * (2 * r + side) + 2 * pair
                one, two = pick(j), pick(j + 1)
                even.append(jnp.where(left, one, pltpu.roll(two, 64, 1)))
                odd.append(jnp.where(left, pltpu.roll(one, 64, 1), two))
            sources.append(jnp.concatenate(even, axis=1))
            sources.append(jnp.concatenate(odd, axis=1))
        sources = jnp.concatenate(sources, axis=0).astype(bf16)
        product = times_rows(sources, w_ref[r * LANES : (r + 1) * LANES, :])
        forcing = jnp.where(left_two, product[:16], product[16:])
        f_ref[16 * r : 16 * r + 16, :] = forcing
    odd = odd_ref[0, 0] == 1
    for i in range(HALO - 1):
        up = f_ref[16 * (ROWS - HALO + 1 + i) : 16 * (ROWS - HALO + 2 + i), :]
        down = f_ref[16 * i : 16 * i + 16, :]
        one_ref[i] = jnp.where(odd, up, down).astype(bf16)
        two_ref[i] = jnp.where(odd, down, up).astype(bf16)
    whole = np.linalg.matrix_power(turn, STEPS)
    wet = wet_ref[...].astype(f32)
    push = [surface_push * f_ref[pl.ds(6 + 8 * v, ROWS, stride=16), :] for v in range(2)]
    for v in range(2):
        ahead = float(whole[v, 0]) * u_ref[0] + float(whole[v, 1]) * u_ref[1] + push[v]
        u_out_ref[v] = u_ref[v] + wet * (ahead - u_ref[v])


def returned_rows(fields, w_ref, place, rows):
    blocks = 2 * ROWS
    block, lane = iota((blocks, LANES), 0), iota((blocks, LANES), 1)
    spread = []
    for field in fields:
        parts = []
        for r in range(ROWS):
            mine = block == 2 * r + (lane >= 64).astype(jnp.int32)
            parts.append(jnp.where(mine, field[r : r + 1], 0.0))
        spread.append(jnp.concatenate(parts, axis=1))
    terms = times(jnp.concatenate(spread, axis=0).astype(bf16), w_ref[...])
    high_parts, low_parts, ones = [], [], []
    target = iota((rows, LANES), 0)
    for f in range(len(fields)):
        mine = terms[f * blocks : (f + 1) * blocks]
        pieces = []
        for half in range(2):
            for k in range(4):
                piece = mine[:, (k // 2) * LANES : (k // 2 + 1) * LANES]
                if k % 2 != half:
                    piece = pltpu.roll(piece, 64, 1)
                pieces.append(jnp.where((lane >= 64) == (half == 1), piece, 0.0))
        high, low = halves(jnp.concatenate(pieces, axis=0))
        high_parts.append(high)
        low_parts.append(low)
        ones.append(one_hot(target == place + f))
    return times(
        jnp.concatenate(ones + ones, axis=1), jnp.concatenate(high_parts + low_parts, axis=0)
    )


def tracer_body(t, *refs):
    x_ref, edge_x_ref, coef_ref, edge_coef_ref, wet_ref, edge_wet_ref = refs[:6]
    mix_ref, f_ref, before_ref, after_ref, edge_force_ref = refs[6:11]
    if t == 0:
        column_ref, w_ref, place_ref, u_ref, out_hbm, send_ref = refs[11:17]
        one_ref, two_ref, force_ref, cat_ref, out_ref, sem, sst_ref = refs[17:]
    else:
        _, out_hbm, one_ref, two_ref, force_ref, cat_ref, out_ref, sem = refs[11:19]
        x_hbm, coef_hbm = x_ref, coef_ref
        x_ref, coef_ref, sems = refs[19:]
        loads = [
            pltpu.make_async_copy(x_hbm, x_ref, sems.at[0]),
            pltpu.make_async_copy(coef_hbm, coef_ref, sems.at[1]),
        ]
        for copy in loads:
            copy.start()
    levels = mix_ref.shape[0]
    for idx in range(1, TILES):
        if idx == EXT - 1:
            continue
        if idx >= EXT:
            wet, forcing = edge_wet_ref[idx - EXT], edge_force_ref[idx - EXT]
        else:
            wet = wet_ref[idx]
            if idx < HALO:
                forcing = before_ref[idx - 1].astype(f32)
            elif idx < HALO + ROWS:
                forcing = f_ref[16 * (idx - HALO) : 16 * (idx - HALO) + 16, :]
            else:
                forcing = after_ref[idx - HALO - ROWS].astype(f32)
        force_ref[idx] = surface_gain[t] * wet * forcing[8 * t : 8 * t + 8]
    if t == 0:
        column = jnp.broadcast_to(column_ref[:, 0:1], (levels, LANES))
        for idx in range(1, TILES):
            if idx != EXT - 1:
                first = x_ref[idx] if idx < EXT else edge_x_ref[idx - EXT]
                one_ref[idx] = first + column * force_ref[idx, 0:1, :]
        old, new = one_ref, two_ref
    else:
        for copy in loads:
            copy.wait()
        old, new = None, one_ref
    for n in range(1 if t == 0 else 0, STEPS):

        def store(idx, value, new=new):
            new[idx] = value

        def force(idx, n=n):
            return force_ref[idx, n : n + 1, :]

        if old is None:
            x = two_refs(x_ref, edge_x_ref)
        else:

            def x(idx, at, old=old):
                return old[idx, at : at + 16, :]

        main, edges = step_tiles(n)
        coef = two_coefs(coef_ref, edge_coef_ref)
        ocean_step(main + edges, x, coef, mix_ref, cat_ref, store, force)
        if t == 1 and n == 0:
            old, new = one_ref, two_ref
        else:
            old, new = new, old
    lane = iota((16, LANES), 1)
    for r in range(ROWS):
        idx = HALO + r
        at = SIDE * (idx // EDGES) + HALO
        edge = EXT + idx % EDGES
        for lo in range(0, levels, 16):
            side = old[edge, lo : lo + 16, :]
            value = jnp.where(
                lane < HALO, pltpu.roll(side, (LANES - at) % LANES, 1), old[idx, lo : lo + 16, :]
            )
            here = at + REACH + HALO
            value = jnp.where(
                lane >= LANES - HALO, pltpu.roll(side, (LANES - HALO - here) % LANES, 1), value
            )
            out_ref[pl.ds(lo * ROWS + r, 16, stride=ROWS), :] = value
            if t == 0 and lo == 0:
                sst_ref[r : r + 1, :] = value[0:1]
    copy = pltpu.make_async_copy(out_ref, out_hbm.at[t], sem)
    copy.start()
    if t == 0:
        fields = [sst_ref[...], u_ref[0], u_ref[1]]
        fields = [field.astype(bf16).astype(f32) for field in fields]
        send_ref[...] = returned_rows(fields, w_ref, place_ref[...], send_ref.shape[0])
    copy.wait()


def swaps(size):
    rounds = []
    for start in (1, 0):
        pairs = [(i, i + 1) for i in range(start, size - 1, 2)]
        rounds.append(pairs + [(j, i) for i, j in pairs])
    return rounds


def neighbours(size):
    up = [(i, i + 1) for i in range(size - 1)]
    return up, [(j, i) for i, j in up]


def on_device(
    atmosphere_level_state,
    atmosphere_mixing_map,
    sea_surface_temps,
    tracers,
    currents,
    ocean_advect_velocity,
    ocean_mixing_map,
    ocean_cell_mask,
    remap_weight_tiles,
    outgoing_block_table,
    arrival_slot_table,
):
    band = ("row", "col")
    peers = lax.axis_size(band)
    levels = tracers.shape[1]
    air_levels, air_columns = atmosphere_level_state.shape[1:]
    rows_axis = ("comp", "row")
    up, down = neighbours(lax.axis_size(rows_axis))
    row_rounds = swaps(lax.axis_size(rows_axis))
    col_rounds = swaps(lax.axis_size("col"))
    odd = jnp.stack([lax.axis_index(rows_axis) % 2, lax.axis_index("col") % 2])
    odd = odd.astype(jnp.int32).reshape(1, 2)
    spread_moves, own_moves = moves()

    table = outgoing_block_table.reshape(peers, 2).T
    arrival = arrival_slot_table.reshape(1, 64)
    by_k = arrival.reshape(2 * ROWS, 4).T.reshape(1, 64)
    place = jnp.concatenate(
        [jnp.where(by_k % 2 == side, (by_k // 2) * 4, -64) for side in range(2)], axis=1
    )

    payload, gained = call(
        flux_body,
        (shape((peers * 16, LANES), bf16), shape((4, 8, air_columns))),
        "fluxes",
        [SMEM, HBM, HBM, HBM],
        (VMEM, HBM),
        scratch=[
            pltpu.VMEM((64, LANES), f32),
            pltpu.VMEM((4, 8, air_columns), f32),
            pltpu.VMEM(atmosphere_level_state.shape, f32),
            pltpu.VMEM(atmosphere_mixing_map.shape, f32),
            pltpu.VMEM((1, air_columns), f32),
            pltpu.SemaphoreType.DMA((3,)),
            pltpu.SemaphoreType.DMA,
        ],
        limit=56,
        micros=3,
    )(table, atmosphere_level_state, atmosphere_mixing_map, sea_surface_temps[None])
    payload, wet_rows = lax.optimization_barrier((payload, ocean_cell_mask))
    arrived = lax.all_to_all(payload, band, 0, 0, tiled=True)

    flat = tracers.reshape(2, levels * ROWS, LANES)
    depth = 4 * levels + 16
    z = call(
        rows_body,
        shape((ROWS, depth, LANES), bf16),
        "rows",
        [VMEM] * 3,
        scratch=[pltpu.VMEM(flat.shape, f32)],
    )(flat, ocean_advect_velocity.reshape(flat.shape), wet_rows)
    before = lax.ppermute(z[ROWS - HALO :], rows_axis, up)
    after = lax.ppermute(z[:HALO], rows_axis, down)
    gained, wet_rows = lax.optimization_barrier((gained, wet_rows))
    atm_final, token = call(
        atmosphere_body,
        (shape(atmosphere_level_state.shape), shape((8, LANES))),
        "atmosphere",
        [VMEM] * 3,
        micros=3,
    )(atmosphere_level_state, gained, atmosphere_mixing_map)
    cells = call(
        cells_body,
        shape((ROWS * LANES, WIDE), bf16),
        "cells",
        [VMEM],
        scratch=[
            pltpu.VMEM((32 * 64, LANES), f32),
            pltpu.VMEM((ROWS * LANES, LANES), f32),
            pltpu.VMEM((ROWS * LANES, LANES), f32),
        ],
    )(remap_weight_tiles.reshape(64, 4096))
    rounded = lax.reduce_precision(ocean_mixing_map, 8, 7)
    upper, lower = rounded.astype(bf16), (ocean_mixing_map - rounded).astype(bf16)
    mix = jnp.concatenate([upper, lower, upper], axis=1)
    cat = pltpu.VMEM((2, 3 * levels, 4 * LANES), bf16)

    edge_rows = shape((HALO - 1, 16, LANES), bf16)
    forcing, send_one, send_two, ocean_currents = call(
        remap_body,
        (shape((ROWS * 16, LANES)), edge_rows, edge_rows, shape(currents.shape)),
        "remap",
        [SMEM, SMEM] + [VMEM] * 4 + [HBM],
    )(arrival, odd, arrived, cells, currents, ocean_cell_mask, token)
    f_one = lax.ppermute(send_one, rows_axis, row_rounds[0])
    f_two = lax.ppermute(send_two, rows_axis, row_rounds[1])
    strip = shape((depth + 16, LANES), bf16)
    send_one, send_two, f_before, f_after = call(
        pack_body, (strip, strip, edge_rows, edge_rows), "pack", [SMEM] + [VMEM] * 6
    )(odd, before, z, after, forcing, f_one, f_two)
    send_one, send_two, mix = lax.optimization_barrier((send_one, send_two, mix))
    one_in = lax.ppermute(send_one, "col", col_rounds[0])
    two_in = lax.ppermute(send_two, "col", col_rounds[1])
    main, side = (EXT, levels, LANES), (EDGES, levels, LANES)
    coef, x1, wet, coef_late, salt = call(
        rows_step_body,
        (
            shape((5, *main)),
            shape(main),
            shape((EXT, 8, LANES)),
            shape((5, *main)),
            shape(main),
        ),
        "rows_step",
        [VMEM] * 5,
        (VMEM, VMEM, VMEM, HBM, HBM),
        scratch=[
            pltpu.VMEM(main, f32),
            pltpu.VMEM((4, EXT, 8, LANES), f32),
            cat,
            pltpu.VMEM(main, f32),
            pltpu.SemaphoreType.DMA((2,)),
        ],
        limit=24,
        micros=2,
    )(before, z, after, flat, mix)
    side_coef, side_x1, side_salt, side_wet, side_force = call(
        edges_step_body,
        (
            shape((5, *side)),
            shape(side),
            shape(side),
            shape((EDGES, 8, LANES)),
            shape((EDGES, 16, LANES)),
        ),
        "edges_step",
        [SMEM] + [VMEM] * 11,
        scratch=[
            pltpu.VMEM(side, f32),
            pltpu.VMEM((4, EDGES, 8, LANES), f32),
            pltpu.VMEM((EDGES, depth, LANES), bf16),
            cat,
        ],
        limit=16,
        micros=1,
    )(
        odd, before, z, after, one_in, two_in, forcing, f_before, f_after,
        mix, spread_moves, own_moves,
    )

    shared = (side_coef, wet, side_wet, mix, forcing, f_before, f_after, side_force)
    wide = (TILES, levels, LANES)
    scratch = [
        pltpu.VMEM(wide, f32),
        pltpu.VMEM(wide, f32),
        pltpu.VMEM((TILES, 8, LANES), f32),
        cat,
        pltpu.VMEM(flat.shape[1:], f32),
        pltpu.SemaphoreType.DMA,
    ]
    warm, terms = call(
        functools.partial(tracer_body, 0),
        (shape(flat.shape), shape((peers * 4, LANES))),
        "temperature",
        [VMEM] * 15,
        (HBM, VMEM),
        scratch=scratch + [pltpu.VMEM((ROWS, LANES), f32)],
        limit=24,
        micros=6,
    )(x1, side_x1, coef, *shared, ocean_mixing_map, cells, place, ocean_currents)
    home = lax.all_to_all(terms, band, 0, 0, tiled=True)
    both = call(
        functools.partial(tracer_body, 1),
        shape(flat.shape),
        "salinity",
        [HBM, VMEM, HBM] + [VMEM] * 8 + [HBM],
        HBM,
        scratch=scratch
        + [pltpu.VMEM(main, f32), pltpu.VMEM((5, *main), f32), pltpu.SemaphoreType.DMA((2,))],
        aliases={11: 0},
        limit=56,
        micros=6,
    )(salt, side_salt, coef_late, *shared, warm)
    returned = call(finish_body, shape((3, air_columns)), "finish", [VMEM, VMEM])(
        jnp.repeat(table, 4, axis=1), home
    )
    return (atm_final, both.reshape(tracers.shape), ocean_currents, returned)


def solution(mesh):
    return jax.shard_map(
        on_device,
        mesh=mesh,
        in_specs=(
            P(None, None, ("comp", "row", "col")),
            P(),
            P(("comp", "row", "col")),
            P(None, None, ("comp", "row"), "col"),
            P(None, ("comp", "row"), "col"),
            P(None, None, ("comp", "row"), "col"),
            P(),
            P(("comp", "row"), "col"),
            P("comp", ("row", "col"), None, None),
            P("comp", ("row", "col"), None, None),
            P("comp", ("row", "col"), None),
        ),
        out_specs=(
            P(None, None, ("comp", "row", "col")),
            P(None, None, ("comp", "row"), "col"),
            P(None, ("comp", "row"), "col"),
            P(None, ("comp", "row", "col")),
        ),
        check_vma=False,
    )
```

```python
import functools

import jax
import jax.numpy as jnp
import numpy as np
from jax import lax
from jax.experimental import pallas as pl
from jax.experimental.pallas import tpu as pltpu
from jax.sharding import PartitionSpec as P

STEPS = 6
HALO = 6
ROWS = 8
EXT = ROWS + 2 * HALO
REACH = 2 * HALO
GROUP = 3
EDGES = -(-EXT // GROUP)
TILES = EXT + EDGES
SIDE = 2 * (HALO + REACH)
LANES = 128
WIDE = 256
HIGHEST = lax.Precision.HIGHEST
MIB = 1024 * 1024

heat_rate = 0.5
vapour_rate = 0.5
drag_rate = 0.3
saturation = 0.6
flux_gains = (0.3, 0.3, -0.3, -0.3)
diffusion = 0.15
surface_gain = (-0.3, 0.3)
surface_push = 0.3
current_drag = 0.1
coriolis = 0.2
turn = np.array([[1.0 - current_drag, coriolis], [-coriolis, 1.0 - current_drag]])

f32 = jnp.float32
bf16 = jnp.bfloat16
VMEM = pl.BlockSpec(memory_space=pltpu.VMEM)
HBM = pl.BlockSpec(memory_space=pltpu.HBM)
SMEM = pl.BlockSpec(memory_space=pltpu.SMEM)


def call(body, out_shape, name, in_specs, out_specs=None, scratch=(), aliases=None, limit=8, micros=1):
    if out_specs is None:
        out_specs = jax.tree.map(lambda _: VMEM, out_shape)
    return pl.pallas_call(
        body,
        out_shape=out_shape,
        in_specs=in_specs,
        out_specs=out_specs,
        scratch_shapes=list(scratch),
        input_output_aliases=aliases or {},
        compiler_params=pltpu.CompilerParams(vmem_limit_bytes=limit * MIB),
        cost_estimate=pl.CostEstimate(
            flops=int(micros * 1e9), bytes_accessed=int(micros * 3e6), transcendentals=0
        ),
        name=name,
    )


def shape(dims, dtype=f32):
    return jax.ShapeDtypeStruct(dims, dtype)


def exact(a, b):
    return jnp.dot(a, b, precision=HIGHEST, preferred_element_type=f32)


def times(a, b):
    return jnp.dot(a, b, preferred_element_type=f32)


def times_rows(a, b):
    return lax.dot_general(a, b, (((1,), (1,)), ((), ())), preferred_element_type=f32)


def iota(dims, axis):
    return lax.broadcasted_iota(jnp.int32, dims, axis)


def one_hot(condition):
    return condition.astype(f32).astype(bf16)


def halves(x):
    high = x.astype(bf16)
    return high, (x - high.astype(f32)).astype(bf16)


def moves():
    spread = np.zeros((2, LANES, EDGES, LANES), np.float32)
    own = np.zeros((GROUP, LANES, LANES), np.float32)
    for r in range(EXT):
        at = SIDE * (r // EDGES)
        for c in range(HALO):
            spread[0, HALO * r + c, r % EDGES, at + SIDE - HALO + c] = 1
            spread[1, HALO * r + c, r % EDGES, at + c] = 1
    for k in range(GROUP):
        for c in range(REACH):
            own[k, c, SIDE * k + HALO + c] = 1
            own[k, LANES - REACH + c, SIDE * k + HALO + REACH + c] = 1
    return (
        jnp.asarray(spread.reshape(2 * LANES, EDGES * LANES), bf16),
        jnp.asarray(own.reshape(GROUP * LANES, LANES), bf16),
    )


def mixing_powers(m_ref):
    power = {1: m_ref[...]}
    power[2] = exact(power[1], power[1])
    power[3] = exact(power[1], power[2])
    power[4] = exact(power[2], power[2])
    power[5] = exact(power[2], power[3])
    power[6] = exact(power[3], power[3])
    return power


def flux_body(
    table_ref, a_hbm, m_hbm, sst_hbm, pay_ref, g_hbm, block_ref, g_ref, a_ref, m_ref, sst_ref, sems, sem
):
    loads = [
        pltpu.make_async_copy(m_hbm, m_ref, sems.at[0]),
        pltpu.make_async_copy(sst_hbm, sst_ref, sems.at[1]),
        pltpu.make_async_copy(a_hbm, a_ref, sems.at[2]),
    ]
    for load in loads:
        load.start()
    loads[0].wait()
    levels = m_ref.shape[0]
    bottom = levels - 1
    power = mixing_powers(m_ref)
    first = (iota((1, levels), 1) == bottom).astype(f32)
    rows = [first] + [power[n][bottom:, :] for n in range(1, STEPS)]
    rows = jnp.concatenate(rows + [jnp.zeros((8 - STEPS, levels), f32)], axis=0)
    row_high, row_low = halves(rows)
    both = jnp.concatenate([row_high.astype(f32), row_low.astype(f32)], axis=0).astype(bf16)
    loads[1].wait()
    loads[2].wait()
    base = []
    for v in range(4):
        high, low = halves(a_ref[v])
        one = times(both, high)
        base.append(one[:8] + one[8:] + times(row_high, low))
    corner = {n: power[n][bottom:, bottom:] for n in range(1, STEPS)}
    sst = sst_ref[...]
    gained = []
    fluxes = []
    east, north = jnp.zeros_like(sst), jnp.zeros_like(sst)
    for n in range(STEPS):
        now = []
        for v in range(4):
            value = base[v][n : n + 1]
            for k in range(n):
                value = value + corner[n - k] * gained[k][v]
            now.append(value)
        wind = jnp.sqrt(now[2] * now[2] + now[3] * now[3] + 1.0)
        flux = (
            heat_rate * wind * (sst - now[0]),
            vapour_rate * wind * (saturation * sst - now[1]),
            drag_rate * wind * now[2],
            drag_rate * wind * now[3],
        )
        fluxes.append(flux)
        gained.append([flux_gains[v] * flux[v] for v in range(4)])
        east, north = (
            turn[0, 0] * east + turn[0, 1] * north + flux[2],
            turn[1, 0] * east + turn[1, 1] * north + flux[3],
        )
    blank = [jnp.zeros_like(sst)] * (8 - STEPS)
    for v in range(4):
        g_ref[v] = jnp.concatenate([gained[n][v] for n in range(STEPS)] + blank, axis=0)
    copy = pltpu.make_async_copy(g_ref, g_hbm, sem)
    copy.start()
    pairs = [(fluxes[n][0], fluxes[n][1]) for n in range(STEPS)] + [(east, north)]
    block = iota((8, LANES), 0)
    left = iota((8, LANES), 1) < 64
    even = block % 2 == 0
    for i, pair in enumerate(pairs):
        parts = []
        for side in range(2):
            spread = jnp.zeros((8, LANES), f32)
            for q in range(4):
                tile = jnp.broadcast_to(pair[side][:, q * LANES : (q + 1) * LANES], (8, LANES))
                spread = jnp.where(block // 2 == q, tile, spread)
            parts.append(jnp.where(even == (side == 0), spread, pltpu.roll(spread, 64, 1)))
        block_ref[pl.ds(i, 8, stride=8), :] = jnp.where(left, parts[0], parts[1])
    block_ref[pl.ds(7, 8, stride=8), :] = jnp.zeros((8, LANES), f32)
    for d in range(pay_ref.shape[0] // 16):
        chosen = []
        for side in range(2):
            at = jnp.maximum(table_ref[side, d], 0) * 8
            chosen.append(block_ref[pl.ds(pl.multiple_of(at, 8), 8), :])
        pay_ref[16 * d : 16 * d + 16, :] = jnp.concatenate(chosen, axis=0).astype(bf16)
    copy.wait()


def atmosphere_body(a_ref, g_ref, m_ref, out_ref, token_ref):
    token_ref[...] = jnp.zeros_like(token_ref)
    levels = m_ref.shape[0]
    power = mixing_powers(m_ref)
    lane = iota((levels, 8), 1)
    edge = jnp.zeros((levels, 8), f32)
    for n in range(STEPS):
        edge = jnp.where(lane == n, power[STEPS - n][:, levels - 1 :], edge)
    for v in range(4):
        out_ref[v] = exact(power[STEPS], a_ref[v]) + exact(edge, g_ref[v])


def finish_body(table_ref, in_ref, out_ref):
    rows = in_ref.shape[0]
    block, lane = iota((8, rows), 0), iota((8, rows), 1)
    ones = []
    for side in range(2):
        named = table_ref[side : side + 1, :] == block
        for f in range(3):
            ones.append((named & (lane % 4 == f)).astype(f32))
    ones = jnp.concatenate(ones, axis=0).astype(bf16)
    high, low = halves(in_ref[...])
    sums = times(ones, high) + times(ones, low)
    left = iota((1, LANES), 1) < 64
    for f in range(3):
        low = sums[8 * f : 8 * f + 8] + pltpu.roll(sums[24 + 8 * f : 32 + 8 * f], 64, 1)
        high = pltpu.roll(low, 64, 1)
        for q in range(4):
            out_ref[f : f + 1, q * LANES : (q + 1) * LANES] = jnp.where(
                left, low[2 * q : 2 * q + 1], high[2 * q + 1 : 2 * q + 2]
            )


def cells_body(w_ref, out_ref, t_ref, low_ref, high_ref):
    left = iota((16, LANES), 1) < 64
    tiles = w_ref.shape[1] // LANES
    for i in range(tiles):
        t_ref[i * 64 : (i + 1) * 64] = w_ref[:, i * LANES : (i + 1) * LANES].astype(f32)
    for i in range(tiles):
        k = [t_ref[pl.ds(i * 64 + s, 16, stride=4), :] for s in range(4)]
        moved = [pltpu.roll(x, 64, 1) for x in k]
        low_ref[pl.ds(2 * i, 16, stride=64), :] = jnp.where(left, k[0], moved[1])
        high_ref[pl.ds(2 * i, 16, stride=64), :] = jnp.where(left, k[2], moved[3])
        low_ref[pl.ds(2 * i + 1, 16, stride=64), :] = jnp.where(left, moved[0], k[1])
        high_ref[pl.ds(2 * i + 1, 16, stride=64), :] = jnp.where(left, moved[2], k[3])
    out_ref[:, :LANES] = low_ref[...].astype(bf16)
    out_ref[:, LANES:] = high_ref[...].astype(bf16)


def rows_body(x_ref, v_ref, wet_ref, z_ref, f_ref):
    levels = x_ref.shape[1] // ROWS
    for t in range(2):
        f_ref[t] = v_ref[t].astype(f32)
    for r in range(ROWS):
        for t in range(2):
            z_ref[r, (2 + t) * levels : (3 + t) * levels, :] = f_ref[
                t, pl.ds(r, levels, stride=ROWS), :
            ].astype(bf16)
        wet = jnp.broadcast_to(wet_ref[r : r + 1, :].astype(f32), (16, LANES))
        z_ref[r, 4 * levels :, :] = wet.astype(bf16)
    for r in range(ROWS):
        for t in range(2):
            z_ref[r, t * levels : (t + 1) * levels, :] = x_ref[
                t, pl.ds(r, levels, stride=ROWS), :
            ].astype(bf16)


def widened(before_ref, own_ref, after_ref):
    rows = [before_ref[r] for r in range(HALO)]
    rows += [own_ref[r] for r in range(ROWS)]
    return rows + [after_ref[r] for r in range(HALO)]


def forcing_rows(f_ref, before_ref, after_ref):
    blank = [jnp.zeros((16, LANES), bf16)]
    rows = blank + [before_ref[r] for r in range(HALO - 1)]
    rows += [f_ref[16 * r : 16 * r + 16].astype(bf16) for r in range(ROWS)]
    return rows + [after_ref[r] for r in range(HALO - 1)] + blank


def pack_matrix():
    row, lane = iota((LANES, LANES), 0), iota((LANES, LANES), 1)
    first = jnp.where(row < HALO, lane - row, -LANES)
    last = jnp.where(row >= LANES - HALO, lane - row + LANES - HALO, -LANES)
    both = [
        jnp.concatenate([one_hot(first == HALO * r), one_hot(last == HALO * r)], axis=1)
        for r in range(EXT)
    ]
    return jnp.concatenate(both, axis=0)


def pack_body(
    odd_ref, before_ref, z_ref, after_ref, f_ref, one_ref, two_ref,
    send_one_ref, send_two_ref, f_before_ref, f_after_ref,
):
    odd_row, odd_col = odd_ref[0, 0] == 1, odd_ref[0, 1] == 1
    for i in range(HALO - 1):
        one, two = one_ref[i].astype(f32), two_ref[i].astype(f32)
        f_before_ref[i] = jnp.where(odd_row, two, one).astype(bf16)
        f_after_ref[i] = jnp.where(odd_row, one, two).astype(bf16)
    rows = jnp.concatenate(widened(before_ref, z_ref, after_ref), axis=1)
    forcing = jnp.concatenate(forcing_rows(f_ref, f_before_ref, f_after_ref), axis=1)
    packed = times(jnp.concatenate([rows, forcing], axis=0), pack_matrix())
    first, last = packed[:, :LANES], packed[:, LANES:]
    send_one_ref[...] = jnp.where(odd_col, last, first).astype(bf16)
    send_two_ref[...] = jnp.where(odd_col, first, last).astype(bf16)


def edge_tile(g, rows, sides, spread_ref, own_ref):
    mine = [rows[r] for r in range(g, EXT, EDGES)]
    return times(jnp.concatenate(mine, axis=1), own_ref[: len(mine) * LANES, :]) + times(
        sides, spread_ref[:, g * LANES : (g + 1) * LANES]
    )


def around(idx, get):
    here = get(idx)
    if idx < EXT:
        north, south = get(idx + 1), get(idx - 1)
    else:
        north = get(idx + 1) if idx + 1 < TILES else pltpu.roll(get(EXT), LANES - SIDE, 1)
        south = get(idx - 1) if idx > EXT else pltpu.roll(get(TILES - 1), SIDE, 1)
    return here, pltpu.roll(here, LANES - 1, 1), pltpu.roll(here, 1, 1), north, south


def ocean_step(tiles, x, coef, mix_ref, cat_ref, store, force=None):
    levels = mix_ref.shape[0]
    first = iota((8, LANES), 0) == 0
    for lo in range(0, len(tiles), 4):
        some = tiles[lo : lo + 4]
        slot = (lo // 4) % 2
        for at in range(0, levels, 16):
            for i, idx in enumerate(some):
                here, east, west, north, south = around(idx, lambda j: x(j, at))
                stepped = (
                    coef(0, idx, at) * here
                    + (coef(1, idx, at) * east + coef(2, idx, at) * west)
                    + (coef(3, idx, at) * north + coef(4, idx, at) * south)
                )
                if force is not None and at == 0:
                    top = stepped[:8] + jnp.where(first, force(idx), 0.0)
                    stepped = jnp.concatenate([top, stepped[8:]], axis=0)
                upper, lower = halves(stepped)
                cols = slice(i * LANES, (i + 1) * LANES)
                cat_ref[slot, at : at + 16, cols] = upper
                cat_ref[slot, levels + at : levels + at + 16, cols] = upper
                cat_ref[slot, 2 * levels + at : 2 * levels + at + 16, cols] = lower
        mixed = times(mix_ref[...], cat_ref[slot, :, : len(some) * LANES])
        for i, idx in enumerate(some):
            store(idx, mixed[:, i * LANES : (i + 1) * LANES])


def step_tiles(n):
    return list(range(n + 1, EXT - 1 - n)), list(range(EXT, TILES))


def two_refs(main_ref, edge_ref):
    def get(idx, at):
        if idx < EXT:
            return main_ref[idx, at : at + 16, :]
        return edge_ref[idx - EXT, at : at + 16, :]

    return get


def two_coefs(main_ref, edge_ref):
    def get(s, idx, at):
        if idx < EXT:
            return main_ref[s, idx, at : at + 16, :]
        return edge_ref[s, idx - EXT, at : at + 16, :]

    return get


def coefficients(inner, base, of, wets, levels, near_ref, coef_ref):
    for idx in inner:
        here, *near = around(idx, lambda j: wets[j])
        for s in range(4):
            near_ref[s, idx - base] = here * near[s]

    def part(c, carry):
        at = pl.multiple_of(c * 16, 16)
        here_at = pl.ds(at, 16)
        for idx in inner:
            along = 0.5 * of(idx, pl.ds(2 * levels + at, 16))
            across = 0.5 * of(idx, pl.ds(3 * levels + at, 16))
            near = []
            for s in range(4):
                one = near_ref[s, idx - base]
                near.append(jnp.concatenate([one, one], axis=0))
            c_east = near[0] * (diffusion - along)
            c_west = near[1] * (diffusion + along)
            c_north = near[2] * (diffusion - across)
            c_south = near[3] * (diffusion + across)
            coef_ref[0, idx - base, here_at, :] = 1.0 - ((c_east + c_west) + (c_north + c_south))
            coef_ref[1, idx - base, here_at, :] = c_east
            coef_ref[2, idx - base, here_at, :] = c_west
            coef_ref[3, idx - base, here_at, :] = c_north
            coef_ref[4, idx - base, here_at, :] = c_south
        return carry

    lax.fori_loop(0, levels // 16, part, 0)


def row_reader(before_ref, z_ref, after_ref):
    def of(idx, at):
        if idx < HALO:
            return before_ref[idx, at, :].astype(f32)
        if idx < HALO + ROWS:
            return z_ref[idx - HALO, at, :].astype(f32)
        return after_ref[idx - HALO - ROWS, at, :].astype(f32)

    return of


def row_start(t, of, x_ref, levels, near_ref, coef_ref, wet_ref, x0_ref):
    wets = [of(idx, pl.ds(4 * levels, 16))[:8] for idx in range(EXT)]
    for idx in range(EXT):
        wet_ref[idx] = wets[idx]
    coefficients(step_tiles(0)[0], 0, of, wets, levels, near_ref, coef_ref)
    for idx in range(EXT):
        if HALO <= idx < HALO + ROWS:
            x0_ref[idx] = x_ref[t, pl.ds(idx - HALO, levels, stride=ROWS), :]
        else:
            x0_ref[idx] = of(idx, pl.ds(t * levels, levels))


def rows_step_body(
    before_ref, z_ref, after_ref, x_ref, mix_ref, coef_ref, x1_ref, wet_ref, x0_ref, near_ref, cat_ref
):
    of = row_reader(before_ref, z_ref, after_ref)
    row_start(0, of, x_ref, mix_ref.shape[0], near_ref, coef_ref, wet_ref, x0_ref)

    def store(idx, value):
        x1_ref[idx] = value

    inner = step_tiles(0)[0]
    ocean_step(inner, two_refs(x0_ref, None), two_coefs(coef_ref, None), mix_ref, cat_ref, store)


def edges_step_body(
    odd_ref, before_ref, z_ref, after_ref, one_ref, two_ref, f_ref, f_before_ref, f_after_ref,
    mix_ref, spread_ref, own_ref,
    coef_ref, x1_ref, salt_ref, wet_ref, force_ref, x0_ref, near_ref, edge_ref, cat_ref,
):
    levels = mix_ref.shape[0]
    depth = z_ref.shape[1]
    rows = widened(before_ref, z_ref, after_ref)
    forcing = forcing_rows(f_ref, f_before_ref, f_after_ref)
    rows = [jnp.concatenate(pair, axis=0) for pair in zip(rows, forcing)]
    odd = odd_ref[0, 1] == 1
    one, two = one_ref[...].astype(f32), two_ref[...].astype(f32)
    sides = jnp.concatenate([jnp.where(odd, one, two), jnp.where(odd, two, one)], axis=1)
    sides = sides.astype(bf16)
    for g in range(EDGES):
        tile = edge_tile(g, rows, sides, spread_ref, own_ref)
        edge_ref[g] = tile[:depth].astype(bf16)
        force_ref[g] = tile[depth:]
        x0_ref[g] = tile[:levels]
        salt_ref[g] = tile[levels : 2 * levels]
        wet_ref[g] = tile[4 * levels : 4 * levels + 8]

    def of(idx, at):
        return edge_ref[idx - EXT, at, :].astype(f32)

    inner = step_tiles(0)[1]
    wets = {idx: wet_ref[idx - EXT] for idx in inner}
    coefficients(inner, EXT, of, wets, levels, near_ref, coef_ref)

    def store(idx, value):
        x1_ref[idx - EXT] = value

    ocean_step(inner, two_refs(None, x0_ref), two_coefs(None, coef_ref), mix_ref, cat_ref, store)


def remap_body(arrival_ref, odd_ref, in_ref, w_ref, u_ref, wet_ref, _, f_ref, one_ref, two_ref, u_out_ref):
    def pick(j):
        t = arrival_ref[0, j]
        at = pl.multiple_of((t >> 1) * 16, 16)
        window = in_ref[pl.ds(at, 16), :].astype(f32)
        return jnp.where((t & 1) == 1, window[8:], window[:8])

    left = iota((8, LANES), 1) < 64
    left_two = iota((16, LANES), 1) < 64
    for r in range(ROWS):
        sources = []
        for side in range(2):
            even, odd = [], []
            for pair in range(2):
                j = 4 * (2 * r + side) + 2 * pair
                one, two = pick(j), pick(j + 1)
                even.append(jnp.where(left, one, pltpu.roll(two, 64, 1)))
                odd.append(jnp.where(left, pltpu.roll(one, 64, 1), two))
            sources.append(jnp.concatenate(even, axis=1))
            sources.append(jnp.concatenate(odd, axis=1))
        sources = jnp.concatenate(sources, axis=0).astype(bf16)
        product = times_rows(sources, w_ref[r * LANES : (r + 1) * LANES, :])
        forcing = jnp.where(left_two, product[:16], product[16:])
        f_ref[16 * r : 16 * r + 16, :] = forcing
    odd = odd_ref[0, 0] == 1
    for i in range(HALO - 1):
        up = f_ref[16 * (ROWS - HALO + 1 + i) : 16 * (ROWS - HALO + 2 + i), :]
        down = f_ref[16 * i : 16 * i + 16, :]
        one_ref[i] = jnp.where(odd, up, down).astype(bf16)
        two_ref[i] = jnp.where(odd, down, up).astype(bf16)
    whole = np.linalg.matrix_power(turn, STEPS)
    wet = wet_ref[...].astype(f32)
    push = [surface_push * f_ref[pl.ds(6 + 8 * v, ROWS, stride=16), :] for v in range(2)]
    for v in range(2):
        ahead = float(whole[v, 0]) * u_ref[0] + float(whole[v, 1]) * u_ref[1] + push[v]
        u_out_ref[v] = u_ref[v] + wet * (ahead - u_ref[v])


def returned_rows(fields, w_ref, place, rows):
    blocks = 2 * ROWS
    block, lane = iota((blocks, LANES), 0), iota((blocks, LANES), 1)
    spread = []
    for field in fields:
        parts = []
        for r in range(ROWS):
            mine = block == 2 * r + (lane >= 64).astype(jnp.int32)
            parts.append(jnp.where(mine, field[r : r + 1], 0.0))
        spread.append(jnp.concatenate(parts, axis=1))
    terms = times(jnp.concatenate(spread, axis=0).astype(bf16), w_ref[...])
    high_parts, low_parts, ones = [], [], []
    target = iota((rows, LANES), 0)
    for f in range(len(fields)):
        mine = terms[f * blocks : (f + 1) * blocks]
        pieces = []
        for half in range(2):
            for k in range(4):
                piece = mine[:, (k // 2) * LANES : (k // 2 + 1) * LANES]
                if k % 2 != half:
                    piece = pltpu.roll(piece, 64, 1)
                pieces.append(jnp.where((lane >= 64) == (half == 1), piece, 0.0))
        high, low = halves(jnp.concatenate(pieces, axis=0))
        high_parts.append(high)
        low_parts.append(low)
        ones.append(one_hot(target == place + f))
    return times(
        jnp.concatenate(ones + ones, axis=1), jnp.concatenate(high_parts + low_parts, axis=0)
    )


def tracer_body(t, *refs):
    edge_x_ref, edge_coef_ref, edge_wet_ref, mix_ref, f_ref, before_ref, after_ref, edge_force_ref = refs[:8]
    if t == 0:
        x_ref, coef_ref, wet_ref, column_ref, w_ref, place_ref, u_ref, out_hbm, send_ref = refs[8:17]
        one_ref, two_ref, force_ref, cat_ref, out_ref, sem, sst_ref = refs[17:]
    else:
        z_before_ref, z_ref, z_after_ref, start_ref, _, out_hbm = refs[8:14]
        one_ref, two_ref, force_ref, cat_ref, out_ref, sem, x_ref, coef_ref, wet_ref, near_ref = refs[14:]
        of = row_reader(z_before_ref, z_ref, z_after_ref)
        row_start(1, of, start_ref, mix_ref.shape[0], near_ref, coef_ref, wet_ref, x_ref)
    levels = mix_ref.shape[0]
    for idx in range(1, TILES):
        if idx == EXT - 1:
            continue
        if idx >= EXT:
            wet, forcing = edge_wet_ref[idx - EXT], edge_force_ref[idx - EXT]
        else:
            wet = wet_ref[idx]
            if idx < HALO:
                forcing = before_ref[idx - 1].astype(f32)
            elif idx < HALO + ROWS:
                forcing = f_ref[16 * (idx - HALO) : 16 * (idx - HALO) + 16, :]
            else:
                forcing = after_ref[idx - HALO - ROWS].astype(f32)
        force_ref[idx] = surface_gain[t] * wet * forcing[8 * t : 8 * t + 8]
    if t == 0:
        column = jnp.broadcast_to(column_ref[:, 0:1], (levels, LANES))
        for idx in range(1, TILES):
            if idx != EXT - 1:
                first = x_ref[idx] if idx < EXT else edge_x_ref[idx - EXT]
                one_ref[idx] = first + column * force_ref[idx, 0:1, :]
        old, new = one_ref, two_ref
    else:
        old, new = None, one_ref
    for n in range(1 if t == 0 else 0, STEPS):

        def store(idx, value, new=new):
            new[idx] = value

        def force(idx, n=n):
            return force_ref[idx, n : n + 1, :]

        if old is None:
            x = two_refs(x_ref, edge_x_ref)
        else:

            def x(idx, at, old=old):
                return old[idx, at : at + 16, :]

        main, edges = step_tiles(n)
        coef = two_coefs(coef_ref, edge_coef_ref)
        ocean_step(main + edges, x, coef, mix_ref, cat_ref, store, force)
        if t == 1 and n == 0:
            old, new = one_ref, two_ref
        else:
            old, new = new, old
    lane = iota((16, LANES), 1)
    for r in range(ROWS):
        idx = HALO + r
        at = SIDE * (idx // EDGES) + HALO
        edge = EXT + idx % EDGES
        for lo in range(0, levels, 16):
            side = old[edge, lo : lo + 16, :]
            value = jnp.where(
                lane < HALO, pltpu.roll(side, (LANES - at) % LANES, 1), old[idx, lo : lo + 16, :]
            )
            here = at + REACH + HALO
            value = jnp.where(
                lane >= LANES - HALO, pltpu.roll(side, (LANES - HALO - here) % LANES, 1), value
            )
            out_ref[pl.ds(lo * ROWS + r, 16, stride=ROWS), :] = value
            if t == 0 and lo == 0:
                sst_ref[r : r + 1, :] = value[0:1]
    copy = pltpu.make_async_copy(out_ref, out_hbm.at[t], sem)
    copy.start()
    if t == 0:
        fields = [sst_ref[...], u_ref[0], u_ref[1]]
        fields = [field.astype(bf16).astype(f32) for field in fields]
        send_ref[...] = returned_rows(fields, w_ref, place_ref[...], send_ref.shape[0])
    copy.wait()


def swaps(size):
    rounds = []
    for start in (1, 0):
        pairs = [(i, i + 1) for i in range(start, size - 1, 2)]
        rounds.append(pairs + [(j, i) for i, j in pairs])
    return rounds


def neighbours(size):
    up = [(i, i + 1) for i in range(size - 1)]
    return up, [(j, i) for i, j in up]


def on_device(
    atmosphere_level_state,
    atmosphere_mixing_map,
    sea_surface_temps,
    tracers,
    currents,
    ocean_advect_velocity,
    ocean_mixing_map,
    ocean_cell_mask,
    remap_weight_tiles,
    outgoing_block_table,
    arrival_slot_table,
):
    band = ("row", "col")
    peers = lax.axis_size(band)
    levels = tracers.shape[1]
    air_levels, air_columns = atmosphere_level_state.shape[1:]
    rows_axis = ("comp", "row")
    up, down = neighbours(lax.axis_size(rows_axis))
    row_rounds = swaps(lax.axis_size(rows_axis))
    col_rounds = swaps(lax.axis_size("col"))
    odd = jnp.stack([lax.axis_index(rows_axis) % 2, lax.axis_index("col") % 2])
    odd = odd.astype(jnp.int32).reshape(1, 2)
    spread_moves, own_moves = moves()

    table = outgoing_block_table.reshape(peers, 2).T
    arrival = arrival_slot_table.reshape(1, 64)
    by_k = arrival.reshape(2 * ROWS, 4).T.reshape(1, 64)
    place = jnp.concatenate(
        [jnp.where(by_k % 2 == side, (by_k // 2) * 4, -64) for side in range(2)], axis=1
    )

    payload, gained = call(
        flux_body,
        (shape((peers * 16, LANES), bf16), shape((4, 8, air_columns))),
        "fluxes",
        [SMEM, HBM, HBM, HBM],
        (VMEM, HBM),
        scratch=[
            pltpu.VMEM((64, LANES), f32),
            pltpu.VMEM((4, 8, air_columns), f32),
            pltpu.VMEM(atmosphere_level_state.shape, f32),
            pltpu.VMEM(atmosphere_mixing_map.shape, f32),
            pltpu.VMEM((1, air_columns), f32),
            pltpu.SemaphoreType.DMA((3,)),
            pltpu.SemaphoreType.DMA,
        ],
        limit=56,
        micros=3,
    )(table, atmosphere_level_state, atmosphere_mixing_map, sea_surface_temps[None])
    payload, wet_rows = lax.optimization_barrier((payload, ocean_cell_mask))
    arrived = lax.all_to_all(payload, band, 0, 0, tiled=True)

    flat = tracers.reshape(2, levels * ROWS, LANES)
    depth = 4 * levels + 16
    z = call(
        rows_body,
        shape((ROWS, depth, LANES), bf16),
        "rows",
        [VMEM] * 3,
        scratch=[pltpu.VMEM(flat.shape, f32)],
    )(flat, ocean_advect_velocity.reshape(flat.shape), wet_rows)
    before = lax.ppermute(z[ROWS - HALO :], rows_axis, up)
    after = lax.ppermute(z[:HALO], rows_axis, down)
    gained, wet_rows = lax.optimization_barrier((gained, wet_rows))
    atm_final, token = call(
        atmosphere_body,
        (shape(atmosphere_level_state.shape), shape((8, LANES))),
        "atmosphere",
        [VMEM] * 3,
        micros=3,
    )(atmosphere_level_state, gained, atmosphere_mixing_map)
    cells = call(
        cells_body,
        shape((ROWS * LANES, WIDE), bf16),
        "cells",
        [VMEM],
        scratch=[
            pltpu.VMEM((32 * 64, LANES), f32),
            pltpu.VMEM((ROWS * LANES, LANES), f32),
            pltpu.VMEM((ROWS * LANES, LANES), f32),
        ],
    )(remap_weight_tiles.reshape(64, 4096))
    rounded = lax.reduce_precision(ocean_mixing_map, 8, 7)
    upper, lower = rounded.astype(bf16), (ocean_mixing_map - rounded).astype(bf16)
    mix = jnp.concatenate([upper, lower, upper], axis=1)
    cat = pltpu.VMEM((2, 3 * levels, 4 * LANES), bf16)

    edge_rows = shape((HALO - 1, 16, LANES), bf16)
    forcing, send_one, send_two, ocean_currents = call(
        remap_body,
        (shape((ROWS * 16, LANES)), edge_rows, edge_rows, shape(currents.shape)),
        "remap",
        [SMEM, SMEM] + [VMEM] * 4 + [HBM],
    )(arrival, odd, arrived, cells, currents, ocean_cell_mask, token)
    f_one = lax.ppermute(send_one, rows_axis, row_rounds[0])
    f_two = lax.ppermute(send_two, rows_axis, row_rounds[1])
    strip = shape((depth + 16, LANES), bf16)
    send_one, send_two, f_before, f_after = call(
        pack_body, (strip, strip, edge_rows, edge_rows), "pack", [SMEM] + [VMEM] * 6
    )(odd, before, z, after, forcing, f_one, f_two)
    send_one, send_two, mix = lax.optimization_barrier((send_one, send_two, mix))
    one_in = lax.ppermute(send_one, "col", col_rounds[0])
    two_in = lax.ppermute(send_two, "col", col_rounds[1])
    main, side = (EXT, levels, LANES), (EDGES, levels, LANES)
    coef, x1, wet = call(
        rows_step_body,
        (shape((5, *main)), shape(main), shape((EXT, 8, LANES))),
        "rows_step",
        [VMEM] * 5,
        scratch=[pltpu.VMEM(main, f32), pltpu.VMEM((4, EXT, 8, LANES), f32), cat],
        limit=24,
        micros=2,
    )(before, z, after, flat, mix)
    side_coef, side_x1, side_salt, side_wet, side_force = call(
        edges_step_body,
        (
            shape((5, *side)),
            shape(side),
            shape(side),
            shape((EDGES, 8, LANES)),
            shape((EDGES, 16, LANES)),
        ),
        "edges_step",
        [SMEM] + [VMEM] * 11,
        scratch=[
            pltpu.VMEM(side, f32),
            pltpu.VMEM((4, EDGES, 8, LANES), f32),
            pltpu.VMEM((EDGES, depth, LANES), bf16),
            cat,
        ],
        limit=16,
        micros=1,
    )(
        odd, before, z, after, one_in, two_in, forcing, f_before, f_after,
        mix, spread_moves, own_moves,
    )

    shared = (side_coef, side_wet, mix, forcing, f_before, f_after, side_force)
    wide = (TILES, levels, LANES)
    scratch = [
        pltpu.VMEM(wide, f32),
        pltpu.VMEM(wide, f32),
        pltpu.VMEM((TILES, 8, LANES), f32),
        cat,
        pltpu.VMEM(flat.shape[1:], f32),
        pltpu.SemaphoreType.DMA,
    ]
    warm, terms = call(
        functools.partial(tracer_body, 0),
        (shape(flat.shape), shape((peers * 4, LANES))),
        "temperature",
        [VMEM] * 15,
        (HBM, VMEM),
        scratch=scratch + [pltpu.VMEM((ROWS, LANES), f32)],
        limit=24,
        micros=6,
    )(side_x1, *shared, x1, coef, wet, ocean_mixing_map, cells, place, ocean_currents)
    home = lax.all_to_all(terms, band, 0, 0, tiled=True)
    both = call(
        functools.partial(tracer_body, 1),
        shape(flat.shape),
        "salinity",
        [VMEM] * 12 + [HBM],
        HBM,
        scratch=scratch
        + [
            pltpu.VMEM(main, f32),
            pltpu.VMEM((5, *main), f32),
            pltpu.VMEM((EXT, 8, LANES), f32),
            pltpu.VMEM((4, EXT, 8, LANES), f32),
        ],
        aliases={12: 0},
        limit=56,
        micros=6,
    )(side_salt, *shared, before, z, after, flat, warm)
    returned = call(finish_body, shape((3, air_columns)), "finish", [VMEM, VMEM])(
        jnp.repeat(table, 4, axis=1), home
    )
    return (atm_final, both.reshape(tracers.shape), ocean_currents, returned)


def solution(mesh):
    return jax.shard_map(
        on_device,
        mesh=mesh,
        in_specs=(
            P(None, None, ("comp", "row", "col")),
            P(),
            P(("comp", "row", "col")),
            P(None, None, ("comp", "row"), "col"),
            P(None, ("comp", "row"), "col"),
            P(None, None, ("comp", "row"), "col"),
            P(),
            P(("comp", "row"), "col"),
            P("comp", ("row", "col"), None, None),
            P("comp", ("row", "col"), None, None),
            P("comp", ("row", "col"), None),
        ),
        out_specs=(
            P(None, None, ("comp", "row", "col")),
            P(None, None, ("comp", "row"), "col"),
            P(None, ("comp", "row"), "col"),
            P(None, ("comp", "row", "col")),
        ),
        check_vma=False,
    )
```
